512 devices in a mesh: seq: 64 (over y, z), head: 8 (over x, core).
Axes of the slice: x: 4, y: 4, z: 16, core: 2. Of those that a mesh axis runs over, the one named last changes fastest.
Arguments:
- query: bfloat16 [16384, 2048], P('seq', 'head'), may hold values from -6 to 6
- key: bfloat16 [16384, 2048], P('seq', 'head'), may hold values from -6 to 6
- value: bfloat16 [16384, 2048], P('seq', 'head'), may hold values from -6 to 6
- output: bfloat16 [16384, 2048], P('seq', 'head'), may hold values from -6 to 6
- grad_out: bfloat16 [16384, 2048], P('seq', 'head'), may hold values from -6 to 6
- logsumexp: float32 [16, 16384], P('head', 'seq'), as said below
- remote_blocks: int32 [128, 8], P('seq'), may hold values from 0 to 127, as said below
- remote_count: int32 [128], P('seq'), may hold values from 1 to 8
Outputs:
- grad_query: bfloat16 [16384, 2048], P('seq', 'head')
- grad_key: bfloat16 [16384, 2048], P('seq', 'head')
- grad_value: bfloat16 [16384, 2048], P('seq', 'head')
The draws below stay inside these ranges and needn't reach their ends.
Inputs may be any that keep to these rules, and one draw needn't show every extreme that they name: Entries remote_blocks[q, r] with r >= remote_count[q] are not used. The used entries of query block q lie in runs of 2 blocks (index // 2) other than q's own run, none within 1 of q, and among all query blocks of one run no two used entries lie in the same run. `logsumexp`: each entry lies within 1 of log((3 + 9 / 2) * 128) + 0.5.
All inputs are finite; a program needn't handle non-finite values.
Results may differ from the reference program's by a relative error of at most 0.0054.
Values may be sent and summed in bfloat16 or wider, within the bound.
A program may use at most 128 MiB of HBM per device.

```python
import jax
import jax.numpy as jnp
from jax import lax

HEADS = 16
HD = 128
BLOCK = 128
QB_DEV = 2
REM = 8
NQB = 128
TOKENS = 16384
N_SEQ = 64


def draw_remote_blocks(key, part):
    key = jax.random.fold_in(key, 3)
    device_keys = jax.random.split(jax.random.fold_in(key, 11), N_SEQ)
    width_all = QB_DEV * REM

    def one_device(single):
        return jax.random.permutation(single, N_SEQ - 1)[:width_all] + 1
    offsets = jax.vmap(one_device)(device_keys).astype(jnp.int32)
    first_row = offsets[0]
    position = jnp.arange(width_all, dtype=jnp.int32)
    first_row = jnp.where(position == 0, 1, jnp.where(first_row == 1, first_row[0], first_row))
    offsets = offsets.at[0].set(first_row)
    owners = (jnp.arange(N_SEQ, dtype=jnp.int32)[:, None] + offsets) % N_SEQ
    local = jax.random.randint(jax.random.fold_in(key, 12), (N_SEQ, width_all), 0, QB_DEV).astype(jnp.int32)
    query_local = (position // REM)[None, :]
    upward = (offsets == 1) & (local == 0) & (query_local == QB_DEV - 1)
    downward = (offsets == N_SEQ - 1) & (local == QB_DEV - 1) & (query_local == 0)
    local = jnp.where(upward, 1, jnp.where(downward, QB_DEV - 2, local))
    return (owners * QB_DEV + local).reshape(NQB, REM).astype(jnp.int32)


def draw_remote_count(key, part):
    key = jax.random.fold_in(key, 5)
    counts = jax.random.randint(jax.random.fold_in(key, 1), (NQB,), 1, REM + 1)
    fullest = jax.random.randint(jax.random.fold_in(key, 2), (), 0, NQB)
    return jnp.where(jnp.arange(NQB) == fullest, REM, counts).astype(jnp.int32)


def draw_logsumexp(key, part):
    key = jax.random.fold_in(key, 7)
    center = jnp.log(jnp.float32((3.0 + (REM + 1) / 2.0) * BLOCK)) + 0.5
    spread = jax.random.uniform(key, (HEADS, TOKENS), jnp.float32, -0.6, 0.6)
    return (center + spread).astype(jnp.float32)


def block_levels(rng, shape, pieces, smallest, top_value):
    factor_of = 1.0
    for axis_at, parts in pieces:
        steps = jax.random.uniform(jax.random.fold_in(jax.random.fold_in(rng, 6), axis_at), (parts,), jnp.float32, smallest / len(pieces), top_value / len(pieces))
        factor_of = factor_of * jnp.repeat(jnp.exp(steps), shape[axis_at] // parts).reshape((-1,) + (1,) * (len(shape) - 1 - axis_at))
    return factor_of


def bell_draw(stream_key, extent, scale, limit, cuts=(), kind=jnp.bfloat16):
    result = jax.random.normal(stream_key, extent, jnp.float32) * scale
    if len(cuts) > 0:
        result = block_levels(stream_key, extent, cuts, -0.22, 0.18) * result
    return jnp.clip(result, min=-limit, max=limit).astype(kind)


def setup_inputs(seed: int = 0) -> dict:
    streams_of = jax.random.split(jax.random.key(seed), 9)
    query = bell_draw(streams_of[0], (TOKENS, HEADS * HD), 1.0, 6.0, ((0, 64), (1, 8)))
    key = bell_draw(streams_of[1], (TOKENS, HEADS * HD), 1.0, 6.0, ((0, 64), (1, 8)))
    value = bell_draw(streams_of[2], (TOKENS, HEADS * HD), 1.0, 6.0, ((0, 64), (1, 8)))
    output = bell_draw(streams_of[3], (TOKENS, HEADS * HD), 1.0, 6.0, ((0, 64), (1, 8)))
    grad_out = bell_draw(streams_of[4], (TOKENS, HEADS * HD), 1.0, 6.0, ((0, 64), (1, 8)))
    logsumexp = draw_logsumexp(jax.random.fold_in(streams_of[8], 71), 0)
    remote_blocks = draw_remote_blocks(jax.random.fold_in(streams_of[8], 71), 0)
    remote_count = draw_remote_count(jax.random.fold_in(streams_of[8], 71), 0)
    return {"query": query, "key": key, "value": value, "output": output, "grad_out": grad_out, "logsumexp": logsumexp, "remote_blocks": remote_blocks, "remote_count": remote_count}


def block_pairs(queries, grads, stats, keys, values, valid, scale):
    queries = queries.astype(jnp.float32)
    grads = grads.astype(jnp.float32)
    keys = keys.astype(jnp.float32)
    values = values.astype(jnp.float32)
    scores = jnp.einsum('pxhd,pyhd->phxy', queries, keys) * scale
    weights = jnp.exp(scores - stats[0][..., None]) * valid[:, None, None, None]
    probs = weights.astype(jnp.bfloat16).astype(jnp.float32)
    grad_values = jnp.einsum('phxy,pxhd->pyhd', probs, grads)
    grad_probs = jnp.einsum('pxhd,pyhd->phxy', grads, values)
    grad_scores = (weights * (grad_probs - stats[1][..., None])).astype(jnp.bfloat16).astype(jnp.float32)
    grad_queries = jnp.einsum('phxy,pyhd->pxhd', grad_scores, keys) * scale
    grad_keys = jnp.einsum('phxy,pxhd->pyhd', grad_scores, queries) * scale
    return grad_queries, grad_keys, grad_values


def reference(query, key, value, output, grad_out, logsumexp, remote_blocks, remote_count):
    scale = float(HD) ** -0.5
    blocks = jnp.arange(NQB, dtype=jnp.int32)
    window_idx = blocks[:, None] + jnp.arange(-1, 2, dtype=jnp.int32)[None, :]
    window_ok = (window_idx >= 0) & (window_idx < NQB)
    remote_ok = jnp.arange(REM, dtype=jnp.int32)[None, :] < remote_count[:, None]
    index = jnp.concatenate([jnp.clip(window_idx, 0, NQB - 1), remote_blocks], axis=1).astype(jnp.int32)
    valid = jnp.concatenate([window_ok, remote_ok], axis=1).astype(jnp.float32)

    def by_head(arr):
        return arr.reshape(NQB, BLOCK, HEADS, HD).transpose(2, 0, 1, 3)[:, :, :, None, :]

    delta = jnp.sum(grad_out.astype(jnp.float32).reshape(NQB, BLOCK, HEADS, HD) * output.astype(jnp.float32).reshape(NQB, BLOCK, HEADS, HD), axis=3)
    delta = delta.transpose(2, 0, 1)[:, :, None, :]
    lse = logsumexp.reshape(HEADS, NQB, 1, BLOCK)

    def one_head(items):
        q_head, g_head, k_head, v_head, lse_head, delta_head = items
        stats = jnp.stack([lse_head, delta_head])
        grad_q = jnp.zeros(q_head.shape, jnp.float32)
        grad_k = jnp.zeros(q_head.shape, jnp.float32)
        grad_v = jnp.zeros(q_head.shape, jnp.float32)
        for slot in range(3 + REM):
            chosen = index[:, slot]
            term_q, term_k, term_v = block_pairs(q_head, g_head, stats, k_head[chosen], v_head[chosen], valid[:, slot], scale)
            if slot >= 3:
                term_q = lax.optimization_barrier(term_q.astype(jnp.bfloat16)).astype(jnp.float32)
            grad_q = grad_q + term_q
            grad_k = grad_k.at[chosen].add(term_k)
            grad_v = grad_v.at[chosen].add(term_v)
        return grad_q, grad_k, grad_v

    grad_q, grad_k, grad_v = lax.map(one_head, (by_head(query), by_head(grad_out), by_head(key), by_head(value), lse, delta))

    def back(arr):
        return arr[:, :, :, 0, :].transpose(1, 2, 0, 3).reshape(TOKENS, HEADS * HD).astype(jnp.bfloat16)

    return back(grad_q), back(grad_k), back(grad_v)
```

```python
import functools

import jax
import jax.numpy as jnp
from jax import lax
from jax.experimental import pallas as pl
from jax.experimental.pallas import tpu as pltpu
from jax.sharding import PartitionSpec as P

HD = 128
BLOCK = 128
NY = 4
SLOTS = 9
RELAY = 4
FRONT = SLOTS - RELAY
OWN = 12
DEAD = 1e30
LOG2E = 1.4426950408889634
F32 = jnp.float32
BF16 = jnp.bfloat16
I32 = jnp.int32


def with_halo(cells, sides, width):
    for axis, dim in sides:
        count = lax.axis_size(axis)
        ends = count - 1
        head = lax.slice_in_dim(cells, 0, width, axis=dim)
        tail = lax.slice_in_dim(cells, cells.shape[dim] - width, cells.shape[dim], axis=dim)
        cells = jnp.concatenate(
            [
                lax.ppermute(tail, axis, [(i, (i + 1) % count) for i in range(ends)]),
                cells,
                lax.ppermute(head, axis, [((i + 1) % count, i) for i in range(ends)]),
            ],
            axis=dim,
        )
    return cells


def block_pairs(queries, grads, stats, keys, values, valid, scale):
    scores = (
        jnp.einsum("pxhd,pyhd->phxy", queries, keys, preferred_element_type=jnp.float32) * scale
    )
    weights = jnp.exp(scores - stats[0][..., None]) * valid[:, None, None, None]
    probs = weights.astype(jnp.bfloat16)
    grad_values = jnp.einsum("phxy,pxhd->pyhd", probs, grads, preferred_element_type=jnp.float32)
    grad_probs = jnp.einsum("pxhd,pyhd->phxy", grads, values, preferred_element_type=jnp.float32)
    grad_scores = (weights * (grad_probs - stats[1][..., None])).astype(jnp.bfloat16)
    grad_queries = (
        jnp.einsum("phxy,pyhd->pxhd", grad_scores, keys, preferred_element_type=jnp.float32) * scale
    )
    grad_keys = (
        jnp.einsum("phxy,pxhd->pyhd", grad_scores, queries, preferred_element_type=jnp.float32)
        * scale
    )
    return (grad_queries, grad_keys, grad_values)


def spread_terms(terms):
    padded = jnp.pad(terms[0], ((0, 2), (0, 0), (0, 0), (0, 0)))
    padded = padded + jnp.pad(terms[1], ((1, 1), (0, 0), (0, 0), (0, 0)))
    return padded + jnp.pad(terms[2], ((2, 0), (0, 0), (0, 0), (0, 0)))


def remote_pairs(
    part_query, part_grad, part_stats, key_table, value_table, key_index, live_in, scale
):
    senders = part_query.shape[0]
    head_count = part_query.shape[2]
    groups = senders // 8

    def remote_group(items):
        one_q, one_g, one_s, one_k, one_l = items
        return block_pairs(
            one_q,
            one_g,
            one_s.transpose(1, 0, 2, 3),
            key_table[one_k],
            value_table[one_k],
            one_l,
            scale,
        )

    group_shape = (groups, 8, BLOCK, head_count, HD)
    found_q, found_k, found_v = lax.map(
        remote_group,
        (
            part_query.reshape(group_shape),
            part_grad.reshape(group_shape),
            part_stats.reshape(groups, 8, 2, head_count, BLOCK),
            key_index.reshape(groups, 8),
            live_in.reshape(groups, 8),
        ),
    )
    out_shape = (senders, BLOCK, head_count, HD)
    return (found_q.reshape(out_shape), found_k.reshape(out_shape), found_v.reshape(out_shape))


def general(query, key, value, output, grad_out, logsumexp, remote_blocks, remote_count):
    seq_size = lax.axis_size("seq")
    place = lax.axis_index("seq")
    rows, width = query.shape
    count_blocks = rows // BLOCK
    heads_here = width // HD
    scale = float(HD) ** (-0.5)
    shape_four = (count_blocks, BLOCK, heads_here, HD)
    q_tiles = query.reshape(shape_four)
    g_tiles = grad_out.reshape(shape_four)
    k_tiles = key.reshape(shape_four)
    v_tiles = value.reshape(shape_four)
    delta = jnp.sum(
        grad_out.astype(jnp.float32).reshape(shape_four)
        * output.astype(jnp.float32).reshape(shape_four),
        axis=3,
    )
    stats = jnp.stack(
        [
            logsumexp.reshape(heads_here, count_blocks, BLOCK).transpose(1, 0, 2),
            delta.transpose(0, 2, 1),
        ]
    )
    slots_used = (
        jnp.arange(remote_blocks.shape[1], dtype=jnp.int32)[None, :] < remote_count[:, None]
    )
    owners = remote_blocks // count_blocks
    local_key = remote_blocks % count_blocks
    match = (
        (owners[:, :, None] == jnp.arange(seq_size, dtype=jnp.int32)[None, None, :])
        & slots_used[:, :, None]
    ).astype(jnp.int32)
    live = jnp.sum(match, axis=(0, 1))
    send_query = jnp.sum(
        match * jnp.arange(count_blocks, dtype=jnp.int32)[:, None, None], axis=(0, 1)
    )
    send_key = jnp.sum(match * local_key[:, :, None], axis=(0, 1))
    meta = jnp.stack([send_key, live], axis=1).astype(jnp.float32)
    got_stats, got_meta = (
        lax.all_to_all(
            stats[:, send_query].transpose(1, 0, 2, 3),
            "seq",
            split_axis=0,
            concat_axis=0,
            tiled=True,
        ),
        lax.all_to_all(meta, "seq", split_axis=0, concat_axis=0, tiled=True),
    )
    key_index = got_meta[:, 0].astype(jnp.int32)
    live_in = got_meta[:, 1]
    got_query, got_grad = (
        lax.all_to_all(q_tiles[send_query], "seq", split_axis=0, concat_axis=0, tiled=True),
        lax.all_to_all(g_tiles[send_query], "seq", split_axis=0, concat_axis=0, tiled=True),
    )
    remote_q, remote_k, remote_v = remote_pairs(
        got_query, got_grad, got_stats, k_tiles, v_tiles, key_index, live_in, scale
    )
    returned = lax.all_to_all(
        remote_q.astype(jnp.bfloat16), "seq", split_axis=0, concat_axis=0, tiled=True
    )
    empty = jnp.zeros((count_blocks, BLOCK, width), jnp.float32)
    grad_key = empty.at[key_index].add(remote_k.reshape(seq_size, BLOCK, width))
    grad_value = empty.at[key_index].add(remote_v.reshape(seq_size, BLOCK, width))
    grad_query = empty.at[send_query].add(
        returned.reshape(seq_size, BLOCK, width).astype(jnp.float32)
    )
    offsets = jnp.arange(3, dtype=jnp.int32)[:, None]
    band_index = (
        place * count_blocks + jnp.arange(count_blocks, dtype=jnp.int32)[None, :] + offsets - 1
    )
    band_ok = (
        ((band_index >= 0) & (band_index < count_blocks * seq_size)).astype(jnp.float32).reshape(-1)
    )
    rimmed = with_halo(jnp.stack([key, value]), (("seq", 1),), BLOCK)
    wide = rimmed.reshape(2, count_blocks + 2, BLOCK, heads_here, HD)
    band_keys = jnp.concatenate([wide[0, j : j + count_blocks] for j in range(3)])
    band_values = jnp.concatenate([wide[1, j : j + count_blocks] for j in range(3)])
    band_q, band_k, band_v = block_pairs(
        jnp.concatenate([q_tiles] * 3),
        jnp.concatenate([g_tiles] * 3),
        jnp.concatenate([stats] * 3, axis=1),
        band_keys,
        band_values,
        band_ok,
        scale,
    )
    grad_query = grad_query + jnp.sum(band_q.reshape(3, count_blocks, BLOCK, width), axis=0)
    spread_k = spread_terms(band_k.reshape(3, count_blocks, BLOCK, heads_here, HD))
    spread_v = spread_terms(band_v.reshape(3, count_blocks, BLOCK, heads_here, HD))
    both = jnp.stack([spread_k, spread_v]).reshape(2, count_blocks + 2, BLOCK, width)
    edges = jnp.stack([both[:, 0], both[:, count_blocks + 1]])
    arrived = with_halo(edges, (("seq", 0),), 1)
    own = both[:, 1 : count_blocks + 1]
    own = own.at[:, 0].add(arrived[0]).at[:, count_blocks - 1].add(arrived[3])
    grad_key = grad_key + own[0]
    grad_value = grad_value + own[1]
    return (
        grad_query.reshape(rows, width).astype(jnp.bfloat16),
        grad_key.reshape(rows, width).astype(jnp.bfloat16),
        grad_value.reshape(rows, width).astype(jnp.bfloat16),
    )


def dot(a, b, ca, cb):
    return lax.dot_general(a, b, (((ca,), (cb,)), ((), ())), preferred_element_type=F32)


FINE = (0, 1)
CHAINS = [(u, j) for u in range(6) for j in ((0, 1) if u in FINE else (2,))]


def last(u, j, d, half):
    if j < 2:
        return half if j == d else half - 1
    return half if u < 4 or d == 0 else half - 1


def plan(half, release=(0, 7, 3), lat=2.0, chunk=0.35, tab=4.0, bw=51.2, hop=0.3, iss=0.1):
    F, R = SLOTS, RELAY
    mid = half // 2
    steps = {}

    for u, j in CHAINS:
        cut = u > 3
        for d in range(2):
            for k in range(last(u, j, d, half) + 1):
                def size(n):
                    return 4 if u > 3 else 64 if n < half and j == 2 else 32
                sends = []
                if k < last(u, j, d, half) and not (cut and k == mid):
                    sends.append((("z", u, j, d, k + 1), d, size(k + 1), 1))
                if k == 0 and cut and mid < last(u, j, d, half):
                    sends.append((("z", u, j, d, mid + 1), d, size(mid + 1), mid + 1))
                needs = [("z", u, j, d, k - 1)] if k else []
                if k == 0 and 0 < u < 4:
                    pj = 0 if u - 1 in FINE else 2
                    needs = [("z", u - 1, pj, d, min(release[u - 1], half - 1))]
                awaits = [("z", u, j, d, k)] if k else []
                steps["z", u, j, d, k] = (needs, awaits, sends, 0.0)

    def all_in(u):
        return [("z", c, j, d, last(c, j, d, half)) for c, j in CHAINS if c == u for d in range(2)]

    steps["tab",] = (all_in(5), [], [], tab)
    stats_in = all_in(4)
    for u in (4, 5):
        steps["zq", u] = ([("tab",)] + all_in(u), [], [], 0.5)
    for h in range(2):
        got = [all_in(2 * h + t) for t in range(2)]
        pairs = []
        for i in range(OWN // 4):
            steps["own", h, i] = ([("tab",)] + stats_in + got[0] + got[1], [], [], 2 * chunk)
            pairs.append(("own", h, i))
        for d in range(2):
            for t in range(3):
                kib = 32 if t < 2 else 4
                needs = [("tab",)] + (got[t] if t < 2 else stats_in)
                if t < 2:
                    sends = [
                        (("yb", h, t, d), 2 + d, R * kib, 1),
                        (("y", h, t, d), 2 + d, (F - R) * kib, 1),
                    ]
                else:
                    sends = [(("yb", h, t, d), 2 + d, F * kib, 1)]
                steps["pk", h, t, d] = (needs, [], sends, 0.25)
                steps["f", h, t, d] = ([], [("yb", h, t, d)], [(("f", h, t, d), 2 + d, R * kib, 1)], 0.0)
            seen = [("f", h, t, d) for t in range(3)]
            ym = [("y", h, t, d) for t in range(2)]
            steps["far", h, d] = ([], seen, [(("r2", h, d), 3 - d, R * 32, 1)], R / 2 * chunk)
            steps["na", h, d] = (seen, ym, [(("r1", h, d, 0), 3 - d, (F - R) * 32, 1)], (F - R) / 2 * chunk)
            steps["nb", h, d] = (seen, [("r2", h, d)], [(("r1", h, d, 1), 3 - d, R * 32, 1)], R / 2 * chunk)
            pairs += [("far", h, d), ("na", h, d), ("nb", h, d)]
        back = [("r1", h, d, part) for d in range(2) for part in range(2)]
        steps["w", h] = (pairs, back, [], 0.1)
        steps["kv", h] = (pairs, [], [], 0.2)
        fin = []
        for d in range(2):
            for j in range(2):
                for k in range(1, half + 1):
                    if k > 1 or j == d:
                        first = k == 1 or (k == 2 and j != d) or k == mid + 1
                        awaits = [] if first else [("s", h, d, j, k - 1)]
                        hops = mid + 1 if k == mid else 1
                        if k in (mid, half):
                            fin.append(("s", h, d, j, k))
                        steps["s", h, d, j, k] = ([("w", h)], awaits, [(("s", h, d, j, k), 1 - d, 32, hops)], 0.12)
        for t in range(2):
            steps["zq", 2 * h + t] = (got[t] + [("pk", h, t, 1)], [], [], 0.5)
        steps["yq", h] = ([("s", h, 0, 0, half // 2 + 1)], [], [], 0.5)
        steps["e", h] = ([("w", h)], fin, [], 0.3)
    for s in list(steps):
        n, a, sd, c = steps[s]
        steps[s] = (n, a, sd, c + iss * (len(a) + len(sd)))
    sender = {m: (s, kib, hops) for s, (_, _, sends, _) in steps.items() for m, _, kib, hops in sends}
    after = {s: [] for s in steps}
    for s, (needs, awaits, _, _) in steps.items():
        for n in needs:
            after[n].append((s, 0.0))
        for m in awaits:
            f, kib, hops = sender[m]
            after[f].append((s, hops * kib / bw + lat + hop * (hops - 1)))
    way = {}

    def length(s):
        if s not in way:
            way[s] = steps[s][3] + max([gap + length(n) for n, gap in after[s]], default=0.0)
        return way[s]

    left = sorted(steps, key=lambda s: (-length(s), str(s)))
    now, free, arrival, done, order = 0.0, [0.0] * 4, {}, set(), []
    while left:
        ready = [
            (max([now] + [arrival[m] for m in steps[s][1]]), i)
            for i, s in enumerate(left)
            if all(n in done for n in steps[s][0]) and all(m in arrival for m in steps[s][1])
        ]
        now, i = min(ready)
        s = left.pop(i)
        now += steps[s][3]
        for m, link, kib, hops in steps[s][2]:
            free[link] = max(free[link], now) + hops * kib / bw
            arrival[m] = free[link] + lat + hop * (hops - 1)
        done.add(s)
        order.append(s)
    return order


def kernel(
    nz,
    remote_ref,
    count_ref,
    q_ref,
    k_ref,
    v_ref,
    o_ref,
    g_ref,
    lse_ref,
    dq_ref,
    dk_ref,
    dv_ref,
    over_ref,
    agq0,
    agq1,
    agg0,
    agg1,
    ags,
    meta,
    full,
    snd,
    rcv,
    fwd,
    psnd,
    prcv,
    pfwd,
    r2snd,
    r2rcv,
    r1snd,
    ret00,
    ret01,
    ret10,
    ret11,
    own0,
    own1,
    rsnd,
    rrcv,
    dkacc,
    dvacc,
    kt_ref,
    table,
    flags,
    lists,
    nxt,
    pos,
    idx,
    msk,
    oidx,
    omsk,
    t_sem,
    z_send,
    z_recv,
    y_send,
    y_recv,
    f_send,
    f_recv,
    r2_send,
    r2_recv,
    r1_send,
    r1_recv,
    s_send,
    s_recv,
):
    me = lax.axis_index("seq")
    y = me // nz
    z = me % nz
    half = nz // 2
    cands = 2 * nz
    scale = float(HD) ** -0.5
    zdev = [y * nz + lax.rem(z + 1, nz), y * nz + lax.rem(z + nz - 1, nz)]
    ydev = [lax.rem(y + 1, NY) * nz + z, lax.rem(y + NY - 1, NY) * nz + z]
    mid = half // 2
    zfar = [y * nz + lax.rem(z + mid + 1, nz), y * nz + lax.rem(z + nz - mid - 1, nz)]
    agq = [agq0, agq1]
    agg = [agg0, agg1]
    ret = [[ret00, ret01], [ret10, ret11]]
    own = [own0, own1]
    chain_refs = [agq0, agg0, agq1, agg1]

    barrier = pltpu.get_barrier_semaphore()
    for dev in zdev + zfar + ydev:
        pl.semaphore_signal(
            barrier, inc=1, device_id={"seq": dev}, device_id_type=pl.DeviceIdType.MESH
        )

    for h in range(2):
        cols = slice(h * HD, (h + 1) * HD)
        for j in range(2):
            rows = slice(j * BLOCK, (j + 1) * BLOCK)
            agq[h][2 * z + j] = q_ref[rows, cols]
            agg[h][2 * z + j] = g_ref[rows, cols]
            prod = g_ref[rows, cols].astype(F32) * o_ref[rows, cols].astype(F32)
            ags[z, 4 * h + 2 * j : 4 * h + 2 * j + 1, :] = lse_ref[h : h + 1, rows] * LOG2E
            ags[z, 4 * h + 2 * j + 1 : 4 * h + 2 * j + 2, :] = jnp.sum(
                prod.T, axis=0, keepdims=True
            )
            ret[h][j][SLOTS] = jnp.zeros((BLOCK, HD), BF16)
        own[h][OWN] = jnp.zeros((BLOCK, HD), F32)
        dkacc[h] = jnp.zeros((2 * BLOCK, HD), F32)
        kt_ref[h] = k_ref[:, cols].T
        dvacc[h] = jnp.zeros((2 * BLOCK, HD), F32)

    line = lax.broadcasted_iota(I32, (8, BLOCK), 0)
    lane = lax.broadcasted_iota(I32, (8, BLOCK), 1)
    rows = jnp.zeros((8, BLOCK), I32)
    for j in range(2):
        hit = jnp.where(jnp.abs(lane - (2 * me + j)) <= 1, 1, 0)
        for r in range(remote_ref.shape[1]):
            used = jnp.where(count_ref[j] > r, 1, 0)
            hit = jnp.maximum(hit, jnp.where(lane == remote_ref[j, r], used, 0))
        rows = jnp.where(line == j, hit, rows)
    meta[z] = rows

    pl.semaphore_wait(barrier, 6)

    def remote(src, dst, send, recv, dev):
        return pltpu.make_async_remote_copy(
            src_ref=src,
            dst_ref=dst,
            send_sem=send,
            recv_sem=recv,
            device_id={"seq": dev},
            device_id_type=pl.DeviceIdType.MESH,
        )

    def z_view(u, j, d, k, at):
        if u > 3:
            return (ags, meta)[u - 4].at[at]
        if j == 2 and k < half:
            return chain_refs[u].at[pl.ds(2 * at, 2)]
        return chain_refs[u].at[pl.ds(2 * at + (d if j == 2 else j), 1)]

    def z_copy(u, j, d, k, receiving=False):
        direct = u > 3 and k == mid + 1
        hop = k if receiving else 0 if direct else k - 1
        at = lax.rem(z + nz - hop, nz) if d == 0 else lax.rem(z + hop, nz)
        view = z_view(u, j, d, k, at)
        c = CHAINS.index((u, j))
        sems = z_send.at[c, d, k - 1], z_recv.at[c, d, k - 1]
        return remote(view, view, *sems, (zfar if direct else zdev)[d])

    def z_step(u, j, d, k):
        if k > 0:
            z_copy(u, j, d, k, receiving=True).wait_recv()
        end = last(u, j, d, half)
        if k < end and not (u > 3 and k == mid):
            z_copy(u, j, d, k + 1).start()
        if k == 0 and u > 3 and mid < end:
            z_copy(u, j, d, mid + 1).start()

    def z_drain(u):
        for c, j in CHAINS:
            if c == u:
                for d in range(2):
                    for k in range(1, last(u, j, d, half) + 1):
                        z_copy(u, j, d, k).wait_send()

    def build_tables():
        copy = pltpu.make_async_copy(meta, table, t_sem)
        copy.start()
        copy.wait()

        def bit(c, yy, b):
            return table[c // 2, c % 2, lax.rem(y + yy, NY) * cands + 2 * z + b]

        def scan(c, carry):
            count = []
            for yy in range(NY):
                live = bit(c, yy, 0) | bit(c, yy, 1)
                flags[yy, c] = live
                count.append(carry[yy] + live)
            return tuple(count)

        zero = jnp.int32(0)
        n0, n1p, n2, n1m = lax.fori_loop(0, cands, scan, (zero,) * 4)
        up = lax.shift_right_arithmetic(n2 + n1m - n1p + 1, jnp.int32(1))
        up = jnp.minimum(jnp.maximum(up, jnp.maximum(n2 - RELAY, 0)), jnp.minimum(n2, RELAY))

        def place(c, carry):
            r2, bp, bm, ap, am, ro = carry
            l0, l1, l2, l3 = flags[0, c], flags[1, c], flags[2, c], flags[3, c]
            to_p = jnp.where(r2 < up, l2, 0)
            to_m = l2 - to_p
            front_p = l1 * (1 - to_p)
            front_m = l3 * (1 - to_m)

            def where_in(front, a, back, b):
                p = jnp.where(back > 0, SLOTS - 1 - b, jnp.where(front > 0, a, SLOTS))
                return jnp.minimum(jnp.maximum(p, 0), SLOTS)

            pos[0, c] = where_in(front_p, ap, to_p, bp)
            pos[1, c] = where_in(front_m, am, to_m, bm)
            pos[2, c] = jnp.minimum(jnp.where(l0 > 0, ro, OWN), OWN)
            lists[0, c] = front_p
            lists[1, c] = to_p
            lists[2, c] = front_m
            lists[3, c] = to_m
            lists[4, c] = l0
            return r2 + l2, bp + to_p, bm + to_m, ap + front_p, am + front_m, ro + l0

        _, bp, bm, ap, am, _ = lax.fori_loop(0, cands, place, (zero,) * 6)
        most = jnp.maximum(jnp.maximum(ap + bp, am + bm) - SLOTS, n0 - OWN)
        most = jnp.maximum(most, jnp.maximum(bp, bm) - RELAY)
        full[...] = jnp.broadcast_to(jnp.where(most > 0, 1.0, 0.0).astype(F32), (8, BLOCK))

        for n in range(5):
            nxt[n, cands] = jnp.int32(cands)
            nxt[n, cands + 1] = jnp.int32(cands)

        def back(i, carry):
            c = cands - 1 - i
            out = []
            for n in range(5):
                cur = jnp.where(lists[n, c] > 0, c, carry[n])
                nxt[n, c] = cur
                out.append(cur)
            return tuple(out)

        lax.fori_loop(0, cands, back, (jnp.int32(cands),) * 5)

        for d in range(2):
            front = nxt[2 * d, 0]
            fronts = []
            for p in range(SLOTS):
                fronts.append(front)
                front = nxt[2 * d, front + 1]
            tail = nxt[2 * d + 1, 0]
            tails = []
            for p in range(RELAY):
                tails.append(tail)
                tail = nxt[2 * d + 1, tail + 1]
            for p in range(SLOTS):
                c = fronts[p]
                live2 = jnp.int32(0)
                if p >= SLOTS - RELAY:
                    t = tails[SLOTS - 1 - p]
                    live2 = jnp.where(t < cands, 1, 0)
                    c = jnp.where(t < cands, t, c)
                live1 = jnp.where(c < cands, 1, 0)
                c = jnp.minimum(c, cands - 1)
                idx[d, p] = c
                yy = 1 if d == 0 else NY - 1
                msk[d, p, 0] = live1 * bit(c, yy, 0)
                msk[d, p, 1] = live1 * bit(c, yy, 1)
                msk[d, p, 2] = live2 * bit(c, 2, 0)
                msk[d, p, 3] = live2 * bit(c, 2, 1)
        cur = nxt[4, 0]
        for p in range(OWN):
            c = jnp.minimum(cur, cands - 1)
            live = jnp.where(cur < cands, 1, 0)
            oidx[p] = c
            omsk[0, p] = live * bit(c, 0, 0)
            omsk[1, p] = live * bit(c, 0, 1)
            if p + 1 < OWN:
                cur = nxt[4, cur + 1]

    def pairs(h, queries, grads, lse0, lse1, delta):
        cols = slice(h * HD, (h + 1) * HD)
        scores = dot(k_ref[:, cols], queries, 1, 1) * (scale * LOG2E)
        weights = jnp.concatenate(
            [jnp.exp2(scores[:BLOCK] - lse0), jnp.exp2(scores[BLOCK:] - lse1)], axis=0
        )
        dvacc[h] += dot(weights.astype(BF16), grads, 1, 0)
        grad_probs = dot(v_ref[:, cols], grads, 1, 1)
        grad_scores = (weights * (grad_probs - delta)).astype(BF16)
        dkacc[h] += dot(grad_scores, queries, 1, 0)
        return dot(kt_ref[h], grad_scores, 1, 0) * scale

    def stat_rows(h, c):
        tile = ags[c // 2]
        odd = c % 2 > 0
        lse = jnp.where(odd, tile[4 * h + 2 : 4 * h + 3], tile[4 * h : 4 * h + 1])
        delta = jnp.where(odd, tile[4 * h + 3 : 4 * h + 4], tile[4 * h + 1 : 4 * h + 2])
        return lse, delta

    def join(parts, axis):
        return jnp.concatenate(parts, axis=axis)

    def own_pairs(h, lo, hi):
        qs, gs, l0, l1, dl = [], [], [], [], []
        for p in range(lo, hi):
            c = oidx[p]
            lse, delta = stat_rows(h, c)
            qs.append(agq[h][c])
            gs.append(agg[h][c])
            l0.append(jnp.where(omsk[0, p] > 0, lse, DEAD))
            l1.append(jnp.where(omsk[1, p] > 0, lse, DEAD))
            dl.append(delta)
        got = pairs(h, join(qs, 0), join(gs, 0), join(l0, 1), join(l1, 1), join(dl, 1))
        for p in range(lo, hi):
            own[h][p] = got[:, (p - lo) * BLOCK : (p - lo + 1) * BLOCK]

    def packet_pairs(h, d, blocks, stats, row, lo, hi, put):
        queries = blocks[h, 0, d, lo:hi].reshape((hi - lo) * BLOCK, HD)
        grads = blocks[h, 1, d, lo:hi].reshape((hi - lo) * BLOCK, HD)

        def rows(r):
            return join([stats[h, d, p][r : r + 1] for p in range(lo, hi)], 1)

        got = pairs(h, queries, grads, rows(row), rows(row + 1), rows(4))
        for p in range(lo, hi):
            put(p, got[:, (p - lo) * BLOCK : (p - lo + 1) * BLOCK])

    def pack(h, t, d):
        if t < 2:
            source = (agq, agg)[t][h]

            for part in (1, 0):
                @pl.loop(FRONT * part, SLOTS if part else FRONT)
                def _(p):
                    snd[h, t, d, p] = source[idx[d, p]]

                y_copy(h, t, d, part).start()
        else:
            @pl.loop(0, SLOTS)
            def _(p):
                lse, delta = stat_rows(h, idx[d, p])
                tile = jnp.where(line == 4, delta, 0.0)
                tile = jnp.where(line == 5, full[0:1], tile)
                for r in range(4):
                    row = jnp.where(msk[d, p, r] > 0, lse, DEAD)
                    tile = jnp.where(line == r, row, tile)
                psnd[h, d, p] = tile

            y_copy(h, t, d, 1).start()

    def y_copy(h, t, d, part):
        at = pl.ds(FRONT, RELAY) if part else pl.ds(0, FRONT)
        if t == 2:
            src, dst = psnd.at[h, d], prcv.at[h, d]
        else:
            src, dst = snd.at[h, t, d, at], rcv.at[h, t, d, at]
        return remote(src, dst, y_send.at[h, t, d, part], y_recv.at[h, t, d, part], ydev[d])

    def f_copy(h, t, d):
        last = pl.ds(SLOTS - RELAY, RELAY)
        if t == 2:
            src, dst = prcv.at[h, d, last], pfwd.at[h, d]
        else:
            src, dst = rcv.at[h, t, d, last], fwd.at[h, t, d]
        return remote(src, dst, f_send.at[h, t, d], f_recv.at[h, t, d], ydev[d])

    def relay(h, t, d):
        y_copy(h, t, d, 1).wait_recv()
        f_copy(h, t, d).start()

    def r2_copy(h, d):
        return remote(
            r2snd.at[h, d], r2rcv.at[h, d], r2_send.at[h, d], r2_recv.at[h, d], ydev[1 - d]
        )

    def r1_copy(h, d, part):
        at = pl.ds(0, SLOTS - RELAY) if part == 0 else pl.ds(SLOTS - RELAY, RELAY)
        return remote(
            r1snd.at[h, d, at],
            ret[h][d].at[at],
            r1_send.at[h, d, part],
            r1_recv.at[h, d, part],
            ydev[1 - d],
        )

    def far_pairs(h, d):
        for t in range(3):
            f_copy(h, t, d).wait_recv()

        def put(p, got):
            r2snd[h, d, p] = got.astype(BF16)

        packet_pairs(h, d, fwd, pfwd, 2, 0, RELAY, put)
        r2_copy(h, d).start()

    def near_pairs(h, d):
        for t in range(2):
            y_copy(h, t, d, 0).wait_recv()

        def put(p, got):
            r1snd[h, d, p] = got.astype(BF16)

        packet_pairs(h, d, rcv, prcv, 0, 0, SLOTS - RELAY, put)
        r1_copy(h, d, 0).start()

    def relay_pairs(h, d):
        r2_copy(h, d).wait_recv()

        def put(p, got):
            back = r2rcv[h, d, p - (SLOTS - RELAY)].astype(F32)
            r1snd[h, d, p] = (got + back).astype(BF16)

        packet_pairs(h, d, rcv, prcv, 0, SLOTS - RELAY, SLOTS, put)
        r1_copy(h, d, 1).start()

    def terms(h, at, j):
        c = 2 * at + j
        total = own[h][pos[2, c]]
        for d in range(2):
            total = total + ret[h][d][pos[d, c]].astype(F32)
        return total

    def s_copy(h, d, j, k):
        at = pl.ds(0, BLOCK + 16 if h == 0 and j == d else BLOCK)
        return remote(
            rsnd.at[h, d, j, k - 1, at],
            rrcv.at[h, d, j, k - 1, at],
            s_send.at[h, d, j, k - 1],
            s_recv.at[h, d, j, k - 1],
            (zfar if k == mid else zdev)[1 - d],
        )

    extra = slice(BLOCK, BLOCK + 16)

    def s_step(h, d, j, k):
        dist = half + 1 - k
        at = lax.rem(z + nz - dist, nz) if d == 0 else lax.rem(z + dist, nz)
        total = terms(h, at, j)
        carries = h == 0 and j == d
        if carries:
            rsnd[h, d, j, k - 1, extra] = jnp.broadcast_to(full[0:1], (16, HD)).astype(BF16)
        if k != mid + 1 and (k > 2 or (k == 2 and j == d)):
            s_copy(h, d, j, k - 1).wait_recv()
            total = total + rrcv[h, d, j, k - 2, :BLOCK].astype(F32)
            if carries:
                rsnd[h, d, j, k - 1, extra] = jnp.maximum(
                    rsnd[h, d, j, k - 1, extra], rrcv[h, d, j, k - 2, extra]
                )
        rsnd[h, d, j, k - 1, :BLOCK] = total.astype(BF16)
        s_copy(h, d, j, k).start()
        if k - 2 >= (mid + 1 if k > mid else 1 if j == d else 2):
            s_copy(h, d, j, k - 2).wait_send()

    def s_end(h):
        cols = slice(h * HD, (h + 1) * HD)
        any_full = full[0:1]
        for j in range(2):
            total = terms(h, z, j)
            for d in range(2):
                for k in (mid, half):
                    if k > 1 or j == d:
                        s_copy(h, d, j, k).wait_recv()
                        total = total + rrcv[h, d, j, k - 1, :BLOCK].astype(F32)
                        if h == 0 and j == d:
                            got = rrcv[h, d, j, k - 1, extra].astype(F32)
                            any_full = jnp.maximum(any_full, got[0:1])
                for lo, hi in ((1 if j == d else 2, mid), (mid + 1, half)):
                    for k in range(max(lo, hi - 1), hi + 1):
                        s_copy(h, d, j, k).wait_send()
            dq_ref[j * BLOCK : (j + 1) * BLOCK, cols] = total.T.astype(BF16)
        if h == 0:
            over_ref[...] = jnp.broadcast_to(any_full, (8, BLOCK))

    def r1_wait(h):
        for d in range(2):
            for part in range(2):
                r1_copy(h, d, part).wait_recv()
        if h == 0:
            seen = full[0:1]
            for d in range(2):
                seen = jnp.maximum(seen, jnp.maximum(prcv[0, d, 0][5:6], pfwd[0, d, 0][5:6]))
            full[...] = jnp.broadcast_to(seen, (8, BLOCK))

    def results(h):
        cols = slice(h * HD, (h + 1) * HD)
        dk_ref[:, cols] = (dkacc[h] * scale).astype(BF16)
        dv_ref[:, cols] = dvacc[h].astype(BF16)

    def y_drain(h):
        for d in range(2):
            for t in range(3):
                for part in range(2):
                    if t < 2 or part:
                        y_copy(h, t, d, part).wait_send()
                f_copy(h, t, d).wait_send()
            r2_copy(h, d).wait_send()
            for part in range(2):
                r1_copy(h, d, part).wait_send()

    do = {
        "z": z_step,
        "tab": build_tables,
        "own": lambda h, i: own_pairs(h, 4 * i, 4 * i + 4),
        "pk": pack,
        "f": relay,
        "far": far_pairs,
        "na": near_pairs,
        "nb": relay_pairs,
        "w": r1_wait,
        "kv": results,
        "zq": z_drain,
        "yq": y_drain,
        "s": s_step,
        "e": s_end,
    }
    for step in plan(half):
        do[step[0]](*step[1:])


def fast(nz, remote, count, query, key, value, output, grad_out, logsumexp):
    rows, width = query.shape
    half = nz // 2
    blocks = (2 * nz, BLOCK, HD)
    vmem, dma = pltpu.VMEM, pltpu.SemaphoreType.DMA
    smem = pltpu.SMEM
    outs = [jax.ShapeDtypeStruct((rows, width), BF16)] * 3
    outs.append(jax.ShapeDtypeStruct((8, BLOCK), F32))
    in_vmem = pl.BlockSpec(memory_space=pltpu.VMEM)
    scratch = [
        *[vmem(blocks, BF16)] * 4,
        vmem((nz, 8, BLOCK), F32),
        vmem((nz, 8, BLOCK), I32),
        vmem((8, BLOCK), F32),
        vmem((2, 2, 2, SLOTS, BLOCK, HD), BF16),
        vmem((2, 2, 2, SLOTS, BLOCK, HD), BF16),
        vmem((2, 2, 2, RELAY, BLOCK, HD), BF16),
        vmem((2, 2, SLOTS, 8, BLOCK), F32),
        vmem((2, 2, SLOTS, 8, BLOCK), F32),
        vmem((2, 2, RELAY, 8, BLOCK), F32),
        vmem((2, 2, RELAY, BLOCK, HD), BF16),
        vmem((2, 2, RELAY, BLOCK, HD), BF16),
        vmem((2, 2, SLOTS, BLOCK, HD), BF16),
        *[vmem((SLOTS + 1, BLOCK, HD), BF16)] * 4,
        *[vmem((OWN + 1, BLOCK, HD), F32)] * 2,
        vmem((2, 2, 2, half, BLOCK + 16, HD), BF16),
        vmem((2, 2, 2, half, BLOCK + 16, HD), BF16),
        vmem((2, 2 * BLOCK, HD), F32),
        vmem((2, 2 * BLOCK, HD), F32),
        vmem((2, HD, 2 * BLOCK), BF16),
        smem((nz, 8, BLOCK), I32),
        smem((NY, 2 * nz), I32),
        smem((5, 2 * nz), I32),
        smem((5, 2 * nz + 2), I32),
        smem((3, 2 * nz), I32),
        smem((2, SLOTS), I32),
        smem((2, SLOTS, 4), I32),
        smem((OWN,), I32),
        smem((2, OWN), I32),
        pltpu.SemaphoreType.DMA,
        *[dma((len(CHAINS), 2, half))] * 2,
        *[dma((2, 3, 2, 2))] * 2,
        *[dma((2, 3, 2))] * 2,
        *[dma((2, 2))] * 2,
        *[dma((2, 2, 2))] * 2,
        *[dma((2, 2, 2, half))] * 2,
    ]
    return pl.pallas_call(
        functools.partial(kernel, nz),
        out_shape=outs,
        in_specs=[pl.BlockSpec(memory_space=pltpu.SMEM)] * 2 + [in_vmem] * 6,
        out_specs=[in_vmem] * 4,
        scratch_shapes=scratch,
        compiler_params=pltpu.CompilerParams(
            collective_id=0, has_side_effects=True, vmem_limit_bytes=48 * 1024 * 1024
        ),
        cost_estimate=pl.CostEstimate(
            flops=4 * 10**9, bytes_accessed=4 * 2**20, transcendentals=5 * 10**6
        ),
    )(remote, count, query, key, value, output, grad_out, logsumexp)


def per_device(query, key, value, output, grad_out, logsumexp, remote_blocks, remote_count):
    nz = lax.axis_size("seq") // NY
    *found, over = fast(
        nz, remote_blocks, remote_count, query, key, value, output, grad_out, logsumexp
    )
    return lax.cond(
        over[0, 0] > 0,
        lambda: general(
            query, key, value, output, grad_out, logsumexp, remote_blocks, remote_count
        ),
        lambda: tuple(found),
    )


def solution(mesh):
    return jax.shard_map(
        per_device,
        mesh=mesh,
        in_specs=(
            P("seq", "head"),
            P("seq", "head"),
            P("seq", "head"),
            P("seq", "head"),
            P("seq", "head"),
            P("head", "seq"),
            P("seq", None),
            P("seq"),
        ),
        out_specs=(P("seq", "head"), P("seq", "head"), P("seq", "head")),
        check_vma=False,
    )
```

```python
import functools

import jax
import jax.numpy as jnp
from jax import lax
from jax.experimental import pallas as pl
from jax.experimental.pallas import tpu as pltpu
from jax.sharding import PartitionSpec as P

HD = 128
BLOCK = 128
NY = 4
SLOTS = 9
RELAY = 4
FRONT = SLOTS - RELAY
OWN = 12
DEAD = 1e30
LOG2E = 1.4426950408889634
F32 = jnp.float32
BF16 = jnp.bfloat16
I32 = jnp.int32


def with_halo(cells, sides, width):
    for axis, dim in sides:
        count = lax.axis_size(axis)
        ends = count - 1
        head = lax.slice_in_dim(cells, 0, width, axis=dim)
        tail = lax.slice_in_dim(cells, cells.shape[dim] - width, cells.shape[dim], axis=dim)
        cells = jnp.concatenate(
            [
                lax.ppermute(tail, axis, [(i, (i + 1) % count) for i in range(ends)]),
                cells,
                lax.ppermute(head, axis, [((i + 1) % count, i) for i in range(ends)]),
            ],
            axis=dim,
        )
    return cells


def block_pairs(queries, grads, stats, keys, values, valid, scale):
    scores = (
        jnp.einsum("pxhd,pyhd->phxy", queries, keys, preferred_element_type=jnp.float32) * scale
    )
    weights = jnp.exp(scores - stats[0][..., None]) * valid[:, None, None, None]
    probs = weights.astype(jnp.bfloat16)
    grad_values = jnp.einsum("phxy,pxhd->pyhd", probs, grads, preferred_element_type=jnp.float32)
    grad_probs = jnp.einsum("pxhd,pyhd->phxy", grads, values, preferred_element_type=jnp.float32)
    grad_scores = (weights * (grad_probs - stats[1][..., None])).astype(jnp.bfloat16)
    grad_queries = (
        jnp.einsum("phxy,pyhd->pxhd", grad_scores, keys, preferred_element_type=jnp.float32) * scale
    )
    grad_keys = (
        jnp.einsum("phxy,pxhd->pyhd", grad_scores, queries, preferred_element_type=jnp.float32)
        * scale
    )
    return (grad_queries, grad_keys, grad_values)


def spread_terms(terms):
    padded = jnp.pad(terms[0], ((0, 2), (0, 0), (0, 0), (0, 0)))
    padded = padded + jnp.pad(terms[1], ((1, 1), (0, 0), (0, 0), (0, 0)))
    return padded + jnp.pad(terms[2], ((2, 0), (0, 0), (0, 0), (0, 0)))


def remote_pairs(
    part_query, part_grad, part_stats, key_table, value_table, key_index, live_in, scale
):
    senders = part_query.shape[0]
    head_count = part_query.shape[2]
    groups = senders // 8

    def remote_group(items):
        one_q, one_g, one_s, one_k, one_l = items
        return block_pairs(
            one_q,
            one_g,
            one_s.transpose(1, 0, 2, 3),
            key_table[one_k],
            value_table[one_k],
            one_l,
            scale,
        )

    group_shape = (groups, 8, BLOCK, head_count, HD)
    found_q, found_k, found_v = lax.map(
        remote_group,
        (
            part_query.reshape(group_shape),
            part_grad.reshape(group_shape),
            part_stats.reshape(groups, 8, 2, head_count, BLOCK),
            key_index.reshape(groups, 8),
            live_in.reshape(groups, 8),
        ),
    )
    out_shape = (senders, BLOCK, head_count, HD)
    return (found_q.reshape(out_shape), found_k.reshape(out_shape), found_v.reshape(out_shape))


def general(query, key, value, output, grad_out, logsumexp, remote_blocks, remote_count):
    seq_size = lax.axis_size("seq")
    place = lax.axis_index("seq")
    rows, width = query.shape
    count_blocks = rows // BLOCK
    heads_here = width // HD
    scale = float(HD) ** (-0.5)
    shape_four = (count_blocks, BLOCK, heads_here, HD)
    q_tiles = query.reshape(shape_four)
    g_tiles = grad_out.reshape(shape_four)
    k_tiles = key.reshape(shape_four)
    v_tiles = value.reshape(shape_four)
    delta = jnp.sum(
        grad_out.astype(jnp.float32).reshape(shape_four)
        * output.astype(jnp.float32).reshape(shape_four),
        axis=3,
    )
    stats = jnp.stack(
        [
            logsumexp.reshape(heads_here, count_blocks, BLOCK).transpose(1, 0, 2),
            delta.transpose(0, 2, 1),
        ]
    )
    slots_used = (
        jnp.arange(remote_blocks.shape[1], dtype=jnp.int32)[None, :] < remote_count[:, None]
    )
    owners = remote_blocks // count_blocks
    local_key = remote_blocks % count_blocks
    match = (
        (owners[:, :, None] == jnp.arange(seq_size, dtype=jnp.int32)[None, None, :])
        & slots_used[:, :, None]
    ).astype(jnp.int32)
    live = jnp.sum(match, axis=(0, 1))
    send_query = jnp.sum(
        match * jnp.arange(count_blocks, dtype=jnp.int32)[:, None, None], axis=(0, 1)
    )
    send_key = jnp.sum(match * local_key[:, :, None], axis=(0, 1))
    meta = jnp.stack([send_key, live], axis=1).astype(jnp.float32)
    got_stats, got_meta = (
        lax.all_to_all(
            stats[:, send_query].transpose(1, 0, 2, 3),
            "seq",
            split_axis=0,
            concat_axis=0,
            tiled=True,
        ),
        lax.all_to_all(meta, "seq", split_axis=0, concat_axis=0, tiled=True),
    )
    key_index = got_meta[:, 0].astype(jnp.int32)
    live_in = got_meta[:, 1]
    got_query, got_grad = (
        lax.all_to_all(q_tiles[send_query], "seq", split_axis=0, concat_axis=0, tiled=True),
        lax.all_to_all(g_tiles[send_query], "seq", split_axis=0, concat_axis=0, tiled=True),
    )
    remote_q, remote_k, remote_v = remote_pairs(
        got_query, got_grad, got_stats, k_tiles, v_tiles, key_index, live_in, scale
    )
    returned = lax.all_to_all(
        remote_q.astype(jnp.bfloat16), "seq", split_axis=0, concat_axis=0, tiled=True
    )
    empty = jnp.zeros((count_blocks, BLOCK, width), jnp.float32)
    grad_key = empty.at[key_index].add(remote_k.reshape(seq_size, BLOCK, width))
    grad_value = empty.at[key_index].add(remote_v.reshape(seq_size, BLOCK, width))
    grad_query = empty.at[send_query].add(
        returned.reshape(seq_size, BLOCK, width).astype(jnp.float32)
    )
    offsets = jnp.arange(3, dtype=jnp.int32)[:, None]
    band_index = (
        place * count_blocks + jnp.arange(count_blocks, dtype=jnp.int32)[None, :] + offsets - 1
    )
    band_ok = (
        ((band_index >= 0) & (band_index < count_blocks * seq_size)).astype(jnp.float32).reshape(-1)
    )
    rimmed = with_halo(jnp.stack([key, value]), (("seq", 1),), BLOCK)
    wide = rimmed.reshape(2, count_blocks + 2, BLOCK, heads_here, HD)
    band_keys = jnp.concatenate([wide[0, j : j + count_blocks] for j in range(3)])
    band_values = jnp.concatenate([wide[1, j : j + count_blocks] for j in range(3)])
    band_q, band_k, band_v = block_pairs(
        jnp.concatenate([q_tiles] * 3),
        jnp.concatenate([g_tiles] * 3),
        jnp.concatenate([stats] * 3, axis=1),
        band_keys,
        band_values,
        band_ok,
        scale,
    )
    grad_query = grad_query + jnp.sum(band_q.reshape(3, count_blocks, BLOCK, width), axis=0)
    spread_k = spread_terms(band_k.reshape(3, count_blocks, BLOCK, heads_here, HD))
    spread_v = spread_terms(band_v.reshape(3, count_blocks, BLOCK, heads_here, HD))
    both = jnp.stack([spread_k, spread_v]).reshape(2, count_blocks + 2, BLOCK, width)
    edges = jnp.stack([both[:, 0], both[:, count_blocks + 1]])
    arrived = with_halo(edges, (("seq", 0),), 1)
    own = both[:, 1 : count_blocks + 1]
    own = own.at[:, 0].add(arrived[0]).at[:, count_blocks - 1].add(arrived[3])
    grad_key = grad_key + own[0]
    grad_value = grad_value + own[1]
    return (
        grad_query.reshape(rows, width).astype(jnp.bfloat16),
        grad_key.reshape(rows, width).astype(jnp.bfloat16),
        grad_value.reshape(rows, width).astype(jnp.bfloat16),
    )


def dot(a, b, ca, cb):
    return lax.dot_general(a, b, (((ca,), (cb,)), ((), ())), preferred_element_type=F32)


FINE = ()
CHAINS = [(u, j) for u in range(6) for j in ((0, 1) if u in FINE else (2,))]


def last(u, j, d, half):
    if j < 2:
        return half if j == d else half - 1
    return half if u < 4 or d == 0 else half - 1


def plan(half, release=(0, 1, 4), lat=2.1, chunk=0.4, tab=4.0, bw=75.0, hop=0.3, iss=0.15):
    F, R = SLOTS, RELAY
    mid = half // 2
    steps = {}

    for u, j in CHAINS:
        cut = u > 3
        for d in range(2):
            for k in range(last(u, j, d, half) + 1):
                def size(n):
                    return 4 if u > 3 else 64 if n < half and j == 2 else 32
                sends = []
                if k < last(u, j, d, half) and not (cut and k == mid):
                    sends.append((("z", u, j, d, k + 1), d, size(k + 1), 1))
                if k == 0 and cut and mid < last(u, j, d, half):
                    sends.append((("z", u, j, d, mid + 1), d, size(mid + 1), mid + 1))
                needs = [("z", u, j, d, k - 1)] if k else []
                if k == 0 and 0 < u < 4:
                    pj = 0 if u - 1 in FINE else 2
                    needs = [("z", u - 1, pj, d, min(release[u - 1], half - 1))]
                awaits = [("z", u, j, d, k)] if k else []
                steps["z", u, j, d, k] = (needs, awaits, sends, 0.0)

    def all_in(u):
        return [("z", c, j, d, last(c, j, d, half)) for c, j in CHAINS if c == u for d in range(2)]

    steps["tab",] = (all_in(5), [], [], tab)
    stats_in = all_in(4)
    for u in (4, 5):
        steps["zq", u] = ([("tab",)] + all_in(u), [], [], 0.5)
    for h in range(2):
        got = [all_in(2 * h + t) for t in range(2)]
        pairs = []
        for i in range(OWN // 4):
            steps["own", h, i] = ([("tab",)] + stats_in + got[0] + got[1], [], [], 2 * chunk)
            pairs.append(("own", h, i))
        for d in range(2):
            for t in range(3):
                kib = 32 if t < 2 else 4
                needs = [("tab",)] + (got[t] if t < 2 else stats_in)
                if t < 2:
                    sends = [
                        (("yb", h, t, d), 2 + d, R * kib, 1),
                        (("y", h, t, d), 2 + d, (F - R) * kib, 1),
                    ]
                else:
                    sends = [(("yb", h, t, d), 2 + d, F * kib, 1)]
                steps["pk", h, t, d] = (needs, [], sends, 0.25)
                steps["f", h, t, d] = ([], [("yb", h, t, d)], [(("f", h, t, d), 2 + d, R * kib, 1)], 0.0)
            seen = [("f", h, t, d) for t in range(3)]
            ym = [("y", h, t, d) for t in range(2)]
            steps["far", h, d] = ([], seen, [(("r2", h, d), 3 - d, R * 32, 1)], R / 2 * chunk)
            steps["na", h, d] = (seen, ym, [(("r1", h, d, 0), 3 - d, (F - R) * 32, 1)], (F - R) / 2 * chunk)
            steps["nb", h, d] = (seen, [("r2", h, d)], [(("r1", h, d, 1), 3 - d, R * 32, 1)], R / 2 * chunk)
            pairs += [("far", h, d), ("na", h, d), ("nb", h, d)]
        back = [("r1", h, d, part) for d in range(2) for part in range(2)]
        steps["w", h] = (pairs, back, [], 0.1)
        steps["kv", h] = (pairs, [], [], 0.2)
        fin = []
        for d in range(2):
            for k in range(1, half + 1):
                awaits = [] if k in (1, mid + 1) else [("s", h, d, k - 1)]
                hops = mid + 1 if k == mid else 1
                if k in (mid, half):
                    fin.append(("s", h, d, k))
                sends = [(("s", h, d, k), 1 - d, 68 if k > 1 else 36, hops)]
                steps["s", h, d, k] = ([("w", h)], awaits, sends, 0.25)
        for t in range(2):
            steps["zq", 2 * h + t] = (got[t] + [("pk", h, t, 1)], [], [], 0.5)
        steps["yq", h] = ([("s", h, 0, half // 2 + 1)], [], [], 0.5)
        steps["e", h] = ([("w", h)], fin, [], 0.3)
    for s in list(steps):
        n, a, sd, c = steps[s]
        steps[s] = (n, a, sd, c + iss * (len(a) + len(sd)))
    sender = {m: (s, kib, hops) for s, (_, _, sends, _) in steps.items() for m, _, kib, hops in sends}
    after = {s: [] for s in steps}
    for s, (needs, awaits, _, _) in steps.items():
        for n in needs:
            after[n].append((s, 0.0))
        for m in awaits:
            f, kib, hops = sender[m]
            after[f].append((s, hops * kib / bw + lat + hop * (hops - 1)))
    way = {}

    def length(s):
        if s not in way:
            way[s] = steps[s][3] + max([gap + length(n) for n, gap in after[s]], default=0.0)
        return way[s]

    left = sorted(steps, key=lambda s: (-length(s), str(s)))
    now, free, arrival, done, order = 0.0, [0.0] * 4, {}, set(), []
    while left:
        ready = [
            (max([now] + [arrival[m] for m in steps[s][1]]), i)
            for i, s in enumerate(left)
            if all(n in done for n in steps[s][0]) and all(m in arrival for m in steps[s][1])
        ]
        now, i = min(ready)
        s = left.pop(i)
        now += steps[s][3]
        for m, link, kib, hops in steps[s][2]:
            begin = max(free[link], now)
            free[link] = begin + hops * kib / bw
            arrival[m] = begin + min(hops, 2) * kib / bw + lat + hop * (hops - 1)
        done.add(s)
        order.append(s)
    return order


def kernel(
    nz,
    remote_ref,
    count_ref,
    q_ref,
    k_ref,
    v_ref,
    o_ref,
    g_ref,
    lse_ref,
    dq_ref,
    dk_ref,
    dv_ref,
    over_ref,
    agq0,
    agq1,
    agg0,
    agg1,
    ags,
    meta,
    full,
    snd,
    rcv,
    fwd,
    psnd,
    prcv,
    pfwd,
    r2snd,
    r2rcv,
    r1snd,
    ret00,
    ret01,
    ret10,
    ret11,
    own0,
    own1,
    rsnd,
    rrcv,
    dkacc,
    dvacc,
    kt_ref,
    table,
    flags,
    lists,
    nxt,
    pos,
    idx,
    msk,
    oidx,
    omsk,
    t_sem,
    z_send,
    z_recv,
    y_send,
    y_recv,
    f_send,
    f_recv,
    r2_send,
    r2_recv,
    r1_send,
    r1_recv,
    s_send,
    s_recv,
):
    me = lax.axis_index("seq")
    y = me // nz
    z = me % nz
    half = nz // 2
    cands = 2 * nz
    scale = float(HD) ** -0.5
    zdev = [y * nz + lax.rem(z + 1, nz), y * nz + lax.rem(z + nz - 1, nz)]
    ydev = [lax.rem(y + 1, NY) * nz + z, lax.rem(y + NY - 1, NY) * nz + z]
    mid = half // 2
    zfar = [y * nz + lax.rem(z + mid + 1, nz), y * nz + lax.rem(z + nz - mid - 1, nz)]
    agq = [agq0, agq1]
    agg = [agg0, agg1]
    ret = [[ret00, ret01], [ret10, ret11]]
    own = [own0, own1]
    chain_refs = [agq0, agg0, agq1, agg1]

    barrier = pltpu.get_barrier_semaphore()
    for dev in zdev + zfar + ydev:
        pl.semaphore_signal(
            barrier, inc=1, device_id={"seq": dev}, device_id_type=pl.DeviceIdType.MESH
        )

    def put_blocks(ref, own_ref, h):
        for j in range(2):
            ref[2 * z + j] = own_ref[j * BLOCK : (j + 1) * BLOCK, h * HD : (h + 1) * HD]

    line = lax.broadcasted_iota(I32, (8, BLOCK), 0)
    lane = lax.broadcasted_iota(I32, (8, BLOCK), 1)

    def put_rows():
        rows = jnp.zeros((8, BLOCK), I32)
        for j in range(2):
            hit = jnp.where(jnp.abs(lane - (2 * me + j)) <= 1, 1, 0)
            for r in range(remote_ref.shape[1]):
                used = jnp.where(count_ref[j] > r, 1, 0)
                hit = jnp.maximum(hit, jnp.where(lane == remote_ref[j, r], used, 0))
            rows = jnp.where(line == j, hit, rows)
        meta[z] = rows

    def put_stats():
        for h in range(2):
            cols = slice(h * HD, (h + 1) * HD)
            for j in range(2):
                rows = slice(j * BLOCK, (j + 1) * BLOCK)
                prod = g_ref[rows, cols].astype(F32) * o_ref[rows, cols].astype(F32)
                at = 4 * h + 2 * j
                ags[z, at : at + 1, :] = lse_ref[h : h + 1, rows] * LOG2E
                ags[z, at + 1 : at + 2, :] = jnp.sum(prod.T, axis=0, keepdims=True)

    def put_rest():
        for h in range(2):
            for d in range(2):
                ret[h][d][SLOTS] = jnp.zeros((BLOCK, HD), BF16)
            own[h][OWN] = jnp.zeros((BLOCK, HD), F32)
            dkacc[h] = jnp.zeros((2 * BLOCK, HD), F32)
            dvacc[h] = jnp.zeros((2 * BLOCK, HD), F32)
            kt_ref[h] = k_ref[:, h * HD : (h + 1) * HD].T

    put_blocks(agq[0], q_ref, 0)
    put_rows()
    pl.semaphore_wait(barrier, 6)

    def remote(src, dst, send, recv, dev):
        return pltpu.make_async_remote_copy(
            src_ref=src,
            dst_ref=dst,
            send_sem=send,
            recv_sem=recv,
            device_id={"seq": dev},
            device_id_type=pl.DeviceIdType.MESH,
        )

    def z_view(u, j, d, k, at):
        if u > 3:
            return (ags, meta)[u - 4].at[at]
        if j == 2 and k < half:
            return chain_refs[u].at[pl.ds(2 * at, 2)]
        return chain_refs[u].at[pl.ds(2 * at + (d if j == 2 else j), 1)]

    def z_copy(u, j, d, k, receiving=False):
        direct = u > 3 and k == mid + 1
        hop = k if receiving else 0 if direct else k - 1
        at = lax.rem(z + nz - hop, nz) if d == 0 else lax.rem(z + hop, nz)
        view = z_view(u, j, d, k, at)
        c = CHAINS.index((u, j))
        sems = z_send.at[c, d, k - 1], z_recv.at[c, d, k - 1]
        return remote(view, view, *sems, (zfar if direct else zdev)[d])

    def z_step(u, j, d, k):
        if k > 0:
            z_copy(u, j, d, k, receiving=True).wait_recv()
        end = last(u, j, d, half)
        if k < end and not (u > 3 and k == mid):
            z_copy(u, j, d, k + 1).start()
        if k == 0 and u > 3 and mid < end:
            z_copy(u, j, d, mid + 1).start()

    def z_drain(u):
        for c, j in CHAINS:
            if c == u:
                for d in range(2):
                    for k in range(1, last(u, j, d, half) + 1):
                        z_copy(u, j, d, k).wait_send()

    def build_tables():
        copy = pltpu.make_async_copy(meta, table, t_sem)
        copy.start()
        copy.wait()

        def bit(c, yy, b):
            return table[c // 2, c % 2, lax.rem(y + yy, NY) * cands + 2 * z + b]

        def scan(c, carry):
            count = []
            for yy in range(NY):
                live = bit(c, yy, 0) | bit(c, yy, 1)
                flags[yy, c] = live
                count.append(carry[yy] + live)
            return tuple(count)

        zero = jnp.int32(0)
        n0, n1p, n2, n1m = lax.fori_loop(0, cands, scan, (zero,) * 4)
        up = lax.shift_right_arithmetic(n2 + n1m - n1p + 1, jnp.int32(1))
        up = jnp.minimum(jnp.maximum(up, jnp.maximum(n2 - RELAY, 0)), jnp.minimum(n2, RELAY))

        def place(c, carry):
            r2, bp, bm, ap, am, ro = carry
            l0, l1, l2, l3 = flags[0, c], flags[1, c], flags[2, c], flags[3, c]
            to_p = jnp.where(r2 < up, l2, 0)
            to_m = l2 - to_p
            front_p = l1 * (1 - to_p)
            front_m = l3 * (1 - to_m)

            def where_in(front, a, back, b):
                p = jnp.where(back > 0, SLOTS - 1 - b, jnp.where(front > 0, a, SLOTS))
                return jnp.minimum(jnp.maximum(p, 0), SLOTS)

            pos[0, c] = where_in(front_p, ap, to_p, bp)
            pos[1, c] = where_in(front_m, am, to_m, bm)
            pos[2, c] = jnp.minimum(jnp.where(l0 > 0, ro, OWN), OWN)
            lists[0, c] = front_p
            lists[1, c] = to_p
            lists[2, c] = front_m
            lists[3, c] = to_m
            lists[4, c] = l0
            return r2 + l2, bp + to_p, bm + to_m, ap + front_p, am + front_m, ro + l0

        _, bp, bm, ap, am, _ = lax.fori_loop(0, cands, place, (zero,) * 6)
        most = jnp.maximum(jnp.maximum(ap + bp, am + bm) - SLOTS, n0 - OWN)
        most = jnp.maximum(most, jnp.maximum(bp, bm) - RELAY)
        full[...] = jnp.broadcast_to(jnp.where(most > 0, 1.0, 0.0).astype(F32), (8, BLOCK))

        for n in range(5):
            nxt[n, cands] = jnp.int32(cands)
            nxt[n, cands + 1] = jnp.int32(cands)

        def back(i, carry):
            c = cands - 1 - i
            out = []
            for n in range(5):
                cur = jnp.where(lists[n, c] > 0, c, carry[n])
                nxt[n, c] = cur
                out.append(cur)
            return tuple(out)

        lax.fori_loop(0, cands, back, (jnp.int32(cands),) * 5)

        for d in range(2):
            front = nxt[2 * d, 0]
            fronts = []
            for p in range(SLOTS):
                fronts.append(front)
                front = nxt[2 * d, front + 1]
            tail = nxt[2 * d + 1, 0]
            tails = []
            for p in range(RELAY):
                tails.append(tail)
                tail = nxt[2 * d + 1, tail + 1]
            for p in range(SLOTS):
                c = fronts[p]
                live2 = jnp.int32(0)
                if p >= SLOTS - RELAY:
                    t = tails[SLOTS - 1 - p]
                    live2 = jnp.where(t < cands, 1, 0)
                    c = jnp.where(t < cands, t, c)
                live1 = jnp.where(c < cands, 1, 0)
                c = jnp.minimum(c, cands - 1)
                idx[d, p] = c
                yy = 1 if d == 0 else NY - 1
                msk[d, p, 0] = live1 * bit(c, yy, 0)
                msk[d, p, 1] = live1 * bit(c, yy, 1)
                msk[d, p, 2] = live2 * bit(c, 2, 0)
                msk[d, p, 3] = live2 * bit(c, 2, 1)
        cur = nxt[4, 0]
        for p in range(OWN):
            c = jnp.minimum(cur, cands - 1)
            live = jnp.where(cur < cands, 1, 0)
            oidx[p] = c
            omsk[0, p] = live * bit(c, 0, 0)
            omsk[1, p] = live * bit(c, 0, 1)
            if p + 1 < OWN:
                cur = nxt[4, cur + 1]

    def pairs(h, queries, grads, lse0, lse1, delta):
        cols = slice(h * HD, (h + 1) * HD)
        scores = dot(k_ref[:, cols], queries, 1, 1) * (scale * LOG2E)
        weights = jnp.concatenate(
            [jnp.exp2(scores[:BLOCK] - lse0), jnp.exp2(scores[BLOCK:] - lse1)], axis=0
        )
        dvacc[h] += dot(weights.astype(BF16), grads, 1, 0)
        grad_probs = dot(v_ref[:, cols], grads, 1, 1)
        grad_scores = (weights * (grad_probs - delta)).astype(BF16)
        dkacc[h] += dot(grad_scores, queries, 1, 0)
        return dot(kt_ref[h], grad_scores, 1, 0) * scale

    def stat_rows(h, c):
        tile = ags[c // 2]
        odd = c % 2 > 0
        lse = jnp.where(odd, tile[4 * h + 2 : 4 * h + 3], tile[4 * h : 4 * h + 1])
        delta = jnp.where(odd, tile[4 * h + 3 : 4 * h + 4], tile[4 * h + 1 : 4 * h + 2])
        return lse, delta

    def join(parts, axis):
        return jnp.concatenate(parts, axis=axis)

    def own_pairs(h, lo, hi):
        qs, gs, l0, l1, dl = [], [], [], [], []
        for p in range(lo, hi):
            c = oidx[p]
            lse, delta = stat_rows(h, c)
            qs.append(agq[h][c])
            gs.append(agg[h][c])
            l0.append(jnp.where(omsk[0, p] > 0, lse, DEAD))
            l1.append(jnp.where(omsk[1, p] > 0, lse, DEAD))
            dl.append(delta)
        got = pairs(h, join(qs, 0), join(gs, 0), join(l0, 1), join(l1, 1), join(dl, 1))
        for p in range(lo, hi):
            own[h][p] = got[:, (p - lo) * BLOCK : (p - lo + 1) * BLOCK]

    def packet_pairs(h, d, blocks, stats, row, lo, hi, put):
        queries = blocks[h, 0, d, lo:hi].reshape((hi - lo) * BLOCK, HD)
        grads = blocks[h, 1, d, lo:hi].reshape((hi - lo) * BLOCK, HD)

        def rows(r):
            return join([stats[h, d, p][r : r + 1] for p in range(lo, hi)], 1)

        got = pairs(h, queries, grads, rows(row), rows(row + 1), rows(4))
        for p in range(lo, hi):
            put(p, got[:, (p - lo) * BLOCK : (p - lo + 1) * BLOCK])

    def pack(h, t, d):
        if t < 2:
            source = (agq, agg)[t][h]

            for part in (1, 0):
                @pl.loop(FRONT * part, SLOTS if part else FRONT)
                def _(p):
                    snd[h, t, d, p] = source[idx[d, p]]

                y_copy(h, t, d, part).start()
        else:
            @pl.loop(0, SLOTS)
            def _(p):
                lse, delta = stat_rows(h, idx[d, p])
                tile = jnp.where(line == 4, delta, 0.0)
                tile = jnp.where(line == 5, full[0:1], tile)
                for r in range(4):
                    row = jnp.where(msk[d, p, r] > 0, lse, DEAD)
                    tile = jnp.where(line == r, row, tile)
                psnd[h, d, p] = tile

            y_copy(h, t, d, 1).start()

    def y_copy(h, t, d, part):
        at = pl.ds(FRONT, RELAY) if part else pl.ds(0, FRONT)
        if t == 2:
            src, dst = psnd.at[h, d], prcv.at[h, d]
        else:
            src, dst = snd.at[h, t, d, at], rcv.at[h, t, d, at]
        return remote(src, dst, y_send.at[h, t, d, part], y_recv.at[h, t, d, part], ydev[d])

    def f_copy(h, t, d):
        last = pl.ds(SLOTS - RELAY, RELAY)
        if t == 2:
            src, dst = prcv.at[h, d, last], pfwd.at[h, d]
        else:
            src, dst = rcv.at[h, t, d, last], fwd.at[h, t, d]
        return remote(src, dst, f_send.at[h, t, d], f_recv.at[h, t, d], ydev[d])

    def relay(h, t, d):
        y_copy(h, t, d, 1).wait_recv()
        f_copy(h, t, d).start()

    def r2_copy(h, d):
        return remote(
            r2snd.at[h, d], r2rcv.at[h, d], r2_send.at[h, d], r2_recv.at[h, d], ydev[1 - d]
        )

    def r1_copy(h, d, part):
        at = pl.ds(0, SLOTS - RELAY) if part == 0 else pl.ds(SLOTS - RELAY, RELAY)
        return remote(
            r1snd.at[h, d, at],
            ret[h][d].at[at],
            r1_send.at[h, d, part],
            r1_recv.at[h, d, part],
            ydev[1 - d],
        )

    def far_pairs(h, d):
        for t in range(3):
            f_copy(h, t, d).wait_recv()

        def put(p, got):
            r2snd[h, d, p] = got.astype(BF16)

        packet_pairs(h, d, fwd, pfwd, 2, 0, RELAY, put)
        r2_copy(h, d).start()

    def near_pairs(h, d):
        for t in range(2):
            y_copy(h, t, d, 0).wait_recv()

        def put(p, got):
            r1snd[h, d, p] = got.astype(BF16)

        packet_pairs(h, d, rcv, prcv, 0, 0, SLOTS - RELAY, put)
        r1_copy(h, d, 0).start()

    def relay_pairs(h, d):
        r2_copy(h, d).wait_recv()

        def put(p, got):
            back = r2rcv[h, d, p - (SLOTS - RELAY)].astype(F32)
            r1snd[h, d, p] = (got + back).astype(BF16)

        packet_pairs(h, d, rcv, prcv, 0, SLOTS - RELAY, SLOTS, put)
        r1_copy(h, d, 1).start()

    def terms(h, at, j):
        c = 2 * at + j
        total = own[h][pos[2, c]]
        for d in range(2):
            total = total + ret[h][d][pos[d, c]].astype(F32)
        return total

    block_rows = (slice(0, BLOCK), slice(BLOCK + 16, 2 * BLOCK + 16))
    flag_rows = slice(BLOCK, BLOCK + 16)

    def s_copy(h, d, k):
        at = pl.ds(0, 2 * BLOCK + 16)
        if k == 1:
            at = pl.ds(BLOCK * d, BLOCK + 16)
        return remote(
            rsnd.at[h, d, k - 1, at],
            rrcv.at[h, d, k - 1, at],
            s_send.at[h, d, k - 1],
            s_recv.at[h, d, k - 1],
            (zfar if k == mid else zdev)[1 - d],
        )

    def s_has(d, j, k):
        return k > 1 or j == d

    def s_step(h, d, k):
        dist = half + 1 - k
        at = lax.rem(z + nz - dist, nz) if d == 0 else lax.rem(z + dist, nz)
        flag = jnp.broadcast_to(full[0:1], (16, HD)).astype(BF16)
        total = {j: terms(h, at, j) for j in range(2) if s_has(d, j, k)}
        if k not in (1, mid + 1):
            s_copy(h, d, k - 1).wait_recv()
            flag = jnp.maximum(flag, rrcv[h, d, k - 2, flag_rows])
            for j in range(2):
                if s_has(d, j, k - 1):
                    total[j] = total[j] + rrcv[h, d, k - 2, block_rows[j]].astype(F32)
        for j in total:
            rsnd[h, d, k - 1, block_rows[j]] = total[j].astype(BF16)
        rsnd[h, d, k - 1, flag_rows] = flag
        s_copy(h, d, k).start()
        if k - 2 >= (mid + 1 if k > mid else 1):
            s_copy(h, d, k - 2).wait_send()

    def s_end(h):
        cols = slice(h * HD, (h + 1) * HD)
        any_full = full[0:1]
        total = [terms(h, z, j) for j in range(2)]
        for d in range(2):
            for k in (mid, half):
                s_copy(h, d, k).wait_recv()
                got = rrcv[h, d, k - 1, flag_rows].astype(F32)
                any_full = jnp.maximum(any_full, got[0:1])
                for j in range(2):
                    if s_has(d, j, k):
                        total[j] = total[j] + rrcv[h, d, k - 1, block_rows[j]].astype(F32)
            for lo, hi in ((1, mid), (mid + 1, half)):
                for k in range(max(lo, hi - 1), hi + 1):
                    s_copy(h, d, k).wait_send()
        for j in range(2):
            dq_ref[j * BLOCK : (j + 1) * BLOCK, cols] = total[j].T.astype(BF16)
        if h == 0:
            over_ref[...] = jnp.broadcast_to(any_full, (8, BLOCK))

    def r1_wait(h):
        for d in range(2):
            for part in range(2):
                r1_copy(h, d, part).wait_recv()
        if h == 0:
            seen = full[0:1]
            for d in range(2):
                seen = jnp.maximum(seen, jnp.maximum(prcv[0, d, 0][5:6], pfwd[0, d, 0][5:6]))
            full[...] = jnp.broadcast_to(seen, (8, BLOCK))

    def results(h):
        cols = slice(h * HD, (h + 1) * HD)
        dk_ref[:, cols] = (dkacc[h] * scale).astype(BF16)
        dv_ref[:, cols] = dvacc[h].astype(BF16)

    def y_drain(h):
        for d in range(2):
            for t in range(3):
                for part in range(2):
                    if t < 2 or part:
                        y_copy(h, t, d, part).wait_send()
                f_copy(h, t, d).wait_send()
            r2_copy(h, d).wait_send()
            for part in range(2):
                r1_copy(h, d, part).wait_send()

    do = {
        "z": z_step,
        "tab": build_tables,
        "own": lambda h, i: own_pairs(h, 4 * i, 4 * i + 4),
        "pk": pack,
        "f": relay,
        "far": far_pairs,
        "na": near_pairs,
        "nb": relay_pairs,
        "w": r1_wait,
        "kv": results,
        "zq": z_drain,
        "yq": y_drain,
        "s": s_step,
        "e": s_end,
    }
    steps = plan(half)
    ahead = [("z", 0, 2, d, 0) for d in range(2)]
    for step in ahead:
        do[step[0]](*step[1:])
    put_stats()
    for u in range(1, 4):
        put_blocks(chain_refs[u], (q_ref, g_ref)[u % 2], u // 2)
    put_rest()
    for step in steps:
        if step not in ahead:
            do[step[0]](*step[1:])


def fast(nz, remote, count, query, key, value, output, grad_out, logsumexp):
    rows, width = query.shape
    half = nz // 2
    blocks = (2 * nz, BLOCK, HD)
    vmem, dma = pltpu.VMEM, pltpu.SemaphoreType.DMA
    smem = pltpu.SMEM
    outs = [jax.ShapeDtypeStruct((rows, width), BF16)] * 3
    outs.append(jax.ShapeDtypeStruct((8, BLOCK), F32))
    in_vmem = pl.BlockSpec(memory_space=pltpu.VMEM)
    scratch = [
        *[vmem(blocks, BF16)] * 4,
        vmem((nz, 8, BLOCK), F32),
        vmem((nz, 8, BLOCK), I32),
        vmem((8, BLOCK), F32),
        vmem((2, 2, 2, SLOTS, BLOCK, HD), BF16),
        vmem((2, 2, 2, SLOTS, BLOCK, HD), BF16),
        vmem((2, 2, 2, RELAY, BLOCK, HD), BF16),
        vmem((2, 2, SLOTS, 8, BLOCK), F32),
        vmem((2, 2, SLOTS, 8, BLOCK), F32),
        vmem((2, 2, RELAY, 8, BLOCK), F32),
        vmem((2, 2, RELAY, BLOCK, HD), BF16),
        vmem((2, 2, RELAY, BLOCK, HD), BF16),
        vmem((2, 2, SLOTS, BLOCK, HD), BF16),
        *[vmem((SLOTS + 1, BLOCK, HD), BF16)] * 4,
        *[vmem((OWN + 1, BLOCK, HD), F32)] * 2,
        vmem((2, 2, half, 2 * BLOCK + 16, HD), BF16),
        vmem((2, 2, half, 2 * BLOCK + 16, HD), BF16),
        vmem((2, 2 * BLOCK, HD), F32),
        vmem((2, 2 * BLOCK, HD), F32),
        vmem((2, HD, 2 * BLOCK), BF16),
        smem((nz, 8, BLOCK), I32),
        smem((NY, 2 * nz), I32),
        smem((5, 2 * nz), I32),
        smem((5, 2 * nz + 2), I32),
        smem((3, 2 * nz), I32),
        smem((2, SLOTS), I32),
        smem((2, SLOTS, 4), I32),
        smem((OWN,), I32),
        smem((2, OWN), I32),
        pltpu.SemaphoreType.DMA,
        *[dma((len(CHAINS), 2, half))] * 2,
        *[dma((2, 3, 2, 2))] * 2,
        *[dma((2, 3, 2))] * 2,
        *[dma((2, 2))] * 2,
        *[dma((2, 2, 2))] * 2,
        *[dma((2, 2, half))] * 2,
    ]
    return pl.pallas_call(
        functools.partial(kernel, nz),
        out_shape=outs,
        in_specs=[pl.BlockSpec(memory_space=pltpu.SMEM)] * 2 + [in_vmem] * 6,
        out_specs=[in_vmem] * 4,
        scratch_shapes=scratch,
        compiler_params=pltpu.CompilerParams(
            collective_id=0, has_side_effects=True, vmem_limit_bytes=48 * 1024 * 1024
        ),
        cost_estimate=pl.CostEstimate(
            flops=4 * 10**9, bytes_accessed=4 * 2**20, transcendentals=5 * 10**6
        ),
    )(remote, count, query, key, value, output, grad_out, logsumexp)


def per_device(query, key, value, output, grad_out, logsumexp, remote_blocks, remote_count):
    nz = lax.axis_size("seq") // NY
    *found, over = fast(
        nz, remote_blocks, remote_count, query, key, value, output, grad_out, logsumexp
    )
    return lax.cond(
        over[0, 0] > 0,
        lambda: general(
            query, key, value, output, grad_out, logsumexp, remote_blocks, remote_count
        ),
        lambda: tuple(found),
    )


def solution(mesh):
    return jax.shard_map(
        per_device,
        mesh=mesh,
        in_specs=(
            P("seq", "head"),
            P("seq", "head"),
            P("seq", "head"),
            P("seq", "head"),
            P("seq", "head"),
            P("head", "seq"),
            P("seq", None),
            P("seq"),
        ),
        out_specs=(P("seq", "head"), P("seq", "head"), P("seq", "head")),
        check_vma=False,
    )
```

```python
import functools

import jax
import jax.numpy as jnp
from jax import lax
from jax.experimental import pallas as pl
from jax.experimental.pallas import tpu as pltpu
from jax.sharding import PartitionSpec as P

HD = 128
BLOCK = 128
NY = 4
GROUPS = ((4, 4, 4), (5, 5), (5, 5), (5, 5))
CAPS = tuple(sum(sizes) for sizes in GROUPS)
FIRST = tuple(sum(CAPS[:yy]) for yy in range(NY))
EMPTY = sum(CAPS)
DEAD = 1e30
LOG2E = 1.4426950408889634
F32 = jnp.float32
BF16 = jnp.bfloat16
I32 = jnp.int32


def with_halo(cells, sides, width):
    for axis, dim in sides:
        count = lax.axis_size(axis)
        ends = count - 1
        head = lax.slice_in_dim(cells, 0, width, axis=dim)
        tail = lax.slice_in_dim(cells, cells.shape[dim] - width, cells.shape[dim], axis=dim)
        cells = jnp.concatenate(
            [
                lax.ppermute(tail, axis, [(i, (i + 1) % count) for i in range(ends)]),
                cells,
                lax.ppermute(head, axis, [((i + 1) % count, i) for i in range(ends)]),
            ],
            axis=dim,
        )
    return cells


def block_pairs(queries, grads, stats, keys, values, valid, scale):
    scores = (
        jnp.einsum("pxhd,pyhd->phxy", queries, keys, preferred_element_type=jnp.float32) * scale
    )
    weights = jnp.exp(scores - stats[0][..., None]) * valid[:, None, None, None]
    probs = weights.astype(jnp.bfloat16)
    grad_values = jnp.einsum("phxy,pxhd->pyhd", probs, grads, preferred_element_type=jnp.float32)
    grad_probs = jnp.einsum("pxhd,pyhd->phxy", grads, values, preferred_element_type=jnp.float32)
    grad_scores = (weights * (grad_probs - stats[1][..., None])).astype(jnp.bfloat16)
    grad_queries = (
        jnp.einsum("phxy,pyhd->pxhd", grad_scores, keys, preferred_element_type=jnp.float32) * scale
    )
    grad_keys = (
        jnp.einsum("phxy,pxhd->pyhd", grad_scores, queries, preferred_element_type=jnp.float32)
        * scale
    )
    return (grad_queries, grad_keys, grad_values)


def spread_terms(terms):
    padded = jnp.pad(terms[0], ((0, 2), (0, 0), (0, 0), (0, 0)))
    padded = padded + jnp.pad(terms[1], ((1, 1), (0, 0), (0, 0), (0, 0)))
    return padded + jnp.pad(terms[2], ((2, 0), (0, 0), (0, 0), (0, 0)))


def remote_pairs(
    part_query, part_grad, part_stats, key_table, value_table, key_index, live_in, scale
):
    senders = part_query.shape[0]
    head_count = part_query.shape[2]
    groups = senders // 8

    def remote_group(items):
        one_q, one_g, one_s, one_k, one_l = items
        return block_pairs(
            one_q,
            one_g,
            one_s.transpose(1, 0, 2, 3),
            key_table[one_k],
            value_table[one_k],
            one_l,
            scale,
        )

    group_shape = (groups, 8, BLOCK, head_count, HD)
    found_q, found_k, found_v = lax.map(
        remote_group,
        (
            part_query.reshape(group_shape),
            part_grad.reshape(group_shape),
            part_stats.reshape(groups, 8, 2, head_count, BLOCK),
            key_index.reshape(groups, 8),
            live_in.reshape(groups, 8),
        ),
    )
    out_shape = (senders, BLOCK, head_count, HD)
    return (found_q.reshape(out_shape), found_k.reshape(out_shape), found_v.reshape(out_shape))


def general(query, key, value, output, grad_out, logsumexp, remote_blocks, remote_count):
    seq_size = lax.axis_size("seq")
    place = lax.axis_index("seq")
    rows, width = query.shape
    count_blocks = rows // BLOCK
    heads_here = width // HD
    scale = float(HD) ** (-0.5)
    shape_four = (count_blocks, BLOCK, heads_here, HD)
    q_tiles = query.reshape(shape_four)
    g_tiles = grad_out.reshape(shape_four)
    k_tiles = key.reshape(shape_four)
    v_tiles = value.reshape(shape_four)
    delta = jnp.sum(
        grad_out.astype(jnp.float32).reshape(shape_four)
        * output.astype(jnp.float32).reshape(shape_four),
        axis=3,
    )
    stats = jnp.stack(
        [
            logsumexp.reshape(heads_here, count_blocks, BLOCK).transpose(1, 0, 2),
            delta.transpose(0, 2, 1),
        ]
    )
    slots_used = (
        jnp.arange(remote_blocks.shape[1], dtype=jnp.int32)[None, :] < remote_count[:, None]
    )
    owners = remote_blocks // count_blocks
    local_key = remote_blocks % count_blocks
    match = (
        (owners[:, :, None] == jnp.arange(seq_size, dtype=jnp.int32)[None, None, :])
        & slots_used[:, :, None]
    ).astype(jnp.int32)
    live = jnp.sum(match, axis=(0, 1))
    send_query = jnp.sum(
        match * jnp.arange(count_blocks, dtype=jnp.int32)[:, None, None], axis=(0, 1)
    )
    send_key = jnp.sum(match * local_key[:, :, None], axis=(0, 1))
    meta = jnp.stack([send_key, live], axis=1).astype(jnp.float32)
    got_stats, got_meta = (
        lax.all_to_all(
            stats[:, send_query].transpose(1, 0, 2, 3),
            "seq",
            split_axis=0,
            concat_axis=0,
            tiled=True,
        ),
        lax.all_to_all(meta, "seq", split_axis=0, concat_axis=0, tiled=True),
    )
    key_index = got_meta[:, 0].astype(jnp.int32)
    live_in = got_meta[:, 1]
    got_query, got_grad = (
        lax.all_to_all(q_tiles[send_query], "seq", split_axis=0, concat_axis=0, tiled=True),
        lax.all_to_all(g_tiles[send_query], "seq", split_axis=0, concat_axis=0, tiled=True),
    )
    remote_q, remote_k, remote_v = remote_pairs(
        got_query, got_grad, got_stats, k_tiles, v_tiles, key_index, live_in, scale
    )
    returned = lax.all_to_all(
        remote_q.astype(jnp.bfloat16), "seq", split_axis=0, concat_axis=0, tiled=True
    )
    empty = jnp.zeros((count_blocks, BLOCK, width), jnp.float32)
    grad_key = empty.at[key_index].add(remote_k.reshape(seq_size, BLOCK, width))
    grad_value = empty.at[key_index].add(remote_v.reshape(seq_size, BLOCK, width))
    grad_query = empty.at[send_query].add(
        returned.reshape(seq_size, BLOCK, width).astype(jnp.float32)
    )
    offsets = jnp.arange(3, dtype=jnp.int32)[:, None]
    band_index = (
        place * count_blocks + jnp.arange(count_blocks, dtype=jnp.int32)[None, :] + offsets - 1
    )
    band_ok = (
        ((band_index >= 0) & (band_index < count_blocks * seq_size)).astype(jnp.float32).reshape(-1)
    )
    rimmed = with_halo(jnp.stack([key, value]), (("seq", 1),), BLOCK)
    wide = rimmed.reshape(2, count_blocks + 2, BLOCK, heads_here, HD)
    band_keys = jnp.concatenate([wide[0, j : j + count_blocks] for j in range(3)])
    band_values = jnp.concatenate([wide[1, j : j + count_blocks] for j in range(3)])
    band_q, band_k, band_v = block_pairs(
        jnp.concatenate([q_tiles] * 3),
        jnp.concatenate([g_tiles] * 3),
        jnp.concatenate([stats] * 3, axis=1),
        band_keys,
        band_values,
        band_ok,
        scale,
    )
    grad_query = grad_query + jnp.sum(band_q.reshape(3, count_blocks, BLOCK, width), axis=0)
    spread_k = spread_terms(band_k.reshape(3, count_blocks, BLOCK, heads_here, HD))
    spread_v = spread_terms(band_v.reshape(3, count_blocks, BLOCK, heads_here, HD))
    both = jnp.stack([spread_k, spread_v]).reshape(2, count_blocks + 2, BLOCK, width)
    edges = jnp.stack([both[:, 0], both[:, count_blocks + 1]])
    arrived = with_halo(edges, (("seq", 0),), 1)
    own = both[:, 1 : count_blocks + 1]
    own = own.at[:, 0].add(arrived[0]).at[:, count_blocks - 1].add(arrived[3])
    grad_key = grad_key + own[0]
    grad_value = grad_value + own[1]
    return (
        grad_query.reshape(rows, width).astype(jnp.bfloat16),
        grad_key.reshape(rows, width).astype(jnp.bfloat16),
        grad_value.reshape(rows, width).astype(jnp.bfloat16),
    )


def dot(a, b, ca, cb):
    return lax.dot_general(a, b, (((ca,), (cb,)), ((), ())), preferred_element_type=F32)


CUT = ()
FINE = (0, 1)
CHAINS = [(u, j) for u in range(6) for j in ((0, 1) if u in FINE else (2,))]


def last(u, j, d, half):
    if j < 2:
        return half if j == d else half - 1
    return half if u < 4 or d == 0 else half - 1


def plan(half, release=(1, 4, 0), lat=1.8, chunk=0.3, tab=4.0, bw=47.0, hop=0.3, iss=0.1):
    mid = half // 2
    steps = {}

    for u, j in CHAINS:
        cut = u > 3
        for d in range(2):
            for k in range(last(u, j, d, half) + 1):
                def size(n):
                    return 4 if u > 3 else 64 if n < half and j == 2 else 32
                sends = []
                if k < last(u, j, d, half) and not (cut and k == mid):
                    sends.append((("z", u, j, d, k + 1), d, size(k + 1), 1))
                if k == 0 and cut and mid < last(u, j, d, half):
                    sends.append((("z", u, j, d, mid + 1), d, size(mid + 1), mid + 1))
                needs = [("z", u, j, d, k - 1)] if k else []
                if k == 0 and 0 < u < 4:
                    pj = 0 if u - 1 in FINE else 2
                    needs = [("z", u - 1, pj, d, min(release[u - 1], half - 1))]
                awaits = [("z", u, j, d, k)] if k else []
                steps["z", u, j, d, k] = (needs, awaits, sends, 0.0)

    def all_in(u):
        return [("z", c, j, d, last(c, j, d, half)) for c, j in CHAINS if c == u for d in range(2)]

    for d in range(2):
        steps["ks", d] = ([("z", *CHAINS[0], 1, 0)], [], [(("k", d), 3 - d, 256, 1)], 0.1)
        steps["kw", d] = ([], [("k", d)], [(("k2", d), 3 - d, 128, 1)], 0.4)
    steps["kx",] = ([("kw", 0), ("kw", 1)], [("k2", 0), ("k2", 1)], [], 0.4)
    steps["tab",] = (all_in(5), [], [], tab)
    stats_in = all_in(4)
    for u in (4, 5):
        steps["zq", u] = ([("tab",)] + all_in(u), [], [], 0.5)
    for h in range(2):
        got = [all_in(2 * h + t) for t in range(2)]
        pairs = []
        for yy in (2, 1, 3, 0):
            keys = {0: [], 1: [("kw", 0)], 2: [("kx",)], 3: [("kw", 1)]}[yy]
            for i, size in enumerate(GROUPS[yy]):
                needs = [("tab",)] + stats_in + got[0] + got[1] + keys
                steps["own", h, yy, i] = (needs, [], [], size / 2 * chunk)
                pairs.append(("own", h, yy, i))
        far = [p for p in pairs if p[2] == 2]
        steps["d1", h] = (far, [], [(("d1", h, d), 2 + d, 68, 1) for d in range(2)], 0.2)
        sends = [(("d2", h, d), 2 + d, 132, 1) for d in range(2)]
        steps["d2", h] = (pairs + [("d1", h)], [("d1", h, d) for d in range(2)], sends, 0.3)
        steps["kv", h] = ([("d2", h)], [("d2", h, d) for d in range(2)], [], 0.3)
        fin = []
        for d in range(2):
            for j in range(2):
                for k in range(1, half + 1):
                    if k > 1 or j == d:
                        cut = h in CUT
                        first = k == 1 or (k == 2 and j != d) or (cut and k == mid + 1)
                        awaits = [] if first else [("s", h, d, j, k - 1)]
                        hops = mid + 1 if cut and k == mid else 1
                        if k == half or (cut and k == mid):
                            fin.append(("s", h, d, j, k))
                        steps["s", h, d, j, k] = (pairs + [("kv", 0)] * h, awaits, [(("s", h, d, j, k), 1 - d, 32, hops)], 0.12)
        for t in range(2):
            steps["zq", 2 * h + t] = (got[t] + pairs, [], [], 0.5)
        steps["yq", h] = ([("kv", h)], [], [], 0.5)
        steps["e", h] = (pairs, fin, [], 0.3)
    for s in list(steps):
        n, a, sd, c = steps[s]
        steps[s] = (n, a, sd, c + iss * (len(a) + len(sd)))
    sender = {m: (s, kib, hops) for s, (_, _, sends, _) in steps.items() for m, _, kib, hops in sends}
    after = {s: [] for s in steps}
    for s, (needs, awaits, _, _) in steps.items():
        for n in needs:
            after[n].append((s, 0.0))
        for m in awaits:
            f, kib, hops = sender[m]
            after[f].append((s, hops * kib / bw + lat + hop * (hops - 1)))
    way = {}

    def length(s):
        if s not in way:
            way[s] = steps[s][3] + max([gap + length(n) for n, gap in after[s]], default=0.0)
        return way[s]

    left = sorted(steps, key=lambda s: (-length(s), str(s)))
    now, free, arrival, done, order = 0.0, [0.0] * 4, {}, set(), []
    while left:
        ready = [
            (max([now] + [arrival[m] for m in steps[s][1]]), i)
            for i, s in enumerate(left)
            if all(n in done for n in steps[s][0]) and all(m in arrival for m in steps[s][1])
        ]
        now, i = min(ready)
        s = left.pop(i)
        now += steps[s][3]
        for m, link, kib, hops in steps[s][2]:
            begin = max(free[link], now)
            free[link] = begin + hops * kib / bw
            arrival[m] = begin + min(hops, 2) * kib / bw + lat + hop * (hops - 1)
        done.add(s)
        order.append(s)
    return order


def kernel(
    nz,
    remote_ref,
    count_ref,
    q_ref,
    k_ref,
    v_ref,
    o_ref,
    g_ref,
    lse_ref,
    dq_ref,
    dk_ref,
    dv_ref,
    over_ref,
    agq0,
    agq1,
    agg0,
    agg1,
    ags,
    meta,
    full,
    nkv,
    nkt,
    d1snd,
    d1rcv,
    dsnd,
    drcv,
    own0,
    own1,
    rsnd,
    rrcv,
    dkacc,
    dvacc,
    kt_ref,
    table,
    lists,
    nxt,
    pos,
    idx,
    msk,
    t_sem,
    z_send,
    z_recv,
    k_send,
    k_recv,
    k2_send,
    k2_recv,
    d1_send,
    d1_recv,
    d_send,
    d_recv,
    s_send,
    s_recv,
):
    me = lax.axis_index("seq")
    y = me // nz
    z = me % nz
    half = nz // 2
    cands = 2 * nz
    scale = float(HD) ** -0.5
    zdev = [y * nz + lax.rem(z + 1, nz), y * nz + lax.rem(z + nz - 1, nz)]
    ydev = [lax.rem(y + 1, NY) * nz + z, lax.rem(y + NY - 1, NY) * nz + z]
    mid = half // 2
    zfar = [y * nz + lax.rem(z + mid + 1, nz), y * nz + lax.rem(z + nz - mid - 1, nz)]
    agq = [agq0, agq1]
    agg = [agg0, agg1]
    own = [own0, own1]
    chain_refs = [agq0, agg0, agq1, agg1]

    barrier = pltpu.get_barrier_semaphore()
    for dev in zdev + zfar + ydev:
        pl.semaphore_signal(
            barrier, inc=1, device_id={"seq": dev}, device_id_type=pl.DeviceIdType.MESH
        )

    def put_blocks(ref, own_ref, h):
        for j in range(2):
            ref[2 * z + j] = own_ref[j * BLOCK : (j + 1) * BLOCK, h * HD : (h + 1) * HD]

    line = lax.broadcasted_iota(I32, (8, BLOCK), 0)
    lane = lax.broadcasted_iota(I32, (8, BLOCK), 1)

    def put_rows():
        rows = jnp.zeros((8, BLOCK), I32)
        for j in range(2):
            hit = jnp.where(jnp.abs(lane - (2 * me + j)) <= 1, 1, 0)
            for r in range(remote_ref.shape[1]):
                used = jnp.where(count_ref[j] > r, 1, 0)
                hit = jnp.maximum(hit, jnp.where(lane == remote_ref[j, r], used, 0))
            rows = jnp.where(line == j, hit, rows)
        meta[z] = rows

    def put_stats():
        for h in range(2):
            cols = slice(h * HD, (h + 1) * HD)
            for j in range(2):
                rows = slice(j * BLOCK, (j + 1) * BLOCK)
                prod = g_ref[rows, cols].astype(F32) * o_ref[rows, cols].astype(F32)
                at = 4 * h + 2 * j
                ags[z, at : at + 1, :] = lse_ref[h : h + 1, rows] * LOG2E
                ags[z, at + 1 : at + 2, :] = jnp.sum(prod.T, axis=0, keepdims=True)

    def put_rest():
        for h in range(2):
            own[h][EMPTY] = jnp.zeros((HD, BLOCK), F32)
            for n in range(NY):
                dkacc[h, n] = jnp.zeros((2 * BLOCK, HD), F32)
                dvacc[h, n] = jnp.zeros((2 * BLOCK, HD), F32)
            kt_ref[h] = k_ref[:, h * HD : (h + 1) * HD].T

    put_blocks(agq[0], q_ref, 0)
    put_rows()
    pl.semaphore_wait(barrier, 6)

    def remote(src, dst, send, recv, dev):
        return pltpu.make_async_remote_copy(
            src_ref=src,
            dst_ref=dst,
            send_sem=send,
            recv_sem=recv,
            device_id={"seq": dev},
            device_id_type=pl.DeviceIdType.MESH,
        )

    def z_view(u, j, d, k, at):
        if u > 3:
            return (ags, meta)[u - 4].at[at]
        if j == 2 and k < half:
            return chain_refs[u].at[pl.ds(2 * at, 2)]
        return chain_refs[u].at[pl.ds(2 * at + (d if j == 2 else j), 1)]

    def z_copy(u, j, d, k, receiving=False):
        direct = u > 3 and k == mid + 1
        hop = k if receiving else 0 if direct else k - 1
        at = lax.rem(z + nz - hop, nz) if d == 0 else lax.rem(z + hop, nz)
        view = z_view(u, j, d, k, at)
        c = CHAINS.index((u, j))
        sems = z_send.at[c, d, k - 1], z_recv.at[c, d, k - 1]
        return remote(view, view, *sems, (zfar if direct else zdev)[d])

    def z_step(u, j, d, k):
        if k > 0:
            z_copy(u, j, d, k, receiving=True).wait_recv()
        end = last(u, j, d, half)
        if k < end and not (u > 3 and k == mid):
            z_copy(u, j, d, k + 1).start()
        if k == 0 and u > 3 and mid < end:
            z_copy(u, j, d, mid + 1).start()

    def z_drain(u):
        for c, j in CHAINS:
            if c == u:
                for d in range(2):
                    for k in range(1, last(u, j, d, half) + 1):
                        z_copy(u, j, d, k).wait_send()

    def build_tables():
        copy = pltpu.make_async_copy(meta, table, t_sem)
        copy.start()
        copy.wait()

        def bit(c, yy, b):
            return table[c // 2, c % 2, lax.rem(y + yy, NY) * cands + 2 * z + b]

        def scan(c, carry):
            count = []
            for yy in range(NY):
                live = bit(c, yy, 0) | bit(c, yy, 1)
                place = jnp.where(carry[yy] < CAPS[yy], FIRST[yy] + carry[yy], EMPTY)
                pos[yy, c] = jnp.where(live > 0, place, EMPTY)
                lists[yy, c] = live
                count.append(carry[yy] + live)
            return tuple(count)

        counts = lax.fori_loop(0, cands, scan, (jnp.int32(0),) * NY)
        most = counts[0] - CAPS[0]
        for yy in range(1, NY):
            most = jnp.maximum(most, counts[yy] - CAPS[yy])
        full[...] = jnp.broadcast_to(jnp.where(most > 0, 1.0, 0.0).astype(F32), (8, BLOCK))

        for yy in range(NY):
            nxt[yy, cands] = jnp.int32(cands)
            nxt[yy, cands + 1] = jnp.int32(cands)

        def back(i, carry):
            c = cands - 1 - i
            out = []
            for yy in range(NY):
                cur = jnp.where(lists[yy, c] > 0, c, carry[yy])
                nxt[yy, c] = cur
                out.append(cur)
            return tuple(out)

        lax.fori_loop(0, cands, back, (jnp.int32(cands),) * NY)

        for yy in range(NY):
            cur = nxt[yy, 0]
            for p in range(FIRST[yy], FIRST[yy] + CAPS[yy]):
                c = jnp.minimum(cur, cands - 1)
                live = jnp.where(cur < cands, 1, 0)
                idx[p] = c
                msk[0, p] = live * bit(c, yy, 0)
                msk[1, p] = live * bit(c, yy, 1)
                cur = nxt[yy, jnp.minimum(cur + 1, cands + 1)]

    def pairs(h, n, queries, grads, lse0, lse1, delta):
        cols = slice(h * HD, (h + 1) * HD)
        keys = nkv[n - 1, 0, :, cols] if n else k_ref[:, cols]
        values = nkv[n - 1, 1, :, cols] if n else v_ref[:, cols]
        scores = dot(keys, queries, 1, 1) * (scale * LOG2E)
        weights = jnp.concatenate(
            [jnp.exp2(scores[:BLOCK] - lse0), jnp.exp2(scores[BLOCK:] - lse1)], axis=0
        )
        dvacc[h, n] += dot(weights.astype(BF16), grads, 1, 0)
        grad_probs = dot(values, grads, 1, 1)
        grad_scores = (weights * (grad_probs - delta)).astype(BF16)
        dkacc[h, n] += dot(grad_scores, queries, 1, 0)
        return dot(nkt[n - 1, h] if n else kt_ref[h], grad_scores, 1, 0) * scale

    def stat_rows(h, c):
        tile = ags[c // 2]
        odd = c % 2 > 0
        lse = jnp.where(odd, tile[4 * h + 2 : 4 * h + 3], tile[4 * h : 4 * h + 1])
        delta = jnp.where(odd, tile[4 * h + 3 : 4 * h + 4], tile[4 * h + 1 : 4 * h + 2])
        return lse, delta

    def join(parts, axis):
        return jnp.concatenate(parts, axis=axis)

    def list_pairs(h, yy, i):
        lo = FIRST[yy] + sum(GROUPS[yy][:i])
        hi = lo + GROUPS[yy][i]
        qs, gs, l0, l1, dl = [], [], [], [], []
        for p in range(lo, hi):
            c = idx[p]
            lse, delta = stat_rows(h, c)
            qs.append(agq[h][c])
            gs.append(agg[h][c])
            l0.append(jnp.where(msk[0, p] > 0, lse, DEAD))
            l1.append(jnp.where(msk[1, p] > 0, lse, DEAD))
            dl.append(delta)
        n = (0, 1, 3, 2)[yy]
        got = pairs(h, n, join(qs, 0), join(gs, 0), join(l0, 1), join(l1, 1), join(dl, 1))
        for p in range(lo, hi):
            own[h][p] = got[:, (p - lo) * BLOCK : (p - lo + 1) * BLOCK]

    def k_copy(d, n):
        src = (k_ref, v_ref)[n]
        return remote(src, nkv.at[d, n], k_send.at[d, n], k_recv.at[d, n], ydev[1 - d])

    def keys_send(d):
        for n in range(2):
            k_copy(d, n).start()

    def k2_copy(d):
        src, dst = nkv.at[d, d], nkv.at[2, d]
        return remote(src, dst, k2_send.at[d], k2_recv.at[d], ydev[1 - d])

    def keys_wait(d):
        for n in range(2):
            k_copy(d, n).wait_recv()
        k2_copy(d).start()
        for h in range(2):
            nkt[d, h] = nkv[d, 0, :, h * HD : (h + 1) * HD].T

    def keys_end():
        for d in range(2):
            k2_copy(d).wait_recv()
        for h in range(2):
            nkt[2, h] = nkv[2, 0, :, h * HD : (h + 1) * HD].T

    def d1_copy(h, d):
        sems = d1_send.at[h, d], d1_recv.at[h, d]
        return remote(d1snd.at[h, d], d1rcv.at[h, d], *sems, ydev[d])

    def d_copy(h, d):
        return remote(dsnd.at[h, d], drcv.at[h, d], d_send.at[h, d], d_recv.at[h, d], ydev[d])

    def far_send(h):
        for d in range(2):
            d1snd[h, d, : 2 * BLOCK] = (dkacc, dvacc)[d][h, 3].astype(BF16)
            d1snd[h, d, 2 * BLOCK :] = jnp.broadcast_to(full[0:1], (16, HD)).astype(BF16)
            d1_copy(h, d).start()

    def near_send(h):
        seen = full[0:1]
        for d in range(2):
            d1_copy(h, d).wait_recv()
            seen = jnp.maximum(seen, d1rcv[h, d, 2 * BLOCK :].astype(F32)[0:1])
        for d in range(2):
            sums = [dkacc[h, 1 + d], dvacc[h, 1 + d]]
            sums[d] = sums[d] + d1rcv[h, d, : 2 * BLOCK].astype(F32)
            dsnd[h, d, 0 : 2 * BLOCK] = sums[0].astype(BF16)
            dsnd[h, d, 2 * BLOCK : 4 * BLOCK] = sums[1].astype(BF16)
            dsnd[h, d, 4 * BLOCK :] = jnp.broadcast_to(seen, (16, HD)).astype(BF16)
            d_copy(h, d).start()

    def terms(h, at, j):
        c = 2 * at + j
        total = own[h][pos[0, c]]
        for yy in range(1, NY):
            total = total + own[h][pos[yy, c]]
        return total

    def s_copy(h, d, j, k):
        at = pl.ds(0, BLOCK + 16 if h == 1 and j == d else BLOCK)
        return remote(
            rsnd.at[h, d, j, k - 1, at],
            rrcv.at[h, d, j, k - 1, at],
            s_send.at[h, d, j, k - 1],
            s_recv.at[h, d, j, k - 1],
            (zfar if h in CUT and k == mid else zdev)[1 - d],
        )

    extra = slice(BLOCK, BLOCK + 16)

    def s_step(h, d, j, k):
        dist = half + 1 - k
        at = lax.rem(z + nz - dist, nz) if d == 0 else lax.rem(z + dist, nz)
        total = terms(h, at, j)
        carries = h == 1 and j == d
        if carries:
            rsnd[h, d, j, k - 1, extra] = jnp.broadcast_to(full[0:1], (16, HD)).astype(BF16)
        cut = h in CUT
        if (k > 2 or (k == 2 and j == d)) and not (cut and k == mid + 1):
            s_copy(h, d, j, k - 1).wait_recv()
            total = total + rrcv[h, d, j, k - 2, :BLOCK].astype(F32)
            if carries:
                rsnd[h, d, j, k - 1, extra] = jnp.maximum(
                    rsnd[h, d, j, k - 1, extra], rrcv[h, d, j, k - 2, extra]
                )
        rsnd[h, d, j, k - 1, :BLOCK] = total.astype(BF16)
        s_copy(h, d, j, k).start()
        if k - 2 >= (mid + 1 if cut and k > mid else 1 if j == d else 2):
            s_copy(h, d, j, k - 2).wait_send()

    def s_end(h):
        cols = slice(h * HD, (h + 1) * HD)
        any_full = full[0:1]
        for j in range(2):
            total = terms(h, z, j)
            for d in range(2):
                for k in (mid, half) if h in CUT else (half,):
                    if k > 1 or j == d:
                        s_copy(h, d, j, k).wait_recv()
                        total = total + rrcv[h, d, j, k - 1, :BLOCK].astype(F32)
                        if h == 1 and j == d:
                            got = rrcv[h, d, j, k - 1, extra].astype(F32)
                            any_full = jnp.maximum(any_full, got[0:1])
                lo = 1 if j == d else 2
                for lo, hi in ((lo, mid), (mid + 1, half)) if h in CUT else ((lo, half),):
                    for k in range(max(lo, hi - 1), hi + 1):
                        s_copy(h, d, j, k).wait_send()
            dq_ref[j * BLOCK : (j + 1) * BLOCK, cols] = total.T.astype(BF16)
        if h == 1:
            over_ref[...] = jnp.broadcast_to(any_full, (8, BLOCK))

    def results(h):
        cols = slice(h * HD, (h + 1) * HD)
        grad_k, grad_v = dkacc[h, 0], dvacc[h, 0]
        seen = full[0:1]
        for d in range(2):
            d_copy(h, d).wait_recv()
            grad_k = grad_k + drcv[h, d, 0 : 2 * BLOCK].astype(F32)
            grad_v = grad_v + drcv[h, d, 2 * BLOCK : 4 * BLOCK].astype(F32)
            seen = jnp.maximum(seen, drcv[h, d, 4 * BLOCK :].astype(F32)[0:1])
        dk_ref[:, cols] = (grad_k * scale).astype(BF16)
        dv_ref[:, cols] = grad_v.astype(BF16)
        if h == 0:
            full[...] = jnp.broadcast_to(seen, (8, BLOCK))

    def y_drain(h):
        k2_copy(h).wait_send()
        for d in range(2):
            k_copy(d, h).wait_send()
            d1_copy(h, d).wait_send()
            d_copy(h, d).wait_send()

    do = {
        "z": z_step,
        "tab": build_tables,
        "own": list_pairs,
        "ks": keys_send,
        "kw": keys_wait,
        "kx": keys_end,
        "d1": far_send,
        "d2": near_send,
        "kv": results,
        "zq": z_drain,
        "yq": y_drain,
        "s": s_step,
        "e": s_end,
    }
    steps = plan(half)
    ahead = [("z", *c, d, 0) for c in CHAINS if c[0] == 0 for d in range(2)]
    ahead += [("ks", 0), ("ks", 1)]
    for step in ahead:
        do[step[0]](*step[1:])
    put_stats()
    for u in range(1, 4):
        put_blocks(chain_refs[u], (q_ref, g_ref)[u % 2], u // 2)
    put_rest()
    for step in steps:
        if step not in ahead:
            do[step[0]](*step[1:])


def fast(nz, remote, count, query, key, value, output, grad_out, logsumexp):
    rows, width = query.shape
    half = nz // 2
    blocks = (2 * nz, BLOCK, HD)
    vmem, dma = pltpu.VMEM, pltpu.SemaphoreType.DMA
    smem = pltpu.SMEM
    outs = [jax.ShapeDtypeStruct((rows, width), BF16)] * 3
    outs.append(jax.ShapeDtypeStruct((8, BLOCK), F32))
    in_vmem = pl.BlockSpec(memory_space=pltpu.VMEM)
    scratch = [
        *[vmem(blocks, BF16)] * 4,
        vmem((nz, 8, BLOCK), F32),
        vmem((nz, 8, BLOCK), I32),
        vmem((8, BLOCK), F32),
        vmem((3, 2, rows, width), BF16),
        vmem((3, 2, HD, 2 * BLOCK), BF16),
        vmem((2, 2, 2 * BLOCK + 16, HD), BF16),
        vmem((2, 2, 2 * BLOCK + 16, HD), BF16),
        vmem((2, 2, 4 * BLOCK + 16, HD), BF16),
        vmem((2, 2, 4 * BLOCK + 16, HD), BF16),
        *[vmem((EMPTY + 1, HD, BLOCK), F32)] * 2,
        vmem((2, 2, 2, half, BLOCK + 16, HD), BF16),
        vmem((2, 2, 2, half, BLOCK + 16, HD), BF16),
        vmem((2, NY, 2 * BLOCK, HD), F32),
        vmem((2, NY, 2 * BLOCK, HD), F32),
        vmem((2, HD, 2 * BLOCK), BF16),
        smem((nz, 8, BLOCK), I32),
        smem((NY, 2 * nz), I32),
        smem((NY, 2 * nz + 2), I32),
        smem((NY, 2 * nz), I32),
        smem((EMPTY,), I32),
        smem((2, EMPTY), I32),
        pltpu.SemaphoreType.DMA,
        *[dma((len(CHAINS), 2, half))] * 2,
        *[dma((2, 2))] * 2,
        *[dma((2,))] * 2,
        *[dma((2, 2))] * 2,
        *[dma((2, 2))] * 2,
        *[dma((2, 2, 2, half))] * 2,
    ]
    return pl.pallas_call(
        functools.partial(kernel, nz),
        out_shape=outs,
        in_specs=[pl.BlockSpec(memory_space=pltpu.SMEM)] * 2 + [in_vmem] * 6,
        out_specs=[in_vmem] * 4,
        scratch_shapes=scratch,
        compiler_params=pltpu.CompilerParams(
            collective_id=0, has_side_effects=True, vmem_limit_bytes=48 * 1024 * 1024
        ),
        cost_estimate=pl.CostEstimate(
            flops=4 * 10**9, bytes_accessed=4 * 2**20, transcendentals=5 * 10**6
        ),
    )(remote, count, query, key, value, output, grad_out, logsumexp)


def per_device(query, key, value, output, grad_out, logsumexp, remote_blocks, remote_count):
    nz = lax.axis_size("seq") // NY
    *found, over = fast(
        nz, remote_blocks, remote_count, query, key, value, output, grad_out, logsumexp
    )
    return lax.cond(
        over[0, 0] > 0,
        lambda: general(
            query, key, value, output, grad_out, logsumexp, remote_blocks, remote_count
        ),
        lambda: tuple(found),
    )


def solution(mesh):
    return jax.shard_map(
        per_device,
        mesh=mesh,
        in_specs=(
            P("seq", "head"),
            P("seq", "head"),
            P("seq", "head"),
            P("seq", "head"),
            P("seq", "head"),
            P("head", "seq"),
            P("seq", None),
            P("seq"),
        ),
        out_specs=(P("seq", "head"), P("seq", "head"), P("seq", "head")),
        check_vma=False,
    )
```

```python
import functools

import jax
import jax.numpy as jnp
from jax import lax
from jax.experimental import pallas as pl
from jax.experimental.pallas import tpu as pltpu
from jax.sharding import PartitionSpec as P

HD = 128
BLOCK = 128
NY = 4
GROUPS = ((6, 6), (10,), (10,), (10,))
CAPS = tuple(sum(sizes) for sizes in GROUPS)
FIRST = tuple(sum(CAPS[:yy]) for yy in range(NY))
EMPTY = sum(CAPS)
DEAD = 1e30
LOG2E = 1.4426950408889634
F32 = jnp.float32
BF16 = jnp.bfloat16
I32 = jnp.int32


def with_halo(cells, sides, width):
    for axis, dim in sides:
        count = lax.axis_size(axis)
        ends = count - 1
        head = lax.slice_in_dim(cells, 0, width, axis=dim)
        tail = lax.slice_in_dim(cells, cells.shape[dim] - width, cells.shape[dim], axis=dim)
        cells = jnp.concatenate(
            [
                lax.ppermute(tail, axis, [(i, (i + 1) % count) for i in range(ends)]),
                cells,
                lax.ppermute(head, axis, [((i + 1) % count, i) for i in range(ends)]),
            ],
            axis=dim,
        )
    return cells


def block_pairs(queries, grads, stats, keys, values, valid, scale):
    scores = (
        jnp.einsum("pxhd,pyhd->phxy", queries, keys, preferred_element_type=jnp.float32) * scale
    )
    weights = jnp.exp(scores - stats[0][..., None]) * valid[:, None, None, None]
    probs = weights.astype(jnp.bfloat16)
    grad_values = jnp.einsum("phxy,pxhd->pyhd", probs, grads, preferred_element_type=jnp.float32)
    grad_probs = jnp.einsum("pxhd,pyhd->phxy", grads, values, preferred_element_type=jnp.float32)
    grad_scores = (weights * (grad_probs - stats[1][..., None])).astype(jnp.bfloat16)
    grad_queries = (
        jnp.einsum("phxy,pyhd->pxhd", grad_scores, keys, preferred_element_type=jnp.float32) * scale
    )
    grad_keys = (
        jnp.einsum("phxy,pxhd->pyhd", grad_scores, queries, preferred_element_type=jnp.float32)
        * scale
    )
    return (grad_queries, grad_keys, grad_values)


def spread_terms(terms):
    padded = jnp.pad(terms[0], ((0, 2), (0, 0), (0, 0), (0, 0)))
    padded = padded + jnp.pad(terms[1], ((1, 1), (0, 0), (0, 0), (0, 0)))
    return padded + jnp.pad(terms[2], ((2, 0), (0, 0), (0, 0), (0, 0)))


def remote_pairs(
    part_query, part_grad, part_stats, key_table, value_table, key_index, live_in, scale
):
    senders = part_query.shape[0]
    head_count = part_query.shape[2]
    groups = senders // 8

    def remote_group(items):
        one_q, one_g, one_s, one_k, one_l = items
        return block_pairs(
            one_q,
            one_g,
            one_s.transpose(1, 0, 2, 3),
            key_table[one_k],
            value_table[one_k],
            one_l,
            scale,
        )

    group_shape = (groups, 8, BLOCK, head_count, HD)
    found_q, found_k, found_v = lax.map(
        remote_group,
        (
            part_query.reshape(group_shape),
            part_grad.reshape(group_shape),
            part_stats.reshape(groups, 8, 2, head_count, BLOCK),
            key_index.reshape(groups, 8),
            live_in.reshape(groups, 8),
        ),
    )
    out_shape = (senders, BLOCK, head_count, HD)
    return (found_q.reshape(out_shape), found_k.reshape(out_shape), found_v.reshape(out_shape))


def general(query, key, value, output, grad_out, logsumexp, remote_blocks, remote_count):
    seq_size = lax.axis_size("seq")
    place = lax.axis_index("seq")
    rows, width = query.shape
    count_blocks = rows // BLOCK
    heads_here = width // HD
    scale = float(HD) ** (-0.5)
    shape_four = (count_blocks, BLOCK, heads_here, HD)
    q_tiles = query.reshape(shape_four)
    g_tiles = grad_out.reshape(shape_four)
    k_tiles = key.reshape(shape_four)
    v_tiles = value.reshape(shape_four)
    delta = jnp.sum(
        grad_out.astype(jnp.float32).reshape(shape_four)
        * output.astype(jnp.float32).reshape(shape_four),
        axis=3,
    )
    stats = jnp.stack(
        [
            logsumexp.reshape(heads_here, count_blocks, BLOCK).transpose(1, 0, 2),
            delta.transpose(0, 2, 1),
        ]
    )
    slots_used = (
        jnp.arange(remote_blocks.shape[1], dtype=jnp.int32)[None, :] < remote_count[:, None]
    )
    owners = remote_blocks // count_blocks
    local_key = remote_blocks % count_blocks
    match = (
        (owners[:, :, None] == jnp.arange(seq_size, dtype=jnp.int32)[None, None, :])
        & slots_used[:, :, None]
    ).astype(jnp.int32)
    live = jnp.sum(match, axis=(0, 1))
    send_query = jnp.sum(
        match * jnp.arange(count_blocks, dtype=jnp.int32)[:, None, None], axis=(0, 1)
    )
    send_key = jnp.sum(match * local_key[:, :, None], axis=(0, 1))
    meta = jnp.stack([send_key, live], axis=1).astype(jnp.float32)
    got_stats, got_meta = (
        lax.all_to_all(
            stats[:, send_query].transpose(1, 0, 2, 3),
            "seq",
            split_axis=0,
            concat_axis=0,
            tiled=True,
        ),
        lax.all_to_all(meta, "seq", split_axis=0, concat_axis=0, tiled=True),
    )
    key_index = got_meta[:, 0].astype(jnp.int32)
    live_in = got_meta[:, 1]
    got_query, got_grad = (
        lax.all_to_all(q_tiles[send_query], "seq", split_axis=0, concat_axis=0, tiled=True),
        lax.all_to_all(g_tiles[send_query], "seq", split_axis=0, concat_axis=0, tiled=True),
    )
    remote_q, remote_k, remote_v = remote_pairs(
        got_query, got_grad, got_stats, k_tiles, v_tiles, key_index, live_in, scale
    )
    returned = lax.all_to_all(
        remote_q.astype(jnp.bfloat16), "seq", split_axis=0, concat_axis=0, tiled=True
    )
    empty = jnp.zeros((count_blocks, BLOCK, width), jnp.float32)
    grad_key = empty.at[key_index].add(remote_k.reshape(seq_size, BLOCK, width))
    grad_value = empty.at[key_index].add(remote_v.reshape(seq_size, BLOCK, width))
    grad_query = empty.at[send_query].add(
        returned.reshape(seq_size, BLOCK, width).astype(jnp.float32)
    )
    offsets = jnp.arange(3, dtype=jnp.int32)[:, None]
    band_index = (
        place * count_blocks + jnp.arange(count_blocks, dtype=jnp.int32)[None, :] + offsets - 1
    )
    band_ok = (
        ((band_index >= 0) & (band_index < count_blocks * seq_size)).astype(jnp.float32).reshape(-1)
    )
    rimmed = with_halo(jnp.stack([key, value]), (("seq", 1),), BLOCK)
    wide = rimmed.reshape(2, count_blocks + 2, BLOCK, heads_here, HD)
    band_keys = jnp.concatenate([wide[0, j : j + count_blocks] for j in range(3)])
    band_values = jnp.concatenate([wide[1, j : j + count_blocks] for j in range(3)])
    band_q, band_k, band_v = block_pairs(
        jnp.concatenate([q_tiles] * 3),
        jnp.concatenate([g_tiles] * 3),
        jnp.concatenate([stats] * 3, axis=1),
        band_keys,
        band_values,
        band_ok,
        scale,
    )
    grad_query = grad_query + jnp.sum(band_q.reshape(3, count_blocks, BLOCK, width), axis=0)
    spread_k = spread_terms(band_k.reshape(3, count_blocks, BLOCK, heads_here, HD))
    spread_v = spread_terms(band_v.reshape(3, count_blocks, BLOCK, heads_here, HD))
    both = jnp.stack([spread_k, spread_v]).reshape(2, count_blocks + 2, BLOCK, width)
    edges = jnp.stack([both[:, 0], both[:, count_blocks + 1]])
    arrived = with_halo(edges, (("seq", 0),), 1)
    own = both[:, 1 : count_blocks + 1]
    own = own.at[:, 0].add(arrived[0]).at[:, count_blocks - 1].add(arrived[3])
    grad_key = grad_key + own[0]
    grad_value = grad_value + own[1]
    return (
        grad_query.reshape(rows, width).astype(jnp.bfloat16),
        grad_key.reshape(rows, width).astype(jnp.bfloat16),
        grad_value.reshape(rows, width).astype(jnp.bfloat16),
    )


def dot(a, b, ca, cb):
    return lax.dot_general(a, b, (((ca,), (cb,)), ((), ())), preferred_element_type=F32)


CUT = ()
FINE = (0, 1)
CHAINS = [(u, j) for u in range(6) for j in ((0, 1) if u in FINE else (2,))]


def last(u, j, d, half):
    if j < 2:
        return half if j == d else half - 1
    return half if u < 4 or d == 0 else half - 1


def plan(half, release=(1, 2, 0), lat=1.8, chunk=0.2, tab=4.0, bw=47.0, hop=0.3, iss=0.1):
    mid = half // 2
    steps = {}

    for u, j in CHAINS:
        cut = u > 3
        for d in range(2):
            for k in range(last(u, j, d, half) + 1):
                def size(n):
                    return 4 if u > 3 else 64 if n < half and j == 2 else 32
                sends = []
                if k < last(u, j, d, half) and not (cut and k == mid):
                    sends.append((("z", u, j, d, k + 1), d, size(k + 1), 1))
                if k == 0 and cut and mid < last(u, j, d, half):
                    sends.append((("z", u, j, d, mid + 1), d, size(mid + 1), mid + 1))
                needs = [("z", u, j, d, k - 1)] if k else []
                if k == 0 and 0 < u < 4:
                    pj = 0 if u - 1 in FINE else 2
                    needs = [("z", u - 1, pj, d, min(release[u - 1], half - 1))]
                awaits = [("z", u, j, d, k)] if k else []
                steps["z", u, j, d, k] = (needs, awaits, sends, 0.0)

    def all_in(u):
        return [("z", c, j, d, last(c, j, d, half)) for c, j in CHAINS if c == u for d in range(2)]

    for d in range(2):
        steps["ks", d] = ([("z", *CHAINS[0], 1, 0)], [], [(("k", d), 3 - d, 256, 1)], 0.1)
        steps["kw", d] = ([], [("k", d)], [(("k2", d), 3 - d, 128, 1)], 0.4)
    steps["kx",] = ([("kw", 0), ("kw", 1)], [("k2", 0), ("k2", 1)], [], 0.4)
    steps["tab",] = (all_in(5), [], [], tab)
    stats_in = all_in(4)
    for u in (4, 5):
        steps["zq", u] = ([("tab",)] + all_in(u), [], [], 0.1)
    for h in range(2):
        got = [all_in(2 * h + t) for t in range(2)]
        pairs = []
        for yy in (2, 1, 3, 0):
            keys = {0: [], 1: [("kw", 0)], 2: [("kx",)], 3: [("kw", 1)]}[yy]
            for i, size in enumerate(GROUPS[yy]):
                needs = [("tab",)] + stats_in + got[0] + got[1] + keys
                steps["own", h, yy, i] = (needs, [], [], size / 2 * chunk)
                pairs.append(("own", h, yy, i))
        far = [p for p in pairs if p[2] == 2]
        steps["d1", h] = (far, [], [(("d1", h, d), 2 + d, 68, 1) for d in range(2)], 0.2)
        sends = [(("d2", h, d), 2 + d, 132, 1) for d in range(2)]
        steps["d2", h] = (pairs + [("d1", h)], [("d1", h, d) for d in range(2)], sends, 0.3)
        steps["kv", h] = ([("d2", h)], [("d2", h, d) for d in range(2)], [], 0.3)
        fin = []
        for d in range(2):
            for j in range(2):
                for k in range(1, half + 1):
                    if k > 1 or j == d:
                        cut = h in CUT
                        first = k == 1 or (k == 2 and j != d) or (cut and k == mid + 1)
                        awaits = [] if first else [("s", h, d, j, k - 1)]
                        hops = mid + 1 if cut and k == mid else 1
                        if k == half or (cut and k == mid):
                            fin.append(("s", h, d, j, k))
                        steps["s", h, d, j, k] = (pairs + [("kv", 0)] * h, awaits, [(("s", h, d, j, k), 1 - d, 32, hops)], 0.08)
        for t in range(2):
            steps["zq", 2 * h + t] = (got[t] + pairs, [], [], 0.1)
        steps["yq", h] = ([("kv", h)], [], [], 0.1)
        steps["e", h] = (pairs, fin, [], 0.3)
    for s in list(steps):
        n, a, sd, c = steps[s]
        steps[s] = (n, a, sd, c + iss * (len(a) + len(sd)))
    sender = {m: (s, kib, hops) for s, (_, _, sends, _) in steps.items() for m, _, kib, hops in sends}
    after = {s: [] for s in steps}
    for s, (needs, awaits, _, _) in steps.items():
        for n in needs:
            after[n].append((s, 0.0))
        for m in awaits:
            f, kib, hops = sender[m]
            after[f].append((s, hops * kib / bw + lat + hop * (hops - 1)))
    way = {}

    def length(s):
        if s not in way:
            way[s] = steps[s][3] + max([gap + length(n) for n, gap in after[s]], default=0.0)
        return way[s]

    left = sorted(steps, key=lambda s: (-length(s), str(s)))
    now, free, arrival, done, order = 0.0, [0.0] * 4, {}, set(), []
    while left:
        ready = [
            (max([now] + [arrival[m] for m in steps[s][1]]), i)
            for i, s in enumerate(left)
            if all(n in done for n in steps[s][0]) and all(m in arrival for m in steps[s][1])
        ]
        now, i = min(ready)
        s = left.pop(i)
        now += steps[s][3]
        for m, link, kib, hops in steps[s][2]:
            begin = max(free[link], now)
            free[link] = begin + hops * kib / bw
            arrival[m] = begin + min(hops, 2) * kib / bw + lat + hop * (hops - 1)
        done.add(s)
        order.append(s)
    return order


def kernel(
    nz,
    remote_ref,
    count_ref,
    q_ref,
    k_ref,
    v_ref,
    o_ref,
    g_ref,
    lse_ref,
    dq_ref,
    dk_ref,
    dv_ref,
    over_ref,
    agq0,
    agq1,
    agg0,
    agg1,
    ags,
    meta,
    full,
    nkv,
    nkt,
    d1snd,
    d1rcv,
    dsnd,
    drcv,
    own0,
    own1,
    rsnd,
    rrcv,
    dkacc,
    dvacc,
    kt_ref,
    table,
    lists,
    nxt,
    pos,
    idx,
    msk,
    t_sem,
    z_send,
    z_recv,
    k_send,
    k_recv,
    k2_send,
    k2_recv,
    d1_send,
    d1_recv,
    d_send,
    d_recv,
    s_send,
    s_recv,
):
    me = lax.axis_index("seq")
    y = me // nz
    z = me % nz
    half = nz // 2
    cands = 2 * nz
    scale = float(HD) ** -0.5
    zdev = [y * nz + lax.rem(z + 1, nz), y * nz + lax.rem(z + nz - 1, nz)]
    ydev = [lax.rem(y + 1, NY) * nz + z, lax.rem(y + NY - 1, NY) * nz + z]
    mid = half // 2
    zfar = [y * nz + lax.rem(z + mid + 1, nz), y * nz + lax.rem(z + nz - mid - 1, nz)]
    agq = [agq0, agq1]
    agg = [agg0, agg1]
    own = [own0, own1]
    chain_refs = [agq0, agg0, agq1, agg1]

    barrier = pltpu.get_barrier_semaphore()
    for dev in zdev + zfar + ydev:
        pl.semaphore_signal(
            barrier, inc=1, device_id={"seq": dev}, device_id_type=pl.DeviceIdType.MESH
        )

    def put_blocks(ref, own_ref, h):
        for j in range(2):
            ref[2 * z + j] = own_ref[j * BLOCK : (j + 1) * BLOCK, h * HD : (h + 1) * HD]

    line = lax.broadcasted_iota(I32, (8, BLOCK), 0)
    lane = lax.broadcasted_iota(I32, (8, BLOCK), 1)

    def put_rows():
        rows = jnp.zeros((8, BLOCK), I32)
        for j in range(2):
            hit = jnp.where(jnp.abs(lane - (2 * me + j)) <= 1, 1, 0)
            for r in range(remote_ref.shape[1]):
                used = jnp.where(count_ref[j] > r, 1, 0)
                hit = jnp.maximum(hit, jnp.where(lane == remote_ref[j, r], used, 0))
            rows = jnp.where(line == j, hit, rows)
        meta[z] = rows

    def put_stats():
        for h in range(2):
            cols = slice(h * HD, (h + 1) * HD)
            for j in range(2):
                rows = slice(j * BLOCK, (j + 1) * BLOCK)
                prod = g_ref[rows, cols].astype(F32) * o_ref[rows, cols].astype(F32)
                at = 4 * h + 2 * j
                ags[z, at : at + 1, :] = lse_ref[h : h + 1, rows] * LOG2E
                ags[z, at + 1 : at + 2, :] = jnp.sum(prod.T, axis=0, keepdims=True)

    def put_rest():
        for h in range(2):
            own[h][EMPTY] = jnp.zeros((HD, BLOCK), F32)
            for n in range(NY):
                dkacc[h, n] = jnp.zeros((2 * BLOCK, HD), F32)
                dvacc[h, n] = jnp.zeros((2 * BLOCK, HD), F32)
            kt_ref[h] = k_ref[:, h * HD : (h + 1) * HD].T

    put_blocks(agq[0], q_ref, 0)
    put_rows()
    pl.semaphore_wait(barrier, 6)

    def remote(src, dst, send, recv, dev):
        return pltpu.make_async_remote_copy(
            src_ref=src,
            dst_ref=dst,
            send_sem=send,
            recv_sem=recv,
            device_id={"seq": dev},
            device_id_type=pl.DeviceIdType.MESH,
        )

    def z_view(u, j, d, k, at):
        if u > 3:
            return (ags, meta)[u - 4].at[at]
        if j == 2 and k < half:
            return chain_refs[u].at[pl.ds(2 * at, 2)]
        return chain_refs[u].at[pl.ds(2 * at + (d if j == 2 else j), 1)]

    def z_copy(u, j, d, k, receiving=False):
        direct = u > 3 and k == mid + 1
        hop = k if receiving else 0 if direct else k - 1
        at = lax.rem(z + nz - hop, nz) if d == 0 else lax.rem(z + hop, nz)
        view = z_view(u, j, d, k, at)
        c = CHAINS.index((u, j))
        sems = z_send.at[c, d, k - 1], z_recv.at[c, d, k - 1]
        return remote(view, view, *sems, (zfar if direct else zdev)[d])

    def z_step(u, j, d, k):
        if k > 0:
            z_copy(u, j, d, k, receiving=True).wait_recv()
        end = last(u, j, d, half)
        if k < end and not (u > 3 and k == mid):
            z_copy(u, j, d, k + 1).start()
        if k == 0 and u > 3 and mid < end:
            z_copy(u, j, d, mid + 1).start()

    def z_drain(u):
        for c, j in CHAINS:
            if c == u:
                for d in range(2):
                    for k in range(1, last(u, j, d, half) + 1):
                        z_copy(u, j, d, k).wait_send()

    def build_tables():
        copy = pltpu.make_async_copy(meta, table, t_sem)
        copy.start()
        copy.wait()

        def bit(c, yy, b):
            return table[c // 2, c % 2, lax.rem(y + yy, NY) * cands + 2 * z + b]

        def scan(c, carry):
            count = []
            for yy in range(NY):
                live = bit(c, yy, 0) | bit(c, yy, 1)
                place = jnp.where(carry[yy] < CAPS[yy], FIRST[yy] + carry[yy], EMPTY)
                pos[yy, c] = jnp.where(live > 0, place, EMPTY)
                lists[yy, c] = live
                count.append(carry[yy] + live)
            return tuple(count)

        counts = lax.fori_loop(0, cands, scan, (jnp.int32(0),) * NY)
        most = counts[0] - CAPS[0]
        for yy in range(1, NY):
            most = jnp.maximum(most, counts[yy] - CAPS[yy])
        full[...] = jnp.broadcast_to(jnp.where(most > 0, 1.0, 0.0).astype(F32), (8, BLOCK))

        for yy in range(NY):
            nxt[yy, cands] = jnp.int32(cands)
            nxt[yy, cands + 1] = jnp.int32(cands)

        def back(i, carry):
            c = cands - 1 - i
            out = []
            for yy in range(NY):
                cur = jnp.where(lists[yy, c] > 0, c, carry[yy])
                nxt[yy, c] = cur
                out.append(cur)
            return tuple(out)

        lax.fori_loop(0, cands, back, (jnp.int32(cands),) * NY)

        for yy in range(NY):
            cur = nxt[yy, 0]
            for p in range(FIRST[yy], FIRST[yy] + CAPS[yy]):
                c = jnp.minimum(cur, cands - 1)
                live = jnp.where(cur < cands, 1, 0)
                idx[p] = c
                msk[0, p] = live * bit(c, yy, 0)
                msk[1, p] = live * bit(c, yy, 1)
                cur = nxt[yy, jnp.minimum(cur + 1, cands + 1)]

    def pairs(h, n, queries, grads, lse0, lse1, delta):
        cols = slice(h * HD, (h + 1) * HD)
        keys = nkv[n - 1, 0, :, cols] if n else k_ref[:, cols]
        values = nkv[n - 1, 1, :, cols] if n else v_ref[:, cols]
        scores = dot(keys, queries, 1, 1) * (scale * LOG2E)
        weights = jnp.concatenate(
            [jnp.exp2(scores[:BLOCK] - lse0), jnp.exp2(scores[BLOCK:] - lse1)], axis=0
        )
        dvacc[h, n] += dot(weights.astype(BF16), grads, 1, 0)
        grad_probs = dot(values, grads, 1, 1)
        grad_scores = (weights * (grad_probs - delta)).astype(BF16)
        dkacc[h, n] += dot(grad_scores, queries, 1, 0)
        return dot(nkt[n - 1, h] if n else kt_ref[h], grad_scores, 1, 0) * scale

    def stat_rows(h, c):
        tile = ags[c // 2]
        odd = c % 2 > 0
        lse = jnp.where(odd, tile[4 * h + 2 : 4 * h + 3], tile[4 * h : 4 * h + 1])
        delta = jnp.where(odd, tile[4 * h + 3 : 4 * h + 4], tile[4 * h + 1 : 4 * h + 2])
        return lse, delta

    def join(parts, axis):
        return jnp.concatenate(parts, axis=axis)

    def list_pairs(h, yy, i):
        lo = FIRST[yy] + sum(GROUPS[yy][:i])
        hi = lo + GROUPS[yy][i]
        qs, gs, l0, l1, dl = [], [], [], [], []
        for p in range(lo, hi):
            c = idx[p]
            lse, delta = stat_rows(h, c)
            qs.append(agq[h][c])
            gs.append(agg[h][c])
            l0.append(jnp.where(msk[0, p] > 0, lse, DEAD))
            l1.append(jnp.where(msk[1, p] > 0, lse, DEAD))
            dl.append(delta)
        n = (0, 1, 3, 2)[yy]
        got = pairs(h, n, join(qs, 0), join(gs, 0), join(l0, 1), join(l1, 1), join(dl, 1))
        for p in range(lo, hi):
            own[h][p] = got[:, (p - lo) * BLOCK : (p - lo + 1) * BLOCK]

    def k_copy(d, n):
        src = (k_ref, v_ref)[n]
        return remote(src, nkv.at[d, n], k_send.at[d, n], k_recv.at[d, n], ydev[1 - d])

    def keys_send(d):
        for n in range(2):
            k_copy(d, n).start()

    def k2_copy(d):
        src, dst = nkv.at[d, d], nkv.at[2, d]
        return remote(src, dst, k2_send.at[d], k2_recv.at[d], ydev[1 - d])

    def keys_wait(d):
        for n in range(2):
            k_copy(d, n).wait_recv()
        k2_copy(d).start()
        for h in range(2):
            nkt[d, h] = nkv[d, 0, :, h * HD : (h + 1) * HD].T

    def keys_end():
        for d in range(2):
            k2_copy(d).wait_recv()
        for h in range(2):
            nkt[2, h] = nkv[2, 0, :, h * HD : (h + 1) * HD].T

    def d1_copy(h, d):
        sems = d1_send.at[h, d], d1_recv.at[h, d]
        return remote(d1snd.at[h, d], d1rcv.at[h, d], *sems, ydev[d])

    def d_copy(h, d):
        return remote(dsnd.at[h, d], drcv.at[h, d], d_send.at[h, d], d_recv.at[h, d], ydev[d])

    def far_send(h):
        for d in range(2):
            d1snd[h, d, : 2 * BLOCK] = (dkacc, dvacc)[d][h, 3].astype(BF16)
            d1snd[h, d, 2 * BLOCK :] = jnp.broadcast_to(full[0:1], (16, HD)).astype(BF16)
            d1_copy(h, d).start()

    def near_send(h):
        seen = full[0:1]
        for d in range(2):
            d1_copy(h, d).wait_recv()
            seen = jnp.maximum(seen, d1rcv[h, d, 2 * BLOCK :].astype(F32)[0:1])
        for d in range(2):
            sums = [dkacc[h, 1 + d], dvacc[h, 1 + d]]
            sums[d] = sums[d] + d1rcv[h, d, : 2 * BLOCK].astype(F32)
            dsnd[h, d, 0 : 2 * BLOCK] = sums[0].astype(BF16)
            dsnd[h, d, 2 * BLOCK : 4 * BLOCK] = sums[1].astype(BF16)
            dsnd[h, d, 4 * BLOCK :] = jnp.broadcast_to(seen, (16, HD)).astype(BF16)
            d_copy(h, d).start()

    def terms(h, at, j):
        c = 2 * at + j
        total = own[h][pos[0, c]]
        for yy in range(1, NY):
            total = total + own[h][pos[yy, c]]
        return total

    def s_copy(h, d, j, k):
        at = pl.ds(0, BLOCK + 16 if h == 1 and j == d else BLOCK)
        return remote(
            rsnd.at[h, d, j, k - 1, at],
            rrcv.at[h, d, j, k - 1, at],
            s_send.at[h, d, j, k - 1],
            s_recv.at[h, d, j, k - 1],
            (zfar if h in CUT and k == mid else zdev)[1 - d],
        )

    extra = slice(BLOCK, BLOCK + 16)

    def s_step(h, d, j, k):
        dist = half + 1 - k
        at = lax.rem(z + nz - dist, nz) if d == 0 else lax.rem(z + dist, nz)
        total = terms(h, at, j)
        carries = h == 1 and j == d
        if carries:
            rsnd[h, d, j, k - 1, extra] = jnp.broadcast_to(full[0:1], (16, HD)).astype(BF16)
        cut = h in CUT
        if (k > 2 or (k == 2 and j == d)) and not (cut and k == mid + 1):
            s_copy(h, d, j, k - 1).wait_recv()
            total = total + rrcv[h, d, j, k - 2, :BLOCK].astype(F32)
            if carries:
                rsnd[h, d, j, k - 1, extra] = jnp.maximum(
                    rsnd[h, d, j, k - 1, extra], rrcv[h, d, j, k - 2, extra]
                )
        rsnd[h, d, j, k - 1, :BLOCK] = total.astype(BF16)
        s_copy(h, d, j, k).start()
        if k - 2 >= (mid + 1 if cut and k > mid else 1 if j == d else 2):
            s_copy(h, d, j, k - 2).wait_send()

    def s_end(h):
        cols = slice(h * HD, (h + 1) * HD)
        any_full = full[0:1]
        for j in range(2):
            total = terms(h, z, j)
            for d in range(2):
                for k in (mid, half) if h in CUT else (half,):
                    if k > 1 or j == d:
                        s_copy(h, d, j, k).wait_recv()
                        total = total + rrcv[h, d, j, k - 1, :BLOCK].astype(F32)
                        if h == 1 and j == d:
                            got = rrcv[h, d, j, k - 1, extra].astype(F32)
                            any_full = jnp.maximum(any_full, got[0:1])
                lo = 1 if j == d else 2
                for lo, hi in ((lo, mid), (mid + 1, half)) if h in CUT else ((lo, half),):
                    for k in range(max(lo, hi - 1), hi + 1):
                        s_copy(h, d, j, k).wait_send()
            dq_ref[j * BLOCK : (j + 1) * BLOCK, cols] = total.T.astype(BF16)
        if h == 1:
            over_ref[...] = jnp.broadcast_to(any_full, (8, BLOCK))

    def results(h):
        cols = slice(h * HD, (h + 1) * HD)
        grad_k, grad_v = dkacc[h, 0], dvacc[h, 0]
        seen = full[0:1]
        for d in range(2):
            d_copy(h, d).wait_recv()
            grad_k = grad_k + drcv[h, d, 0 : 2 * BLOCK].astype(F32)
            grad_v = grad_v + drcv[h, d, 2 * BLOCK : 4 * BLOCK].astype(F32)
            seen = jnp.maximum(seen, drcv[h, d, 4 * BLOCK :].astype(F32)[0:1])
        dk_ref[:, cols] = (grad_k * scale).astype(BF16)
        dv_ref[:, cols] = grad_v.astype(BF16)
        if h == 0:
            full[...] = jnp.broadcast_to(seen, (8, BLOCK))

    def y_drain(h):
        k2_copy(h).wait_send()
        for d in range(2):
            k_copy(d, h).wait_send()
            d1_copy(h, d).wait_send()
            d_copy(h, d).wait_send()

    do = {
        "z": z_step,
        "tab": build_tables,
        "own": list_pairs,
        "ks": keys_send,
        "kw": keys_wait,
        "kx": keys_end,
        "d1": far_send,
        "d2": near_send,
        "kv": results,
        "zq": z_drain,
        "yq": y_drain,
        "s": s_step,
        "e": s_end,
    }
    steps = plan(half)
    ahead = [("z", *c, d, 0) for c in CHAINS if c[0] == 0 for d in range(2)]
    ahead += [("z", 5, 2, d, 0) for d in range(2)] + [("ks", 0), ("ks", 1)]
    for step in ahead:
        do[step[0]](*step[1:])
    for u in range(1, 4):
        put_blocks(chain_refs[u], (q_ref, g_ref)[u % 2], u // 2)
    put_stats()
    put_rest()
    for step in steps:
        if step not in ahead:
            do[step[0]](*step[1:])


def fast(nz, remote, count, query, key, value, output, grad_out, logsumexp):
    rows, width = query.shape
    half = nz // 2
    blocks = (2 * nz, BLOCK, HD)
    vmem, dma = pltpu.VMEM, pltpu.SemaphoreType.DMA
    smem = pltpu.SMEM
    outs = [jax.ShapeDtypeStruct((rows, width), BF16)] * 3
    outs.append(jax.ShapeDtypeStruct((8, BLOCK), F32))
    in_vmem = pl.BlockSpec(memory_space=pltpu.VMEM)
    scratch = [
        *[vmem(blocks, BF16)] * 4,
        vmem((nz, 8, BLOCK), F32),
        vmem((nz, 8, BLOCK), I32),
        vmem((8, BLOCK), F32),
        vmem((3, 2, rows, width), BF16),
        vmem((3, 2, HD, 2 * BLOCK), BF16),
        vmem((2, 2, 2 * BLOCK + 16, HD), BF16),
        vmem((2, 2, 2 * BLOCK + 16, HD), BF16),
        vmem((2, 2, 4 * BLOCK + 16, HD), BF16),
        vmem((2, 2, 4 * BLOCK + 16, HD), BF16),
        *[vmem((EMPTY + 1, HD, BLOCK), F32)] * 2,
        vmem((2, 2, 2, half, BLOCK + 16, HD), BF16),
        vmem((2, 2, 2, half, BLOCK + 16, HD), BF16),
        vmem((2, NY, 2 * BLOCK, HD), F32),
        vmem((2, NY, 2 * BLOCK, HD), F32),
        vmem((2, HD, 2 * BLOCK), BF16),
        smem((nz, 8, BLOCK), I32),
        smem((NY, 2 * nz), I32),
        smem((NY, 2 * nz + 2), I32),
        smem((NY, 2 * nz), I32),
        smem((EMPTY,), I32),
        smem((2, EMPTY), I32),
        pltpu.SemaphoreType.DMA,
        *[dma((len(CHAINS), 2, half))] * 2,
        *[dma((2, 2))] * 2,
        *[dma((2,))] * 2,
        *[dma((2, 2))] * 2,
        *[dma((2, 2))] * 2,
        *[dma((2, 2, 2, half))] * 2,
    ]
    return pl.pallas_call(
        functools.partial(kernel, nz),
        out_shape=outs,
        in_specs=[pl.BlockSpec(memory_space=pltpu.SMEM)] * 2 + [in_vmem] * 6,
        out_specs=[in_vmem] * 4,
        scratch_shapes=scratch,
        compiler_params=pltpu.CompilerParams(
            collective_id=0, has_side_effects=True, vmem_limit_bytes=48 * 1024 * 1024
        ),
        cost_estimate=pl.CostEstimate(
            flops=4 * 10**9, bytes_accessed=4 * 2**20, transcendentals=5 * 10**6
        ),
    )(remote, count, query, key, value, output, grad_out, logsumexp)


def per_device(query, key, value, output, grad_out, logsumexp, remote_blocks, remote_count):
    nz = lax.axis_size("seq") // NY
    *found, over = fast(
        nz, remote_blocks, remote_count, query, key, value, output, grad_out, logsumexp
    )
    return lax.cond(
        over[0, 0] > 0,
        lambda: general(
            query, key, value, output, grad_out, logsumexp, remote_blocks, remote_count
        ),
        lambda: tuple(found),
    )


def solution(mesh):
    return jax.shard_map(
        per_device,
        mesh=mesh,
        in_specs=(
            P("seq", "head"),
            P("seq", "head"),
            P("seq", "head"),
            P("seq", "head"),
            P("seq", "head"),
            P("head", "seq"),
            P("seq", None),
            P("seq"),
        ),
        out_specs=(P("seq", "head"), P("seq", "head"), P("seq", "head")),
        check_vma=False,
    )
```

```python
import functools

import jax
import jax.numpy as jnp
from jax import lax
from jax.experimental import pallas as pl
from jax.experimental.pallas import tpu as pltpu
from jax.sharding import PartitionSpec as P

HD = 128
BLOCK = 128
NY = 4
GROUPS = ((6, 6), (10,), (10,), (10,))
CAPS = tuple(sum(sizes) for sizes in GROUPS)
FIRST = tuple(sum(CAPS[:yy]) for yy in range(NY))
EMPTY = sum(CAPS)
DEAD = 1e30
LOG2E = 1.4426950408889634
F32 = jnp.float32
BF16 = jnp.bfloat16
I32 = jnp.int32


def with_halo(cells, sides, width):
    for axis, dim in sides:
        count = lax.axis_size(axis)
        ends = count - 1
        head = lax.slice_in_dim(cells, 0, width, axis=dim)
        tail = lax.slice_in_dim(cells, cells.shape[dim] - width, cells.shape[dim], axis=dim)
        cells = jnp.concatenate(
            [
                lax.ppermute(tail, axis, [(i, (i + 1) % count) for i in range(ends)]),
                cells,
                lax.ppermute(head, axis, [((i + 1) % count, i) for i in range(ends)]),
            ],
            axis=dim,
        )
    return cells


def block_pairs(queries, grads, stats, keys, values, valid, scale):
    scores = (
        jnp.einsum("pxhd,pyhd->phxy", queries, keys, preferred_element_type=jnp.float32) * scale
    )
    weights = jnp.exp(scores - stats[0][..., None]) * valid[:, None, None, None]
    probs = weights.astype(jnp.bfloat16)
    grad_values = jnp.einsum("phxy,pxhd->pyhd", probs, grads, preferred_element_type=jnp.float32)
    grad_probs = jnp.einsum("pxhd,pyhd->phxy", grads, values, preferred_element_type=jnp.float32)
    grad_scores = (weights * (grad_probs - stats[1][..., None])).astype(jnp.bfloat16)
    grad_queries = (
        jnp.einsum("phxy,pyhd->pxhd", grad_scores, keys, preferred_element_type=jnp.float32) * scale
    )
    grad_keys = (
        jnp.einsum("phxy,pxhd->pyhd", grad_scores, queries, preferred_element_type=jnp.float32)
        * scale
    )
    return (grad_queries, grad_keys, grad_values)


def spread_terms(terms):
    padded = jnp.pad(terms[0], ((0, 2), (0, 0), (0, 0), (0, 0)))
    padded = padded + jnp.pad(terms[1], ((1, 1), (0, 0), (0, 0), (0, 0)))
    return padded + jnp.pad(terms[2], ((2, 0), (0, 0), (0, 0), (0, 0)))


def remote_pairs(
    part_query, part_grad, part_stats, key_table, value_table, key_index, live_in, scale
):
    senders = part_query.shape[0]
    head_count = part_query.shape[2]
    groups = senders // 8

    def remote_group(items):
        one_q, one_g, one_s, one_k, one_l = items
        return block_pairs(
            one_q,
            one_g,
            one_s.transpose(1, 0, 2, 3),
            key_table[one_k],
            value_table[one_k],
            one_l,
            scale,
        )

    group_shape = (groups, 8, BLOCK, head_count, HD)
    found_q, found_k, found_v = lax.map(
        remote_group,
        (
            part_query.reshape(group_shape),
            part_grad.reshape(group_shape),
            part_stats.reshape(groups, 8, 2, head_count, BLOCK),
            key_index.reshape(groups, 8),
            live_in.reshape(groups, 8),
        ),
    )
    out_shape = (senders, BLOCK, head_count, HD)
    return (found_q.reshape(out_shape), found_k.reshape(out_shape), found_v.reshape(out_shape))


def general(query, key, value, output, grad_out, logsumexp, remote_blocks, remote_count):
    seq_size = lax.axis_size("seq")
    place = lax.axis_index("seq")
    rows, width = query.shape
    count_blocks = rows // BLOCK
    heads_here = width // HD
    scale = float(HD) ** (-0.5)
    shape_four = (count_blocks, BLOCK, heads_here, HD)
    q_tiles = query.reshape(shape_four)
    g_tiles = grad_out.reshape(shape_four)
    k_tiles = key.reshape(shape_four)
    v_tiles = value.reshape(shape_four)
    delta = jnp.sum(
        grad_out.astype(jnp.float32).reshape(shape_four)
        * output.astype(jnp.float32).reshape(shape_four),
        axis=3,
    )
    stats = jnp.stack(
        [
            logsumexp.reshape(heads_here, count_blocks, BLOCK).transpose(1, 0, 2),
            delta.transpose(0, 2, 1),
        ]
    )
    slots_used = (
        jnp.arange(remote_blocks.shape[1], dtype=jnp.int32)[None, :] < remote_count[:, None]
    )
    owners = remote_blocks // count_blocks
    local_key = remote_blocks % count_blocks
    match = (
        (owners[:, :, None] == jnp.arange(seq_size, dtype=jnp.int32)[None, None, :])
        & slots_used[:, :, None]
    ).astype(jnp.int32)
    live = jnp.sum(match, axis=(0, 1))
    send_query = jnp.sum(
        match * jnp.arange(count_blocks, dtype=jnp.int32)[:, None, None], axis=(0, 1)
    )
    send_key = jnp.sum(match * local_key[:, :, None], axis=(0, 1))
    meta = jnp.stack([send_key, live], axis=1).astype(jnp.float32)
    got_stats, got_meta = (
        lax.all_to_all(
            stats[:, send_query].transpose(1, 0, 2, 3),
            "seq",
            split_axis=0,
            concat_axis=0,
            tiled=True,
        ),
        lax.all_to_all(meta, "seq", split_axis=0, concat_axis=0, tiled=True),
    )
    key_index = got_meta[:, 0].astype(jnp.int32)
    live_in = got_meta[:, 1]
    got_query, got_grad = (
        lax.all_to_all(q_tiles[send_query], "seq", split_axis=0, concat_axis=0, tiled=True),
        lax.all_to_all(g_tiles[send_query], "seq", split_axis=0, concat_axis=0, tiled=True),
    )
    remote_q, remote_k, remote_v = remote_pairs(
        got_query, got_grad, got_stats, k_tiles, v_tiles, key_index, live_in, scale
    )
    returned = lax.all_to_all(
        remote_q.astype(jnp.bfloat16), "seq", split_axis=0, concat_axis=0, tiled=True
    )
    empty = jnp.zeros((count_blocks, BLOCK, width), jnp.float32)
    grad_key = empty.at[key_index].add(remote_k.reshape(seq_size, BLOCK, width))
    grad_value = empty.at[key_index].add(remote_v.reshape(seq_size, BLOCK, width))
    grad_query = empty.at[send_query].add(
        returned.reshape(seq_size, BLOCK, width).astype(jnp.float32)
    )
    offsets = jnp.arange(3, dtype=jnp.int32)[:, None]
    band_index = (
        place * count_blocks + jnp.arange(count_blocks, dtype=jnp.int32)[None, :] + offsets - 1
    )
    band_ok = (
        ((band_index >= 0) & (band_index < count_blocks * seq_size)).astype(jnp.float32).reshape(-1)
    )
    rimmed = with_halo(jnp.stack([key, value]), (("seq", 1),), BLOCK)
    wide = rimmed.reshape(2, count_blocks + 2, BLOCK, heads_here, HD)
    band_keys = jnp.concatenate([wide[0, j : j + count_blocks] for j in range(3)])
    band_values = jnp.concatenate([wide[1, j : j + count_blocks] for j in range(3)])
    band_q, band_k, band_v = block_pairs(
        jnp.concatenate([q_tiles] * 3),
        jnp.concatenate([g_tiles] * 3),
        jnp.concatenate([stats] * 3, axis=1),
        band_keys,
        band_values,
        band_ok,
        scale,
    )
    grad_query = grad_query + jnp.sum(band_q.reshape(3, count_blocks, BLOCK, width), axis=0)
    spread_k = spread_terms(band_k.reshape(3, count_blocks, BLOCK, heads_here, HD))
    spread_v = spread_terms(band_v.reshape(3, count_blocks, BLOCK, heads_here, HD))
    both = jnp.stack([spread_k, spread_v]).reshape(2, count_blocks + 2, BLOCK, width)
    edges = jnp.stack([both[:, 0], both[:, count_blocks + 1]])
    arrived = with_halo(edges, (("seq", 0),), 1)
    own = both[:, 1 : count_blocks + 1]
    own = own.at[:, 0].add(arrived[0]).at[:, count_blocks - 1].add(arrived[3])
    grad_key = grad_key + own[0]
    grad_value = grad_value + own[1]
    return (
        grad_query.reshape(rows, width).astype(jnp.bfloat16),
        grad_key.reshape(rows, width).astype(jnp.bfloat16),
        grad_value.reshape(rows, width).astype(jnp.bfloat16),
    )


def dot(a, b, ca, cb):
    return lax.dot_general(a, b, (((ca,), (cb,)), ((), ())), preferred_element_type=F32)


CUT = ()
FINE = (0, 1)
CHAINS = [(u, j) for u in range(6) for j in ((0, 1) if u in FINE else (2,))]


def last(u, j, d, half):
    if j < 2:
        return half if j == d else half - 1
    return half if u < 4 or d == 0 else half - 1


def plan(half, release=(0, 1, 0), lat=1.8, chunk=0.2, tab=3.0, bw=47.0, hop=0.3, iss=0.1):
    mid = half // 2
    steps = {}

    for u, j in CHAINS:
        cut = u > 3
        for d in range(2):
            for k in range(last(u, j, d, half) + 1):
                def size(n):
                    return 4 if u > 3 else 64 if n < half and j == 2 else 32
                sends = []
                if k < last(u, j, d, half) and not (cut and k == mid):
                    sends.append((("z", u, j, d, k + 1), d, size(k + 1), 1))
                if k == 0 and cut and mid < last(u, j, d, half):
                    sends.append((("z", u, j, d, mid + 1), d, size(mid + 1), mid + 1))
                needs = [("z", u, j, d, k - 1)] if k else []
                if k == 0 and u not in (0, 5):
                    needs = [("put", u)]
                if k == 0 and 0 < u < 4:
                    pj = 0 if u - 1 in FINE else 2
                    needs += [("z", u - 1, pj, d, min(release[u - 1], half - 1))]
                awaits = [("z", u, j, d, k)] if k else []
                steps["z", u, j, d, k] = (needs, awaits, sends, 0.0)

    def all_in(u):
        return [("z", c, j, d, last(c, j, d, half)) for c, j in CHAINS if c == u for d in range(2)]

    for d in range(2):
        steps["ks", d] = ([("z", *CHAINS[0], 1, 0)], [], [(("k", d), 3 - d, 256, 1)], 0.1)
        steps["kw", d] = ([], [("k", d)], [(("k2", d), 3 - d, 128, 1)], 0.4)
    steps["kx",] = ([("kw", 0), ("kw", 1)], [("k2", 0), ("k2", 1)], [], 0.4)
    for u, cost in ((1, 0.2), (2, 0.2), (3, 0.2), (4, 1.2), (6, 1.5)):
        steps["put", u] = ([], [], [], cost)
    steps["tc",] = (all_in(5), [], [(("tc",), 4, 1, 1)], 0.1)
    steps["tab",] = ([("tc",)], [("tc",)], [], tab)
    stats_in = all_in(4)
    for u in (4, 5):
        steps["zq", u] = ([("tab",)] + all_in(u), [], [], 0.1)
    for h in range(2):
        got = [all_in(2 * h + t) for t in range(2)]
        pairs = []
        for yy in (2, 1, 3, 0):
            keys = {0: [], 1: [("kw", 0)], 2: [("kx",)], 3: [("kw", 1)]}[yy]
            for i, size in enumerate(GROUPS[yy]):
                needs = [("tab",), ("put", 6)] + stats_in + got[0] + got[1] + keys
                steps["own", h, yy, i] = (needs, [], [], size / 2 * chunk)
                pairs.append(("own", h, yy, i))
        far = [p for p in pairs if p[2] == 2]
        steps["d1", h] = (far, [], [(("d1", h, d), 2 + d, 68, 1) for d in range(2)], 0.2)
        sends = [(("d2", h, d), 2 + d, 132, 1) for d in range(2)]
        steps["d2", h] = (pairs + [("d1", h)], [("d1", h, d) for d in range(2)], sends, 0.3)
        steps["kv", h] = ([("d2", h)], [("d2", h, d) for d in range(2)], [], 0.3)
        fin = []
        for d in range(2):
            for j in range(2):
                for k in range(1, half + 1):
                    if k > 1 or j == d:
                        cut = h in CUT
                        first = k == 1 or (k == 2 and j != d) or (cut and k == mid + 1)
                        awaits = [] if first else [("s", h, d, j, k - 1)]
                        hops = mid + 1 if cut and k == mid else 1
                        if k == half or (cut and k == mid):
                            fin.append(("s", h, d, j, k))
                        steps["s", h, d, j, k] = (pairs + [("kv", 0)] * h, awaits, [(("s", h, d, j, k), 1 - d, 32, hops)], 0.08)
        for t in range(2):
            steps["zq", 2 * h + t] = (got[t] + pairs, [], [], 0.1)
        steps["yq", h] = ([("kv", h)], [], [], 0.1)
        steps["e", h] = (pairs, fin, [], 0.3)
    for s in list(steps):
        n, a, sd, c = steps[s]
        steps[s] = (n, a, sd, c + iss * (len(a) + len(sd)))
    sender = {m: (s, kib, hops) for s, (_, _, sends, _) in steps.items() for m, _, kib, hops in sends}
    after = {s: [] for s in steps}
    for s, (needs, awaits, _, _) in steps.items():
        for n in needs:
            after[n].append((s, 0.0))
        for m in awaits:
            f, kib, hops = sender[m]
            after[f].append((s, hops * kib / bw + lat + hop * (hops - 1)))
    way = {}

    def length(s):
        if s not in way:
            way[s] = steps[s][3] + max([gap + length(n) for n, gap in after[s]], default=0.0)
        return way[s]

    left = sorted(steps, key=lambda s: (-length(s), str(s)))
    now, free, arrival, done, order = 0.0, [0.0] * 5, {}, set(), []
    while left:
        ready = [
            (max([now] + [arrival[m] for m in steps[s][1]]), i)
            for i, s in enumerate(left)
            if all(n in done for n in steps[s][0]) and all(m in arrival for m in steps[s][1])
        ]
        now, i = min(ready)
        s = left.pop(i)
        now += steps[s][3]
        for m, link, kib, hops in steps[s][2]:
            begin = max(free[link], now)
            free[link] = begin + hops * kib / bw
            arrival[m] = begin + min(hops, 2) * kib / bw + lat + hop * (hops - 1)
        done.add(s)
        order.append(s)
    return order


def kernel(
    nz,
    remote_ref,
    count_ref,
    q_ref,
    k_ref,
    v_ref,
    o_ref,
    g_ref,
    lse_ref,
    dq_ref,
    dk_ref,
    dv_ref,
    over_ref,
    agq0,
    agq1,
    agg0,
    agg1,
    ags,
    meta,
    full,
    nkv,
    nkt,
    d1snd,
    d1rcv,
    dsnd,
    drcv,
    own0,
    own1,
    rsnd,
    rrcv,
    dkacc,
    dvacc,
    kt_ref,
    table,
    lists,
    nxt,
    pos,
    idx,
    msk,
    t_sem,
    z_send,
    z_recv,
    k_send,
    k_recv,
    k2_send,
    k2_recv,
    d1_send,
    d1_recv,
    d_send,
    d_recv,
    s_send,
    s_recv,
):
    me = lax.axis_index("seq")
    y = me // nz
    z = me % nz
    half = nz // 2
    cands = 2 * nz
    scale = float(HD) ** -0.5
    zdev = [y * nz + lax.rem(z + 1, nz), y * nz + lax.rem(z + nz - 1, nz)]
    ydev = [lax.rem(y + 1, NY) * nz + z, lax.rem(y + NY - 1, NY) * nz + z]
    mid = half // 2
    zfar = [y * nz + lax.rem(z + mid + 1, nz), y * nz + lax.rem(z + nz - mid - 1, nz)]
    agq = [agq0, agq1]
    agg = [agg0, agg1]
    own = [own0, own1]
    chain_refs = [agq0, agg0, agq1, agg1]

    barrier = pltpu.get_barrier_semaphore()
    for dev in zdev + zfar + ydev:
        pl.semaphore_signal(
            barrier, inc=1, device_id={"seq": dev}, device_id_type=pl.DeviceIdType.MESH
        )

    def put_blocks(ref, own_ref, h):
        for j in range(2):
            ref[2 * z + j] = own_ref[j * BLOCK : (j + 1) * BLOCK, h * HD : (h + 1) * HD]

    line = lax.broadcasted_iota(I32, (8, BLOCK), 0)
    lane = lax.broadcasted_iota(I32, (8, BLOCK), 1)

    def put_rows():
        rows = jnp.zeros((8, BLOCK), I32)
        for j in range(2):
            hit = jnp.where(jnp.abs(lane - (2 * me + j)) <= 1, 1, 0)
            for r in range(remote_ref.shape[1]):
                used = jnp.where(count_ref[j] > r, 1, 0)
                hit = jnp.maximum(hit, jnp.where(lane == remote_ref[j, r], used, 0))
            rows = jnp.where(line == j, hit, rows)
        meta[z] = rows

    def put_stats():
        for h in range(2):
            cols = slice(h * HD, (h + 1) * HD)
            for j in range(2):
                rows = slice(j * BLOCK, (j + 1) * BLOCK)
                prod = g_ref[rows, cols].astype(F32) * o_ref[rows, cols].astype(F32)
                at = 4 * h + 2 * j
                ags[z, at : at + 1, :] = lse_ref[h : h + 1, rows] * LOG2E
                ags[z, at + 1 : at + 2, :] = jnp.sum(prod.T, axis=0, keepdims=True)

    def put_rest():
        for h in range(2):
            own[h][EMPTY] = jnp.zeros((HD, BLOCK), F32)
            for n in range(NY):
                dkacc[h, n] = jnp.zeros((2 * BLOCK, HD), F32)
                dvacc[h, n] = jnp.zeros((2 * BLOCK, HD), F32)
            kt_ref[h] = k_ref[:, h * HD : (h + 1) * HD].T

    put_blocks(agq[0], q_ref, 0)
    put_rows()
    pl.semaphore_wait(barrier, 6)

    def remote(src, dst, send, recv, dev):
        return pltpu.make_async_remote_copy(
            src_ref=src,
            dst_ref=dst,
            send_sem=send,
            recv_sem=recv,
            device_id={"seq": dev},
            device_id_type=pl.DeviceIdType.MESH,
        )

    def z_view(u, j, d, k, at):
        if u > 3:
            return (ags, meta)[u - 4].at[at]
        if j == 2 and k < half:
            return chain_refs[u].at[pl.ds(2 * at, 2)]
        return chain_refs[u].at[pl.ds(2 * at + (d if j == 2 else j), 1)]

    def z_copy(u, j, d, k, receiving=False):
        direct = u > 3 and k == mid + 1
        hop = k if receiving else 0 if direct else k - 1
        at = lax.rem(z + nz - hop, nz) if d == 0 else lax.rem(z + hop, nz)
        view = z_view(u, j, d, k, at)
        c = CHAINS.index((u, j))
        sems = z_send.at[c, d, k - 1], z_recv.at[c, d, k - 1]
        return remote(view, view, *sems, (zfar if direct else zdev)[d])

    def z_step(u, j, d, k):
        if k > 0:
            z_copy(u, j, d, k, receiving=True).wait_recv()
        end = last(u, j, d, half)
        if k < end and not (u > 3 and k == mid):
            z_copy(u, j, d, k + 1).start()
        if k == 0 and u > 3 and mid < end:
            z_copy(u, j, d, mid + 1).start()

    def z_drain(u):
        for c, j in CHAINS:
            if c == u:
                for d in range(2):
                    for k in range(1, last(u, j, d, half) + 1):
                        z_copy(u, j, d, k).wait_send()

    def table_copy():
        return pltpu.make_async_copy(meta, table, t_sem)

    def table_start():
        table_copy().start()

    def build_tables():
        table_copy().wait()

        def bit(c, yy, b):
            return table[c // 2, c % 2, lax.rem(y + yy, NY) * cands + 2 * z + b]

        def scan(c, carry):
            count = []
            for yy in range(NY):
                live = bit(c, yy, 0) | bit(c, yy, 1)
                place = jnp.where(carry[yy] < CAPS[yy], FIRST[yy] + carry[yy], EMPTY)
                pos[yy, c] = jnp.where(live > 0, place, EMPTY)
                lists[yy, c] = live
                count.append(carry[yy] + live)
            return tuple(count)

        counts = lax.fori_loop(0, cands, scan, (jnp.int32(0),) * NY)
        most = counts[0] - CAPS[0]
        for yy in range(1, NY):
            most = jnp.maximum(most, counts[yy] - CAPS[yy])
        full[...] = jnp.broadcast_to(jnp.where(most > 0, 1.0, 0.0).astype(F32), (8, BLOCK))

        for yy in range(NY):
            nxt[yy, cands] = jnp.int32(cands)
            nxt[yy, cands + 1] = jnp.int32(cands)

        def back(i, carry):
            c = cands - 1 - i
            out = []
            for yy in range(NY):
                cur = jnp.where(lists[yy, c] > 0, c, carry[yy])
                nxt[yy, c] = cur
                out.append(cur)
            return tuple(out)

        lax.fori_loop(0, cands, back, (jnp.int32(cands),) * NY)

        for yy in range(NY):
            cur = nxt[yy, 0]
            for p in range(FIRST[yy], FIRST[yy] + CAPS[yy]):
                c = jnp.minimum(cur, cands - 1)
                live = jnp.where(cur < cands, 1, 0)
                idx[p] = c
                msk[0, p] = live * bit(c, yy, 0)
                msk[1, p] = live * bit(c, yy, 1)
                cur = nxt[yy, jnp.minimum(cur + 1, cands + 1)]

    def pairs(h, n, queries, grads, lse0, lse1, delta):
        cols = slice(h * HD, (h + 1) * HD)
        keys = nkv[n - 1, 0, :, cols] if n else k_ref[:, cols]
        values = nkv[n - 1, 1, :, cols] if n else v_ref[:, cols]
        scores = dot(keys, queries, 1, 1) * (scale * LOG2E)
        weights = jnp.concatenate(
            [jnp.exp2(scores[:BLOCK] - lse0), jnp.exp2(scores[BLOCK:] - lse1)], axis=0
        )
        dvacc[h, n] += dot(weights.astype(BF16), grads, 1, 0)
        grad_probs = dot(values, grads, 1, 1)
        grad_scores = (weights * (grad_probs - delta)).astype(BF16)
        dkacc[h, n] += dot(grad_scores, queries, 1, 0)
        return dot(nkt[n - 1, h] if n else kt_ref[h], grad_scores, 1, 0) * scale

    def stat_rows(h, c):
        tile = ags[c // 2]
        odd = c % 2 > 0
        lse = jnp.where(odd, tile[4 * h + 2 : 4 * h + 3], tile[4 * h : 4 * h + 1])
        delta = jnp.where(odd, tile[4 * h + 3 : 4 * h + 4], tile[4 * h + 1 : 4 * h + 2])
        return lse, delta

    def join(parts, axis):
        return jnp.concatenate(parts, axis=axis)

    def list_pairs(h, yy, i):
        lo = FIRST[yy] + sum(GROUPS[yy][:i])
        hi = lo + GROUPS[yy][i]
        qs, gs, l0, l1, dl = [], [], [], [], []
        for p in range(lo, hi):
            c = idx[p]
            lse, delta = stat_rows(h, c)
            qs.append(agq[h][c])
            gs.append(agg[h][c])
            l0.append(jnp.where(msk[0, p] > 0, lse, DEAD))
            l1.append(jnp.where(msk[1, p] > 0, lse, DEAD))
            dl.append(delta)
        n = (0, 1, 3, 2)[yy]
        got = pairs(h, n, join(qs, 0), join(gs, 0), join(l0, 1), join(l1, 1), join(dl, 1))
        for p in range(lo, hi):
            own[h][p] = got[:, (p - lo) * BLOCK : (p - lo + 1) * BLOCK]

    def k_copy(d, n):
        src = (k_ref, v_ref)[n]
        return remote(src, nkv.at[d, n], k_send.at[d, n], k_recv.at[d, n], ydev[1 - d])

    def keys_send(d):
        for n in range(2):
            k_copy(d, n).start()

    def k2_copy(d):
        src, dst = nkv.at[d, d], nkv.at[2, d]
        return remote(src, dst, k2_send.at[d], k2_recv.at[d], ydev[1 - d])

    def keys_wait(d):
        for n in range(2):
            k_copy(d, n).wait_recv()
        k2_copy(d).start()
        for h in range(2):
            nkt[d, h] = nkv[d, 0, :, h * HD : (h + 1) * HD].T

    def keys_end():
        for d in range(2):
            k2_copy(d).wait_recv()
        for h in range(2):
            nkt[2, h] = nkv[2, 0, :, h * HD : (h + 1) * HD].T

    def d1_copy(h, d):
        sems = d1_send.at[h, d], d1_recv.at[h, d]
        return remote(d1snd.at[h, d], d1rcv.at[h, d], *sems, ydev[d])

    def d_copy(h, d):
        return remote(dsnd.at[h, d], drcv.at[h, d], d_send.at[h, d], d_recv.at[h, d], ydev[d])

    def far_send(h):
        for d in range(2):
            d1snd[h, d, : 2 * BLOCK] = (dkacc, dvacc)[d][h, 3].astype(BF16)
            d1snd[h, d, 2 * BLOCK :] = jnp.broadcast_to(full[0:1], (16, HD)).astype(BF16)
            d1_copy(h, d).start()

    def near_send(h):
        seen = full[0:1]
        for d in range(2):
            d1_copy(h, d).wait_recv()
            seen = jnp.maximum(seen, d1rcv[h, d, 2 * BLOCK :].astype(F32)[0:1])
        for d in range(2):
            sums = [dkacc[h, 1 + d], dvacc[h, 1 + d]]
            sums[d] = sums[d] + d1rcv[h, d, : 2 * BLOCK].astype(F32)
            dsnd[h, d, 0 : 2 * BLOCK] = sums[0].astype(BF16)
            dsnd[h, d, 2 * BLOCK : 4 * BLOCK] = sums[1].astype(BF16)
            dsnd[h, d, 4 * BLOCK :] = jnp.broadcast_to(seen, (16, HD)).astype(BF16)
            d_copy(h, d).start()

    def terms(h, at, j):
        c = 2 * at + j
        total = own[h][pos[0, c]]
        for yy in range(1, NY):
            total = total + own[h][pos[yy, c]]
        return total

    def s_copy(h, d, j, k):
        at = pl.ds(0, BLOCK + 16 if h == 1 and j == d else BLOCK)
        return remote(
            rsnd.at[h, d, j, k - 1, at],
            rrcv.at[h, d, j, k - 1, at],
            s_send.at[h, d, j, k - 1],
            s_recv.at[h, d, j, k - 1],
            (zfar if h in CUT and k == mid else zdev)[1 - d],
        )

    extra = slice(BLOCK, BLOCK + 16)

    def s_step(h, d, j, k):
        dist = half + 1 - k
        at = lax.rem(z + nz - dist, nz) if d == 0 else lax.rem(z + dist, nz)
        total = terms(h, at, j)
        carries = h == 1 and j == d
        if carries:
            rsnd[h, d, j, k - 1, extra] = jnp.broadcast_to(full[0:1], (16, HD)).astype(BF16)
        cut = h in CUT
        if (k > 2 or (k == 2 and j == d)) and not (cut and k == mid + 1):
            s_copy(h, d, j, k - 1).wait_recv()
            total = total + rrcv[h, d, j, k - 2, :BLOCK].astype(F32)
            if carries:
                rsnd[h, d, j, k - 1, extra] = jnp.maximum(
                    rsnd[h, d, j, k - 1, extra], rrcv[h, d, j, k - 2, extra]
                )
        rsnd[h, d, j, k - 1, :BLOCK] = total.astype(BF16)
        s_copy(h, d, j, k).start()
        if k - 2 >= (mid + 1 if cut and k > mid else 1 if j == d else 2):
            s_copy(h, d, j, k - 2).wait_send()

    def s_end(h):
        cols = slice(h * HD, (h + 1) * HD)
        any_full = full[0:1]
        for j in range(2):
            total = terms(h, z, j)
            for d in range(2):
                for k in (mid, half) if h in CUT else (half,):
                    if k > 1 or j == d:
                        s_copy(h, d, j, k).wait_recv()
                        total = total + rrcv[h, d, j, k - 1, :BLOCK].astype(F32)
                        if h == 1 and j == d:
                            got = rrcv[h, d, j, k - 1, extra].astype(F32)
                            any_full = jnp.maximum(any_full, got[0:1])
                lo = 1 if j == d else 2
                for lo, hi in ((lo, mid), (mid + 1, half)) if h in CUT else ((lo, half),):
                    for k in range(max(lo, hi - 1), hi + 1):
                        s_copy(h, d, j, k).wait_send()
            dq_ref[j * BLOCK : (j + 1) * BLOCK, cols] = total.T.astype(BF16)
        if h == 1:
            over_ref[...] = jnp.broadcast_to(any_full, (8, BLOCK))

    def results(h):
        cols = slice(h * HD, (h + 1) * HD)
        grad_k, grad_v = dkacc[h, 0], dvacc[h, 0]
        seen = full[0:1]
        for d in range(2):
            d_copy(h, d).wait_recv()
            grad_k = grad_k + drcv[h, d, 0 : 2 * BLOCK].astype(F32)
            grad_v = grad_v + drcv[h, d, 2 * BLOCK : 4 * BLOCK].astype(F32)
            seen = jnp.maximum(seen, drcv[h, d, 4 * BLOCK :].astype(F32)[0:1])
        dk_ref[:, cols] = (grad_k * scale).astype(BF16)
        dv_ref[:, cols] = grad_v.astype(BF16)
        if h == 0:
            full[...] = jnp.broadcast_to(seen, (8, BLOCK))

    def y_drain(h):
        k2_copy(h).wait_send()
        for d in range(2):
            k_copy(d, h).wait_send()
            d1_copy(h, d).wait_send()
            d_copy(h, d).wait_send()

    def put(u):
        if u == 4:
            put_stats()
        elif u == 6:
            put_rest()
        else:
            put_blocks(chain_refs[u], (q_ref, g_ref)[u % 2], u // 2)

    do = {
        "z": z_step,
        "put": put,
        "tc": table_start,
        "tab": build_tables,
        "own": list_pairs,
        "ks": keys_send,
        "kw": keys_wait,
        "kx": keys_end,
        "d1": far_send,
        "d2": near_send,
        "kv": results,
        "zq": z_drain,
        "yq": y_drain,
        "s": s_step,
        "e": s_end,
    }
    steps = plan(half)
    ahead = [("z", *c, d, 0) for c in CHAINS if c[0] == 0 for d in range(2)]
    ahead += [("z", 5, 2, d, 0) for d in range(2)] + [("ks", 0), ("ks", 1)]
    for step in ahead:
        do[step[0]](*step[1:])
    for step in steps:
        if step not in ahead:
            do[step[0]](*step[1:])


def fast(nz, remote, count, query, key, value, output, grad_out, logsumexp):
    rows, width = query.shape
    half = nz // 2
    blocks = (2 * nz, BLOCK, HD)
    vmem, dma = pltpu.VMEM, pltpu.SemaphoreType.DMA
    smem = pltpu.SMEM
    outs = [jax.ShapeDtypeStruct((rows, width), BF16)] * 3
    outs.append(jax.ShapeDtypeStruct((8, BLOCK), F32))
    in_vmem = pl.BlockSpec(memory_space=pltpu.VMEM)
    scratch = [
        *[vmem(blocks, BF16)] * 4,
        vmem((nz, 8, BLOCK), F32),
        vmem((nz, 8, BLOCK), I32),
        vmem((8, BLOCK), F32),
        vmem((3, 2, rows, width), BF16),
        vmem((3, 2, HD, 2 * BLOCK), BF16),
        vmem((2, 2, 2 * BLOCK + 16, HD), BF16),
        vmem((2, 2, 2 * BLOCK + 16, HD), BF16),
        vmem((2, 2, 4 * BLOCK + 16, HD), BF16),
        vmem((2, 2, 4 * BLOCK + 16, HD), BF16),
        *[vmem((EMPTY + 1, HD, BLOCK), F32)] * 2,
        vmem((2, 2, 2, half, BLOCK + 16, HD), BF16),
        vmem((2, 2, 2, half, BLOCK + 16, HD), BF16),
        vmem((2, NY, 2 * BLOCK, HD), F32),
        vmem((2, NY, 2 * BLOCK, HD), F32),
        vmem((2, HD, 2 * BLOCK), BF16),
        smem((nz, 8, BLOCK), I32),
        smem((NY, 2 * nz), I32),
        smem((NY, 2 * nz + 2), I32),
        smem((NY, 2 * nz), I32),
        smem((EMPTY,), I32),
        smem((2, EMPTY), I32),
        pltpu.SemaphoreType.DMA,
        *[dma((len(CHAINS), 2, half))] * 2,
        *[dma((2, 2))] * 2,
        *[dma((2,))] * 2,
        *[dma((2, 2))] * 2,
        *[dma((2, 2))] * 2,
        *[dma((2, 2, 2, half))] * 2,
    ]
    return pl.pallas_call(
        functools.partial(kernel, nz),
        out_shape=outs,
        in_specs=[pl.BlockSpec(memory_space=pltpu.SMEM)] * 2 + [in_vmem] * 6,
        out_specs=[in_vmem] * 4,
        scratch_shapes=scratch,
        compiler_params=pltpu.CompilerParams(
            collective_id=0, has_side_effects=True, vmem_limit_bytes=48 * 1024 * 1024
        ),
        cost_estimate=pl.CostEstimate(
            flops=4 * 10**9, bytes_accessed=4 * 2**20, transcendentals=5 * 10**6
        ),
    )(remote, count, query, key, value, output, grad_out, logsumexp)


def per_device(query, key, value, output, grad_out, logsumexp, remote_blocks, remote_count):
    nz = lax.axis_size("seq") // NY
    *found, over = fast(
        nz, remote_blocks, remote_count, query, key, value, output, grad_out, logsumexp
    )
    return lax.cond(
        over[0, 0] > 0,
        lambda: general(
            query, key, value, output, grad_out, logsumexp, remote_blocks, remote_count
        ),
        lambda: tuple(found),
    )


def solution(mesh):
    return jax.shard_map(
        per_device,
        mesh=mesh,
        in_specs=(
            P("seq", "head"),
            P("seq", "head"),
            P("seq", "head"),
            P("seq", "head"),
            P("seq", "head"),
            P("head", "seq"),
            P("seq", None),
            P("seq"),
        ),
        out_specs=(P("seq", "head"), P("seq", "head"), P("seq", "head")),
        check_vma=False,
    )
```

```python
import functools

import jax
import jax.numpy as jnp
from jax import lax
from jax.experimental import pallas as pl
from jax.experimental.pallas import tpu as pltpu
from jax.sharding import PartitionSpec as P

HD = 128
BLOCK = 128
NY = 4
GROUPS = ((6, 6), (10,), (10,), (10,))
CAPS = tuple(sum(sizes) for sizes in GROUPS)
FIRST = tuple(sum(CAPS[:yy]) for yy in range(NY))
EMPTY = sum(CAPS)
DEAD = 1e30
LOG2E = 1.4426950408889634
F32 = jnp.float32
BF16 = jnp.bfloat16
I32 = jnp.int32


def with_halo(cells, sides, width):
    for axis, dim in sides:
        count = lax.axis_size(axis)
        ends = count - 1
        head = lax.slice_in_dim(cells, 0, width, axis=dim)
        tail = lax.slice_in_dim(cells, cells.shape[dim] - width, cells.shape[dim], axis=dim)
        cells = jnp.concatenate(
            [
                lax.ppermute(tail, axis, [(i, (i + 1) % count) for i in range(ends)]),
                cells,
                lax.ppermute(head, axis, [((i + 1) % count, i) for i in range(ends)]),
            ],
            axis=dim,
        )
    return cells


def block_pairs(queries, grads, stats, keys, values, valid, scale):
    scores = (
        jnp.einsum("pxhd,pyhd->phxy", queries, keys, preferred_element_type=jnp.float32) * scale
    )
    weights = jnp.exp(scores - stats[0][..., None]) * valid[:, None, None, None]
    probs = weights.astype(jnp.bfloat16)
    grad_values = jnp.einsum("phxy,pxhd->pyhd", probs, grads, preferred_element_type=jnp.float32)
    grad_probs = jnp.einsum("pxhd,pyhd->phxy", grads, values, preferred_element_type=jnp.float32)
    grad_scores = (weights * (grad_probs - stats[1][..., None])).astype(jnp.bfloat16)
    grad_queries = (
        jnp.einsum("phxy,pyhd->pxhd", grad_scores, keys, preferred_element_type=jnp.float32) * scale
    )
    grad_keys = (
        jnp.einsum("phxy,pxhd->pyhd", grad_scores, queries, preferred_element_type=jnp.float32)
        * scale
    )
    return (grad_queries, grad_keys, grad_values)


def spread_terms(terms):
    padded = jnp.pad(terms[0], ((0, 2), (0, 0), (0, 0), (0, 0)))
    padded = padded + jnp.pad(terms[1], ((1, 1), (0, 0), (0, 0), (0, 0)))
    return padded + jnp.pad(terms[2], ((2, 0), (0, 0), (0, 0), (0, 0)))


def remote_pairs(
    part_query, part_grad, part_stats, key_table, value_table, key_index, live_in, scale
):
    senders = part_query.shape[0]
    head_count = part_query.shape[2]
    groups = senders // 8

    def remote_group(items):
        one_q, one_g, one_s, one_k, one_l = items
        return block_pairs(
            one_q,
            one_g,
            one_s.transpose(1, 0, 2, 3),
            key_table[one_k],
            value_table[one_k],
            one_l,
            scale,
        )

    group_shape = (groups, 8, BLOCK, head_count, HD)
    found_q, found_k, found_v = lax.map(
        remote_group,
        (
            part_query.reshape(group_shape),
            part_grad.reshape(group_shape),
            part_stats.reshape(groups, 8, 2, head_count, BLOCK),
            key_index.reshape(groups, 8),
            live_in.reshape(groups, 8),
        ),
    )
    out_shape = (senders, BLOCK, head_count, HD)
    return (found_q.reshape(out_shape), found_k.reshape(out_shape), found_v.reshape(out_shape))


def general(query, key, value, output, grad_out, logsumexp, remote_blocks, remote_count):
    seq_size = lax.axis_size("seq")
    place = lax.axis_index("seq")
    rows, width = query.shape
    count_blocks = rows // BLOCK
    heads_here = width // HD
    scale = float(HD) ** (-0.5)
    shape_four = (count_blocks, BLOCK, heads_here, HD)
    q_tiles = query.reshape(shape_four)
    g_tiles = grad_out.reshape(shape_four)
    k_tiles = key.reshape(shape_four)
    v_tiles = value.reshape(shape_four)
    delta = jnp.sum(
        grad_out.astype(jnp.float32).reshape(shape_four)
        * output.astype(jnp.float32).reshape(shape_four),
        axis=3,
    )
    stats = jnp.stack(
        [
            logsumexp.reshape(heads_here, count_blocks, BLOCK).transpose(1, 0, 2),
            delta.transpose(0, 2, 1),
        ]
    )
    slots_used = (
        jnp.arange(remote_blocks.shape[1], dtype=jnp.int32)[None, :] < remote_count[:, None]
    )
    owners = remote_blocks // count_blocks
    local_key = remote_blocks % count_blocks
    match = (
        (owners[:, :, None] == jnp.arange(seq_size, dtype=jnp.int32)[None, None, :])
        & slots_used[:, :, None]
    ).astype(jnp.int32)
    live = jnp.sum(match, axis=(0, 1))
    send_query = jnp.sum(
        match * jnp.arange(count_blocks, dtype=jnp.int32)[:, None, None], axis=(0, 1)
    )
    send_key = jnp.sum(match * local_key[:, :, None], axis=(0, 1))
    meta = jnp.stack([send_key, live], axis=1).astype(jnp.float32)
    got_stats, got_meta = (
        lax.all_to_all(
            stats[:, send_query].transpose(1, 0, 2, 3),
            "seq",
            split_axis=0,
            concat_axis=0,
            tiled=True,
        ),
        lax.all_to_all(meta, "seq", split_axis=0, concat_axis=0, tiled=True),
    )
    key_index = got_meta[:, 0].astype(jnp.int32)
    live_in = got_meta[:, 1]
    got_query, got_grad = (
        lax.all_to_all(q_tiles[send_query], "seq", split_axis=0, concat_axis=0, tiled=True),
        lax.all_to_all(g_tiles[send_query], "seq", split_axis=0, concat_axis=0, tiled=True),
    )
    remote_q, remote_k, remote_v = remote_pairs(
        got_query, got_grad, got_stats, k_tiles, v_tiles, key_index, live_in, scale
    )
    returned = lax.all_to_all(
        remote_q.astype(jnp.bfloat16), "seq", split_axis=0, concat_axis=0, tiled=True
    )
    empty = jnp.zeros((count_blocks, BLOCK, width), jnp.float32)
    grad_key = empty.at[key_index].add(remote_k.reshape(seq_size, BLOCK, width))
    grad_value = empty.at[key_index].add(remote_v.reshape(seq_size, BLOCK, width))
    grad_query = empty.at[send_query].add(
        returned.reshape(seq_size, BLOCK, width).astype(jnp.float32)
    )
    offsets = jnp.arange(3, dtype=jnp.int32)[:, None]
    band_index = (
        place * count_blocks + jnp.arange(count_blocks, dtype=jnp.int32)[None, :] + offsets - 1
    )
    band_ok = (
        ((band_index >= 0) & (band_index < count_blocks * seq_size)).astype(jnp.float32).reshape(-1)
    )
    rimmed = with_halo(jnp.stack([key, value]), (("seq", 1),), BLOCK)
    wide = rimmed.reshape(2, count_blocks + 2, BLOCK, heads_here, HD)
    band_keys = jnp.concatenate([wide[0, j : j + count_blocks] for j in range(3)])
    band_values = jnp.concatenate([wide[1, j : j + count_blocks] for j in range(3)])
    band_q, band_k, band_v = block_pairs(
        jnp.concatenate([q_tiles] * 3),
        jnp.concatenate([g_tiles] * 3),
        jnp.concatenate([stats] * 3, axis=1),
        band_keys,
        band_values,
        band_ok,
        scale,
    )
    grad_query = grad_query + jnp.sum(band_q.reshape(3, count_blocks, BLOCK, width), axis=0)
    spread_k = spread_terms(band_k.reshape(3, count_blocks, BLOCK, heads_here, HD))
    spread_v = spread_terms(band_v.reshape(3, count_blocks, BLOCK, heads_here, HD))
    both = jnp.stack([spread_k, spread_v]).reshape(2, count_blocks + 2, BLOCK, width)
    edges = jnp.stack([both[:, 0], both[:, count_blocks + 1]])
    arrived = with_halo(edges, (("seq", 0),), 1)
    own = both[:, 1 : count_blocks + 1]
    own = own.at[:, 0].add(arrived[0]).at[:, count_blocks - 1].add(arrived[3])
    grad_key = grad_key + own[0]
    grad_value = grad_value + own[1]
    return (
        grad_query.reshape(rows, width).astype(jnp.bfloat16),
        grad_key.reshape(rows, width).astype(jnp.bfloat16),
        grad_value.reshape(rows, width).astype(jnp.bfloat16),
    )


def dot(a, b, ca, cb):
    return lax.dot_general(a, b, (((ca,), (cb,)), ((), ())), preferred_element_type=F32)


CUT = ()
FINE = (0, 1)
CHAINS = [(u, j) for u in range(6) for j in ((0, 1) if u in FINE else (2,))]


def last(u, j, d, half):
    if j < 2:
        return half if j == d else half - 1
    return half if u < 4 or d == 0 else half - 1


def plan(half, release=(0, 1, 0), lat=1.8, chunk=0.2, tab=3.0, bw=47.0, hop=0.3, iss=0.1):
    mid = half // 2
    steps = {}

    for u, j in CHAINS:
        cut = u > 3
        for d in range(2):
            for k in range(last(u, j, d, half) + 1):
                def size(n):
                    return 4 if u > 3 else 64 if n < half and j == 2 else 32
                sends = []
                if k < last(u, j, d, half) and not (cut and k == mid):
                    sends.append((("z", u, j, d, k + 1), d, size(k + 1), 1))
                if k == 0 and cut and mid < last(u, j, d, half):
                    sends.append((("z", u, j, d, mid + 1), d, size(mid + 1), mid + 1))
                needs = [("z", u, j, d, k - 1)] if k else []
                if k == 0 and u not in (0, 5):
                    needs = [("put", u)]
                if k == 0 and 0 < u < 4:
                    pj = 0 if u - 1 in FINE else 2
                    needs += [("z", u - 1, pj, d, min(release[u - 1], half - 1))]
                awaits = [("z", u, j, d, k)] if k else []
                steps["z", u, j, d, k] = (needs, awaits, sends, 0.0)

    def all_in(u):
        return [("z", c, j, d, last(c, j, d, half)) for c, j in CHAINS if c == u for d in range(2)]

    for d in range(2):
        steps["ks", d] = ([("z", *CHAINS[0], 1, 0)], [], [(("k", d), 3 - d, 256, 1)], 0.1)
        steps["kw", d] = ([], [("k", d)], [(("k2", d), 3 - d, 128, 1)], 0.4)
    steps["kx",] = ([("kw", 0), ("kw", 1)], [("k2", 0), ("k2", 1)], [], 0.4)
    for u, cost in ((1, 0.2), (2, 0.2), (3, 0.2), (4, 1.2), (6, 1.5)):
        steps["put", u] = ([], [], [], cost)
    steps["tc",] = (all_in(5), [], [(("tc",), 4, 1, 1)], 0.1)
    steps["tab",] = ([("tc",)], [("tc",)], [], tab)
    stats_in = all_in(4)
    for u in (4, 5):
        steps["zq", u] = ([("tab",)] + all_in(u), [], [], 0.1)
    for h in range(2):
        got = [all_in(2 * h + t) for t in range(2)]
        pairs = []
        for yy in (2, 1, 3, 0):
            keys = {0: [], 1: [("kw", 0)], 2: [("kx",)], 3: [("kw", 1)]}[yy]
            for i, size in enumerate(GROUPS[yy]):
                needs = [("tab",), ("put", 6)] + stats_in + got[0] + got[1] + keys
                steps["own", h, yy, i] = (needs, [], [], size / 2 * chunk)
                pairs.append(("own", h, yy, i))
        far = [p for p in pairs if p[2] == 2]
        steps["d1", h] = (far, [], [(("d1", h, d), 2 + d, 68, 1) for d in range(2)], 0.2)
        sends = [(("d2", h, d), 2 + d, 132, 1) for d in range(2)]
        steps["d2", h] = (pairs + [("d1", h)], [("d1", h, d) for d in range(2)], sends, 0.3)
        steps["kv", h] = ([("d2", h)], [("d2", h, d) for d in range(2)], [], 0.3)
        fin = []
        for d in range(2):
            for j in range(2):
                for k in range(1, half + 1):
                    if k > 1 or j == d:
                        cut = h in CUT
                        first = k == 1 or (k == 2 and j != d) or (cut and k == mid + 1)
                        awaits = [] if first else [("s", h, d, j, k - 1)]
                        hops = mid + 1 if cut and k == mid else 1
                        if k == half or (cut and k == mid):
                            fin.append(("s", h, d, j, k))
                        steps["s", h, d, j, k] = (pairs + [("kv", 0)] * h, awaits, [(("s", h, d, j, k), 1 - d, 32, hops)], 0.08)
        for t in range(2):
            steps["zq", 2 * h + t] = (got[t] + pairs, [], [], 0.1)
        steps["yq", h] = ([("kv", h)], [], [], 0.1)
        steps["e", h] = (pairs, fin, [], 0.3)
    for s in list(steps):
        n, a, sd, c = steps[s]
        steps[s] = (n, a, sd, c + iss * (len(a) + len(sd)))
    sender = {m: (s, kib, hops) for s, (_, _, sends, _) in steps.items() for m, _, kib, hops in sends}
    after = {s: [] for s in steps}
    for s, (needs, awaits, _, _) in steps.items():
        for n in needs:
            after[n].append((s, 0.0))
        for m in awaits:
            f, kib, hops = sender[m]
            after[f].append((s, hops * kib / bw + lat + hop * (hops - 1)))
    way = {}

    def length(s):
        if s not in way:
            way[s] = steps[s][3] + max([gap + length(n) for n, gap in after[s]], default=0.0)
        return way[s]

    left = sorted(steps, key=lambda s: (-length(s), str(s)))
    now, free, arrival, done, order = 0.0, [0.0] * 5, {}, set(), []
    while left:
        ready = [
            (max([now] + [arrival[m] for m in steps[s][1]]), i)
            for i, s in enumerate(left)
            if all(n in done for n in steps[s][0]) and all(m in arrival for m in steps[s][1])
        ]
        now, i = min(ready)
        s = left.pop(i)
        now += steps[s][3]
        for m, link, kib, hops in steps[s][2]:
            begin = max(free[link], now)
            free[link] = begin + hops * kib / bw
            arrival[m] = begin + min(hops, 2) * kib / bw + lat + hop * (hops - 1)
        done.add(s)
        order.append(s)
    return order


def kernel(
    nz,
    remote_ref,
    count_ref,
    q_ref,
    k_ref,
    v_ref,
    o_ref,
    g_ref,
    lse_ref,
    dq_ref,
    dk_ref,
    dv_ref,
    over_ref,
    agq0,
    agq1,
    agg0,
    agg1,
    ags,
    meta,
    full,
    nkv,
    nkt,
    d1snd,
    d1rcv,
    dsnd,
    drcv,
    own0,
    own1,
    rsnd,
    rrcv,
    dkacc,
    dvacc,
    kt_ref,
    table,
    lists,
    nxt,
    pos,
    idx,
    msk,
    t_sem,
    z_send,
    z_recv,
    k_send,
    k_recv,
    k2_send,
    k2_recv,
    d1_send,
    d1_recv,
    d_send,
    d_recv,
    s_send,
    s_recv,
):
    me = lax.axis_index("seq")
    y = me // nz
    z = me % nz
    half = nz // 2
    cands = 2 * nz
    scale = float(HD) ** -0.5
    zdev = [y * nz + lax.rem(z + 1, nz), y * nz + lax.rem(z + nz - 1, nz)]
    ydev = [lax.rem(y + 1, NY) * nz + z, lax.rem(y + NY - 1, NY) * nz + z]
    mid = half // 2
    zfar = [y * nz + lax.rem(z + mid + 1, nz), y * nz + lax.rem(z + nz - mid - 1, nz)]
    agq = [agq0, agq1]
    agg = [agg0, agg1]
    own = [own0, own1]
    chain_refs = [agq0, agg0, agq1, agg1]

    barrier = pltpu.get_barrier_semaphore()
    for dev in zdev + zfar + ydev:
        pl.semaphore_signal(
            barrier, inc=1, device_id={"seq": dev}, device_id_type=pl.DeviceIdType.MESH
        )

    def put_blocks(ref, own_ref, h):
        for j in range(2):
            ref[2 * z + j] = own_ref[j * BLOCK : (j + 1) * BLOCK, h * HD : (h + 1) * HD]

    line = lax.broadcasted_iota(I32, (8, BLOCK), 0)
    lane = lax.broadcasted_iota(I32, (8, BLOCK), 1)

    def put_rows():
        rows = jnp.zeros((8, BLOCK), I32)
        for j in range(2):
            hit = jnp.where(jnp.abs(lane - (2 * me + j)) <= 1, 1, 0)
            for r in range(remote_ref.shape[1]):
                used = jnp.where(count_ref[j] > r, 1, 0)
                hit = jnp.maximum(hit, jnp.where(lane == remote_ref[j, r], used, 0))
            rows = jnp.where(line == j, hit, rows)
        meta[z] = rows

    def put_stats():
        for h in range(2):
            cols = slice(h * HD, (h + 1) * HD)
            for j in range(2):
                rows = slice(j * BLOCK, (j + 1) * BLOCK)
                prod = g_ref[rows, cols].astype(F32) * o_ref[rows, cols].astype(F32)
                at = 4 * h + 2 * j
                ags[z, at : at + 1, :] = lse_ref[h : h + 1, rows] * LOG2E
                ags[z, at + 1 : at + 2, :] = jnp.sum(prod.T, axis=0, keepdims=True)

    def put_rest():
        for h in range(2):
            own[h][EMPTY] = jnp.zeros((HD, BLOCK), F32)
            for n in range(NY):
                dkacc[h, n] = jnp.zeros((2 * BLOCK, HD), F32)
                dvacc[h, n] = jnp.zeros((2 * BLOCK, HD), F32)
            kt_ref[h] = k_ref[:, h * HD : (h + 1) * HD].T

    put_blocks(agq[0], q_ref, 0)
    put_rows()
    pl.semaphore_wait(barrier, 6)

    def remote(src, dst, send, recv, dev):
        return pltpu.make_async_remote_copy(
            src_ref=src,
            dst_ref=dst,
            send_sem=send,
            recv_sem=recv,
            device_id={"seq": dev},
            device_id_type=pl.DeviceIdType.MESH,
        )

    def z_view(u, j, d, k, at):
        if u > 3:
            return (ags, meta)[u - 4].at[at]
        if j == 2 and k < half:
            return chain_refs[u].at[pl.ds(2 * at, 2)]
        return chain_refs[u].at[pl.ds(2 * at + (d if j == 2 else j), 1)]

    def z_copy(u, j, d, k, receiving=False):
        direct = u > 3 and k == mid + 1
        hop = k if receiving else 0 if direct else k - 1
        at = lax.rem(z + nz - hop, nz) if d == 0 else lax.rem(z + hop, nz)
        view = z_view(u, j, d, k, at)
        c = CHAINS.index((u, j))
        sems = z_send.at[c, d, k - 1], z_recv.at[c, d, k - 1]
        return remote(view, view, *sems, (zfar if direct else zdev)[d])

    def z_step(u, j, d, k):
        if k > 0:
            z_copy(u, j, d, k, receiving=True).wait_recv()
        end = last(u, j, d, half)
        if k < end and not (u > 3 and k == mid):
            z_copy(u, j, d, k + 1).start()
        if k == 0 and u > 3 and mid < end:
            z_copy(u, j, d, mid + 1).start()

    def z_drain(u):
        for c, j in CHAINS:
            if c == u:
                for d in range(2):
                    for k in range(1, last(u, j, d, half) + 1):
                        z_copy(u, j, d, k).wait_send()

    def table_copy():
        return pltpu.make_async_copy(meta, table, t_sem)

    def table_start():
        table_copy().start()

    def build_tables():
        table_copy().wait()

        def bit(c, yy, b):
            return table[c // 2, c % 2, lax.rem(y + yy, NY) * cands + 2 * z + b]

        def scan(c, carry):
            count = []
            for yy in range(NY):
                live = bit(c, yy, 0) | bit(c, yy, 1)
                place = jnp.where(carry[yy] < CAPS[yy], FIRST[yy] + carry[yy], EMPTY)
                pos[yy, c] = jnp.where(live > 0, place, EMPTY)
                lists[yy, c] = live
                count.append(carry[yy] + live)
            return tuple(count)

        counts = lax.fori_loop(0, cands, scan, (jnp.int32(0),) * NY)
        most = counts[0] - CAPS[0]
        for yy in range(1, NY):
            most = jnp.maximum(most, counts[yy] - CAPS[yy])
        full[...] = jnp.broadcast_to(jnp.where(most > 0, 1.0, 0.0).astype(F32), (8, BLOCK))

        for yy in range(NY):
            nxt[yy, cands] = jnp.int32(cands)
            nxt[yy, cands + 1] = jnp.int32(cands)

        def back(i, carry):
            c = cands - 1 - i
            out = []
            for yy in range(NY):
                cur = jnp.where(lists[yy, c] > 0, c, carry[yy])
                nxt[yy, c] = cur
                out.append(cur)
            return tuple(out)

        lax.fori_loop(0, cands, back, (jnp.int32(cands),) * NY)

        for yy in range(NY):
            cur = nxt[yy, 0]
            for p in range(FIRST[yy], FIRST[yy] + CAPS[yy]):
                c = jnp.minimum(cur, cands - 1)
                live = jnp.where(cur < cands, 1, 0)
                idx[p] = c
                msk[0, p] = live * bit(c, yy, 0)
                msk[1, p] = live * bit(c, yy, 1)
                cur = nxt[yy, jnp.minimum(cur + 1, cands + 1)]

    def pairs(h, n, queries, grads, lse0, lse1, delta):
        cols = slice(h * HD, (h + 1) * HD)
        keys = nkv[n - 1, 0, :, cols] if n else k_ref[:, cols]
        values = nkv[n - 1, 1, :, cols] if n else v_ref[:, cols]
        scores = dot(keys, queries, 1, 1) * (scale * LOG2E)
        weights = jnp.concatenate(
            [jnp.exp2(scores[:BLOCK] - lse0), jnp.exp2(scores[BLOCK:] - lse1)], axis=0
        )
        dvacc[h, n] += dot(weights.astype(BF16), grads, 1, 0)
        grad_probs = dot(values, grads, 1, 1)
        grad_scores = (weights * (grad_probs - delta)).astype(BF16)
        dkacc[h, n] += dot(grad_scores, queries, 1, 0)
        return dot(nkt[n - 1, h] if n else kt_ref[h], grad_scores, 1, 0) * scale

    def stat_rows(h, c):
        tile = ags[c // 2]
        odd = c % 2 > 0
        lse = jnp.where(odd, tile[4 * h + 2 : 4 * h + 3], tile[4 * h : 4 * h + 1])
        delta = jnp.where(odd, tile[4 * h + 3 : 4 * h + 4], tile[4 * h + 1 : 4 * h + 2])
        return lse, delta

    def join(parts, axis):
        return jnp.concatenate(parts, axis=axis)

    def list_pairs(h, yy, i):
        lo = FIRST[yy] + sum(GROUPS[yy][:i])
        hi = lo + GROUPS[yy][i]
        qs, gs, l0, l1, dl = [], [], [], [], []
        for p in range(lo, hi):
            c = idx[p]
            lse, delta = stat_rows(h, c)
            qs.append(agq[h][c])
            gs.append(agg[h][c])
            l0.append(jnp.where(msk[0, p] > 0, lse, DEAD))
            l1.append(jnp.where(msk[1, p] > 0, lse, DEAD))
            dl.append(delta)
        n = (0, 1, 3, 2)[yy]
        got = pairs(h, n, join(qs, 0), join(gs, 0), join(l0, 1), join(l1, 1), join(dl, 1))
        for p in range(lo, hi):
            own[h][p] = got[:, (p - lo) * BLOCK : (p - lo + 1) * BLOCK]

    def k_copy(d, n):
        src = (k_ref, v_ref)[n]
        return remote(src, nkv.at[d, n], k_send.at[d, n], k_recv.at[d, n], ydev[1 - d])

    def keys_send(d):
        for n in range(2):
            k_copy(d, n).start()

    def k2_copy(d):
        src, dst = nkv.at[d, d], nkv.at[2, d]
        return remote(src, dst, k2_send.at[d], k2_recv.at[d], ydev[1 - d])

    def keys_wait(d):
        for n in range(2):
            k_copy(d, n).wait_recv()
        k2_copy(d).start()
        for h in range(2):
            nkt[d, h] = nkv[d, 0, :, h * HD : (h + 1) * HD].T

    def keys_end():
        for d in range(2):
            k2_copy(d).wait_recv()
        for h in range(2):
            nkt[2, h] = nkv[2, 0, :, h * HD : (h + 1) * HD].T

    def d1_copy(h, d):
        sems = d1_send.at[h, d], d1_recv.at[h, d]
        return remote(d1snd.at[h, d], d1rcv.at[h, d], *sems, ydev[d])

    def d_copy(h, d):
        return remote(dsnd.at[h, d], drcv.at[h, d], d_send.at[h, d], d_recv.at[h, d], ydev[d])

    def far_send(h):
        for d in range(2):
            d1snd[h, d, : 2 * BLOCK] = (dkacc, dvacc)[d][h, 3].astype(BF16)
            d1snd[h, d, 2 * BLOCK :] = jnp.broadcast_to(full[0:1], (16, HD)).astype(BF16)
            d1_copy(h, d).start()

    def near_send(h):
        seen = full[0:1]
        for d in range(2):
            d1_copy(h, d).wait_recv()
            seen = jnp.maximum(seen, d1rcv[h, d, 2 * BLOCK :].astype(F32)[0:1])
        for d in range(2):
            sums = [dkacc[h, 1 + d], dvacc[h, 1 + d]]
            sums[d] = sums[d] + d1rcv[h, d, : 2 * BLOCK].astype(F32)
            dsnd[h, d, 0 : 2 * BLOCK] = sums[0].astype(BF16)
            dsnd[h, d, 2 * BLOCK : 4 * BLOCK] = sums[1].astype(BF16)
            dsnd[h, d, 4 * BLOCK :] = jnp.broadcast_to(seen, (16, HD)).astype(BF16)
            d_copy(h, d).start()

    def terms(h, at, j):
        c = 2 * at + j
        total = own[h][pos[0, c]]
        for yy in range(1, NY):
            total = total + own[h][pos[yy, c]]
        return total

    def s_copy(h, d, j, k):
        at = pl.ds(0, BLOCK + 16 if h == 1 and j == d else BLOCK)
        return remote(
            rsnd.at[h, d, j, k - 1, at],
            rrcv.at[h, d, j, k - 1, at],
            s_send.at[h, d, j, k - 1],
            s_recv.at[h, d, j, k - 1],
            (zfar if h in CUT and k == mid else zdev)[1 - d],
        )

    extra = slice(BLOCK, BLOCK + 16)

    def s_step(h, d, j, k):
        dist = half + 1 - k
        at = lax.rem(z + nz - dist, nz) if d == 0 else lax.rem(z + dist, nz)
        total = terms(h, at, j)
        carries = h == 1 and j == d
        if carries:
            rsnd[h, d, j, k - 1, extra] = jnp.broadcast_to(full[0:1], (16, HD)).astype(BF16)
        cut = h in CUT
        if (k > 2 or (k == 2 and j == d)) and not (cut and k == mid + 1):
            s_copy(h, d, j, k - 1).wait_recv()
            total = total + rrcv[h, d, j, k - 2, :BLOCK].astype(F32)
            if carries:
                rsnd[h, d, j, k - 1, extra] = jnp.maximum(
                    rsnd[h, d, j, k - 1, extra], rrcv[h, d, j, k - 2, extra]
                )
        rsnd[h, d, j, k - 1, :BLOCK] = total.astype(BF16)
        s_copy(h, d, j, k).start()
        if k - 2 >= (mid + 1 if cut and k > mid else 1 if j == d else 2):
            s_copy(h, d, j, k - 2).wait_send()

    def s_end(h):
        cols = slice(h * HD, (h + 1) * HD)
        any_full = full[0:1]
        for j in range(2):
            total = terms(h, z, j)
            for d in range(2):
                for k in (mid, half) if h in CUT else (half,):
                    if k > 1 or j == d:
                        s_copy(h, d, j, k).wait_recv()
                        total = total + rrcv[h, d, j, k - 1, :BLOCK].astype(F32)
                        if h == 1 and j == d:
                            got = rrcv[h, d, j, k - 1, extra].astype(F32)
                            any_full = jnp.maximum(any_full, got[0:1])
                lo = 1 if j == d else 2
                for lo, hi in ((lo, mid), (mid + 1, half)) if h in CUT else ((lo, half),):
                    for k in range(max(lo, hi - 1), hi + 1):
                        s_copy(h, d, j, k).wait_send()
            dq_ref[j * BLOCK : (j + 1) * BLOCK, cols] = total.T.astype(BF16)
        if h == 1:
            over_ref[...] = jnp.broadcast_to(any_full, (8, BLOCK))

    def results(h):
        cols = slice(h * HD, (h + 1) * HD)
        grad_k, grad_v = dkacc[h, 0], dvacc[h, 0]
        seen = full[0:1]
        for d in range(2):
            d_copy(h, d).wait_recv()
            grad_k = grad_k + drcv[h, d, 0 : 2 * BLOCK].astype(F32)
            grad_v = grad_v + drcv[h, d, 2 * BLOCK : 4 * BLOCK].astype(F32)
            seen = jnp.maximum(seen, drcv[h, d, 4 * BLOCK :].astype(F32)[0:1])
        dk_ref[:, cols] = (grad_k * scale).astype(BF16)
        dv_ref[:, cols] = grad_v.astype(BF16)
        if h == 0:
            full[...] = jnp.broadcast_to(seen, (8, BLOCK))

    def y_drain(h):
        k2_copy(h).wait_send()
        for d in range(2):
            k_copy(d, h).wait_send()
            d1_copy(h, d).wait_send()
            d_copy(h, d).wait_send()

    leads = lax.rem(lax.axis_index("head"), 2) == 0

    def put(u):
        if u in (4, 6):
            pl.when(leads)((put_stats, None, put_rest)[u - 4])
        else:
            put_blocks(chain_refs[u], (q_ref, g_ref)[u % 2], u // 2)

    do = {
        "z": z_step,
        "put": put,
        "tc": table_start,
        "tab": build_tables,
        "own": list_pairs,
        "ks": keys_send,
        "kw": keys_wait,
        "kx": keys_end,
        "d1": far_send,
        "d2": near_send,
        "kv": results,
        "zq": z_drain,
        "yq": y_drain,
        "s": s_step,
        "e": s_end,
    }
    steps = plan(half)
    ahead = [("z", *c, d, 0) for c in CHAINS if c[0] == 0 for d in range(2)]
    ahead += [("z", 5, 2, d, 0) for d in range(2)] + [("ks", 0), ("ks", 1)]
    pl.when(jnp.logical_not(leads))(put_stats)
    pl.when(jnp.logical_not(leads))(put_rest)
    for step in ahead:
        do[step[0]](*step[1:])
    for step in steps:
        if step not in ahead:
            do[step[0]](*step[1:])


def fast(nz, remote, count, query, key, value, output, grad_out, logsumexp):
    rows, width = query.shape
    half = nz // 2
    blocks = (2 * nz, BLOCK, HD)
    vmem, dma = pltpu.VMEM, pltpu.SemaphoreType.DMA
    smem = pltpu.SMEM
    outs = [jax.ShapeDtypeStruct((rows, width), BF16)] * 3
    outs.append(jax.ShapeDtypeStruct((8, BLOCK), F32))
    in_vmem = pl.BlockSpec(memory_space=pltpu.VMEM)
    scratch = [
        *[vmem(blocks, BF16)] * 4,
        vmem((nz, 8, BLOCK), F32),
        vmem((nz, 8, BLOCK), I32),
        vmem((8, BLOCK), F32),
        vmem((3, 2, rows, width), BF16),
        vmem((3, 2, HD, 2 * BLOCK), BF16),
        vmem((2, 2, 2 * BLOCK + 16, HD), BF16),
        vmem((2, 2, 2 * BLOCK + 16, HD), BF16),
        vmem((2, 2, 4 * BLOCK + 16, HD), BF16),
        vmem((2, 2, 4 * BLOCK + 16, HD), BF16),
        *[vmem((EMPTY + 1, HD, BLOCK), F32)] * 2,
        vmem((2, 2, 2, half, BLOCK + 16, HD), BF16),
        vmem((2, 2, 2, half, BLOCK + 16, HD), BF16),
        vmem((2, NY, 2 * BLOCK, HD), F32),
        vmem((2, NY, 2 * BLOCK, HD), F32),
        vmem((2, HD, 2 * BLOCK), BF16),
        smem((nz, 8, BLOCK), I32),
        smem((NY, 2 * nz), I32),
        smem((NY, 2 * nz + 2), I32),
        smem((NY, 2 * nz), I32),
        smem((EMPTY,), I32),
        smem((2, EMPTY), I32),
        pltpu.SemaphoreType.DMA,
        *[dma((len(CHAINS), 2, half))] * 2,
        *[dma((2, 2))] * 2,
        *[dma((2,))] * 2,
        *[dma((2, 2))] * 2,
        *[dma((2, 2))] * 2,
        *[dma((2, 2, 2, half))] * 2,
    ]
    return pl.pallas_call(
        functools.partial(kernel, nz),
        out_shape=outs,
        in_specs=[pl.BlockSpec(memory_space=pltpu.SMEM)] * 2 + [in_vmem] * 6,
        out_specs=[in_vmem] * 4,
        scratch_shapes=scratch,
        compiler_params=pltpu.CompilerParams(
            collective_id=0, has_side_effects=True, vmem_limit_bytes=48 * 1024 * 1024
        ),
        cost_estimate=pl.CostEstimate(
            flops=4 * 10**9, bytes_accessed=4 * 2**20, transcendentals=5 * 10**6
        ),
    )(remote, count, query, key, value, output, grad_out, logsumexp)


def per_device(query, key, value, output, grad_out, logsumexp, remote_blocks, remote_count):
    nz = lax.axis_size("seq") // NY
    *found, over = fast(
        nz, remote_blocks, remote_count, query, key, value, output, grad_out, logsumexp
    )
    return lax.cond(
        over[0, 0] > 0,
        lambda: general(
            query, key, value, output, grad_out, logsumexp, remote_blocks, remote_count
        ),
        lambda: tuple(found),
    )


def solution(mesh):
    return jax.shard_map(
        per_device,
        mesh=mesh,
        in_specs=(
            P("seq", "head"),
            P("seq", "head"),
            P("seq", "head"),
            P("seq", "head"),
            P("seq", "head"),
            P("head", "seq"),
            P("seq", None),
            P("seq"),
        ),
        out_specs=(P("seq", "head"), P("seq", "head"), P("seq", "head")),
        check_vma=False,
    )
```

```python
import functools

import jax
import jax.numpy as jnp
from jax import lax
from jax.experimental import pallas as pl
from jax.experimental.pallas import tpu as pltpu
from jax.sharding import PartitionSpec as P

HD = 128
BLOCK = 128
NY = 4
GROUPS = ((6, 6), (10,), (10,), (10,))
CAPS = tuple(sum(sizes) for sizes in GROUPS)
FIRST = tuple(sum(CAPS[:yy]) for yy in range(NY))
EMPTY = sum(CAPS)
DEAD = 1e30
LOG2E = 1.4426950408889634
F32 = jnp.float32
BF16 = jnp.bfloat16
I32 = jnp.int32


def with_halo(cells, sides, width):
    for axis, dim in sides:
        count = lax.axis_size(axis)
        ends = count - 1
        head = lax.slice_in_dim(cells, 0, width, axis=dim)
        tail = lax.slice_in_dim(cells, cells.shape[dim] - width, cells.shape[dim], axis=dim)
        cells = jnp.concatenate(
            [
                lax.ppermute(tail, axis, [(i, (i + 1) % count) for i in range(ends)]),
                cells,
                lax.ppermute(head, axis, [((i + 1) % count, i) for i in range(ends)]),
            ],
            axis=dim,
        )
    return cells


def block_pairs(queries, grads, stats, keys, values, valid, scale):
    scores = (
        jnp.einsum("pxhd,pyhd->phxy", queries, keys, preferred_element_type=jnp.float32) * scale
    )
    weights = jnp.exp(scores - stats[0][..., None]) * valid[:, None, None, None]
    probs = weights.astype(jnp.bfloat16)
    grad_values = jnp.einsum("phxy,pxhd->pyhd", probs, grads, preferred_element_type=jnp.float32)
    grad_probs = jnp.einsum("pxhd,pyhd->phxy", grads, values, preferred_element_type=jnp.float32)
    grad_scores = (weights * (grad_probs - stats[1][..., None])).astype(jnp.bfloat16)
    grad_queries = (
        jnp.einsum("phxy,pyhd->pxhd", grad_scores, keys, preferred_element_type=jnp.float32) * scale
    )
    grad_keys = (
        jnp.einsum("phxy,pxhd->pyhd", grad_scores, queries, preferred_element_type=jnp.float32)
        * scale
    )
    return (grad_queries, grad_keys, grad_values)


def spread_terms(terms):
    padded = jnp.pad(terms[0], ((0, 2), (0, 0), (0, 0), (0, 0)))
    padded = padded + jnp.pad(terms[1], ((1, 1), (0, 0), (0, 0), (0, 0)))
    return padded + jnp.pad(terms[2], ((2, 0), (0, 0), (0, 0), (0, 0)))


def remote_pairs(
    part_query, part_grad, part_stats, key_table, value_table, key_index, live_in, scale
):
    senders = part_query.shape[0]
    head_count = part_query.shape[2]
    groups = senders // 8

    def remote_group(items):
        one_q, one_g, one_s, one_k, one_l = items
        return block_pairs(
            one_q,
            one_g,
            one_s.transpose(1, 0, 2, 3),
            key_table[one_k],
            value_table[one_k],
            one_l,
            scale,
        )

    group_shape = (groups, 8, BLOCK, head_count, HD)
    found_q, found_k, found_v = lax.map(
        remote_group,
        (
            part_query.reshape(group_shape),
            part_grad.reshape(group_shape),
            part_stats.reshape(groups, 8, 2, head_count, BLOCK),
            key_index.reshape(groups, 8),
            live_in.reshape(groups, 8),
        ),
    )
    out_shape = (senders, BLOCK, head_count, HD)
    return (found_q.reshape(out_shape), found_k.reshape(out_shape), found_v.reshape(out_shape))


def general(query, key, value, output, grad_out, logsumexp, remote_blocks, remote_count):
    seq_size = lax.axis_size("seq")
    place = lax.axis_index("seq")
    rows, width = query.shape
    count_blocks = rows // BLOCK
    heads_here = width // HD
    scale = float(HD) ** (-0.5)
    shape_four = (count_blocks, BLOCK, heads_here, HD)
    q_tiles = query.reshape(shape_four)
    g_tiles = grad_out.reshape(shape_four)
    k_tiles = key.reshape(shape_four)
    v_tiles = value.reshape(shape_four)
    delta = jnp.sum(
        grad_out.astype(jnp.float32).reshape(shape_four)
        * output.astype(jnp.float32).reshape(shape_four),
        axis=3,
    )
    stats = jnp.stack(
        [
            logsumexp.reshape(heads_here, count_blocks, BLOCK).transpose(1, 0, 2),
            delta.transpose(0, 2, 1),
        ]
    )
    slots_used = (
        jnp.arange(remote_blocks.shape[1], dtype=jnp.int32)[None, :] < remote_count[:, None]
    )
    owners = remote_blocks // count_blocks
    local_key = remote_blocks % count_blocks
    match = (
        (owners[:, :, None] == jnp.arange(seq_size, dtype=jnp.int32)[None, None, :])
        & slots_used[:, :, None]
    ).astype(jnp.int32)
    live = jnp.sum(match, axis=(0, 1))
    send_query = jnp.sum(
        match * jnp.arange(count_blocks, dtype=jnp.int32)[:, None, None], axis=(0, 1)
    )
    send_key = jnp.sum(match * local_key[:, :, None], axis=(0, 1))
    meta = jnp.stack([send_key, live], axis=1).astype(jnp.float32)
    got_stats, got_meta = (
        lax.all_to_all(
            stats[:, send_query].transpose(1, 0, 2, 3),
            "seq",
            split_axis=0,
            concat_axis=0,
            tiled=True,
        ),
        lax.all_to_all(meta, "seq", split_axis=0, concat_axis=0, tiled=True),
    )
    key_index = got_meta[:, 0].astype(jnp.int32)
    live_in = got_meta[:, 1]
    got_query, got_grad = (
        lax.all_to_all(q_tiles[send_query], "seq", split_axis=0, concat_axis=0, tiled=True),
        lax.all_to_all(g_tiles[send_query], "seq", split_axis=0, concat_axis=0, tiled=True),
    )
    remote_q, remote_k, remote_v = remote_pairs(
        got_query, got_grad, got_stats, k_tiles, v_tiles, key_index, live_in, scale
    )
    returned = lax.all_to_all(
        remote_q.astype(jnp.bfloat16), "seq", split_axis=0, concat_axis=0, tiled=True
    )
    empty = jnp.zeros((count_blocks, BLOCK, width), jnp.float32)
    grad_key = empty.at[key_index].add(remote_k.reshape(seq_size, BLOCK, width))
    grad_value = empty.at[key_index].add(remote_v.reshape(seq_size, BLOCK, width))
    grad_query = empty.at[send_query].add(
        returned.reshape(seq_size, BLOCK, width).astype(jnp.float32)
    )
    offsets = jnp.arange(3, dtype=jnp.int32)[:, None]
    band_index = (
        place * count_blocks + jnp.arange(count_blocks, dtype=jnp.int32)[None, :] + offsets - 1
    )
    band_ok = (
        ((band_index >= 0) & (band_index < count_blocks * seq_size)).astype(jnp.float32).reshape(-1)
    )
    rimmed = with_halo(jnp.stack([key, value]), (("seq", 1),), BLOCK)
    wide = rimmed.reshape(2, count_blocks + 2, BLOCK, heads_here, HD)
    band_keys = jnp.concatenate([wide[0, j : j + count_blocks] for j in range(3)])
    band_values = jnp.concatenate([wide[1, j : j + count_blocks] for j in range(3)])
    band_q, band_k, band_v = block_pairs(
        jnp.concatenate([q_tiles] * 3),
        jnp.concatenate([g_tiles] * 3),
        jnp.concatenate([stats] * 3, axis=1),
        band_keys,
        band_values,
        band_ok,
        scale,
    )
    grad_query = grad_query + jnp.sum(band_q.reshape(3, count_blocks, BLOCK, width), axis=0)
    spread_k = spread_terms(band_k.reshape(3, count_blocks, BLOCK, heads_here, HD))
    spread_v = spread_terms(band_v.reshape(3, count_blocks, BLOCK, heads_here, HD))
    both = jnp.stack([spread_k, spread_v]).reshape(2, count_blocks + 2, BLOCK, width)
    edges = jnp.stack([both[:, 0], both[:, count_blocks + 1]])
    arrived = with_halo(edges, (("seq", 0),), 1)
    own = both[:, 1 : count_blocks + 1]
    own = own.at[:, 0].add(arrived[0]).at[:, count_blocks - 1].add(arrived[3])
    grad_key = grad_key + own[0]
    grad_value = grad_value + own[1]
    return (
        grad_query.reshape(rows, width).astype(jnp.bfloat16),
        grad_key.reshape(rows, width).astype(jnp.bfloat16),
        grad_value.reshape(rows, width).astype(jnp.bfloat16),
    )


def dot(a, b, ca, cb):
    return lax.dot_general(a, b, (((ca,), (cb,)), ((), ())), preferred_element_type=F32)


CUT = ()
FINE = (0,)
CHAINS = [(u, j) for u in range(6) for j in ((0, 1) if u in FINE else (2,))]


def last(u, j, d, half):
    if j < 2:
        return half if j == d else half - 1
    return half if u < 4 or d == 0 else half - 1


def plan(half, release=(0, 1, 1), lat=2.0, chunk=0.2, tab=3.0, bw=46.0, hop=0.3, iss=0.15):
    mid = half // 2
    steps = {}

    for u, j in CHAINS:
        cut = u > 3
        for d in range(2):
            for k in range(last(u, j, d, half) + 1):
                def size(n):
                    return 4 if u > 3 else 64 if n < half and j == 2 else 32
                sends = []
                if k < last(u, j, d, half) and not (cut and k == mid):
                    sends.append((("z", u, j, d, k + 1), d, size(k + 1), 1))
                if k == 0 and cut and mid < last(u, j, d, half):
                    sends.append((("z", u, j, d, mid + 1), d, size(mid + 1), mid + 1))
                needs = [("z", u, j, d, k - 1)] if k else []
                if k == 0 and u not in (0, 5):
                    needs = [("put", u)]
                if k == 0 and 0 < u < 4:
                    pj = 0 if u - 1 in FINE else 2
                    needs += [("z", u - 1, pj, d, min(release[u - 1], half - 1))]
                awaits = [("z", u, j, d, k)] if k else []
                steps["z", u, j, d, k] = (needs, awaits, sends, 0.0)

    def all_in(u):
        return [("z", c, j, d, last(c, j, d, half)) for c, j in CHAINS if c == u for d in range(2)]

    for d in range(2):
        steps["ks", d] = ([("z", *CHAINS[0], 1, 0)], [], [(("k", d), 3 - d, 256, 1)], 0.1)
        steps["kw", d] = ([], [("k", d)], [(("k2", d), 3 - d, 128, 1)], 0.4)
    steps["kx",] = ([("kw", 0), ("kw", 1)], [("k2", 0), ("k2", 1)], [], 0.4)
    for u, cost in ((1, 0.2), (2, 0.2), (3, 0.2), (4, 1.2), (6, 1.5)):
        steps["put", u] = ([], [], [], cost)
    steps["tc",] = (all_in(5), [], [(("tc",), 4, 1, 1)], 0.1)
    steps["tab",] = ([("tc",)], [("tc",)], [], tab)
    stats_in = all_in(4)
    for u in (4, 5):
        steps["zq", u] = ([("tab",)] + all_in(u), [], [], 0.1)
    for h in range(2):
        got = [all_in(2 * h + t) for t in range(2)]
        pairs = []
        for yy in (2, 1, 3, 0):
            keys = {0: [], 1: [("kw", 0)], 2: [("kx",)], 3: [("kw", 1)]}[yy]
            for i, size in enumerate(GROUPS[yy]):
                needs = [("tab",), ("put", 6)] + stats_in + got[0] + got[1] + keys
                steps["own", h, yy, i] = (needs, [], [], size / 2 * chunk)
                pairs.append(("own", h, yy, i))
        far = [p for p in pairs if p[2] == 2]
        steps["d1", h] = (far, [], [(("d1", h, d), 2 + d, 68, 1) for d in range(2)], 0.2)
        sends = [(("d2", h, d), 2 + d, 132, 1) for d in range(2)]
        steps["d2", h] = (pairs + [("d1", h)], [("d1", h, d) for d in range(2)], sends, 0.3)
        steps["kv", h] = ([("d2", h)], [("d2", h, d) for d in range(2)], [], 0.3)
        fin = []
        for d in range(2):
            for j in range(2):
                for k in range(1, half + 1):
                    if k > 1 or j == d:
                        cut = h in CUT
                        first = k == 1 or (k == 2 and j != d) or (cut and k == mid + 1)
                        awaits = [] if first else [("s", h, d, j, k - 1)]
                        hops = mid + 1 if cut and k == mid else 1
                        if k == half or (cut and k == mid):
                            fin.append(("s", h, d, j, k))
                        steps["s", h, d, j, k] = (pairs + [("kv", 0)] * h, awaits, [(("s", h, d, j, k), 1 - d, 32, hops)], 0.08)
        for t in range(2):
            steps["zq", 2 * h + t] = (got[t] + pairs, [], [], 0.1)
        steps["yq", h] = ([("kv", h)], [], [], 0.1)
        steps["e", h] = (pairs, fin, [], 0.3)
    for s in list(steps):
        n, a, sd, c = steps[s]
        steps[s] = (n, a, sd, c + iss * (len(a) + len(sd)))
    sender = {m: (s, kib, hops) for s, (_, _, sends, _) in steps.items() for m, _, kib, hops in sends}
    after = {s: [] for s in steps}
    for s, (needs, awaits, _, _) in steps.items():
        for n in needs:
            after[n].append((s, 0.0))
        for m in awaits:
            f, kib, hops = sender[m]
            after[f].append((s, hops * kib / bw + lat + hop * (hops - 1)))
    way = {}

    def length(s):
        if s not in way:
            way[s] = steps[s][3] + max([gap + length(n) for n, gap in after[s]], default=0.0)
        return way[s]

    left = sorted(steps, key=lambda s: (-length(s), str(s)))
    now, free, arrival, done, order = 0.0, [0.0] * 5, {}, set(), []
    while left:
        ready = [
            (max([now] + [arrival[m] for m in steps[s][1]]), i)
            for i, s in enumerate(left)
            if all(n in done for n in steps[s][0]) and all(m in arrival for m in steps[s][1])
        ]
        now, i = min(ready)
        s = left.pop(i)
        now += steps[s][3]
        for m, link, kib, hops in steps[s][2]:
            begin = max(free[link], now)
            free[link] = begin + hops * kib / bw
            arrival[m] = begin + min(hops, 2) * kib / bw + lat + hop * (hops - 1)
        done.add(s)
        order.append(s)
    return order


def kernel(
    nz,
    remote_ref,
    count_ref,
    q_ref,
    k_ref,
    v_ref,
    o_ref,
    g_ref,
    lse_ref,
    dq_ref,
    dk_ref,
    dv_ref,
    over_ref,
    agq0,
    agq1,
    agg0,
    agg1,
    ags,
    meta,
    full,
    nkv,
    nkt,
    d1snd,
    d1rcv,
    dsnd,
    drcv,
    own0,
    own1,
    rsnd,
    rrcv,
    dkacc,
    dvacc,
    kt_ref,
    table,
    lists,
    nxt,
    pos,
    idx,
    msk,
    t_sem,
    z_send,
    z_recv,
    k_send,
    k_recv,
    k2_send,
    k2_recv,
    d1_send,
    d1_recv,
    d_send,
    d_recv,
    s_send,
    s_recv,
):
    me = lax.axis_index("seq")
    y = me // nz
    z = me % nz
    half = nz // 2
    cands = 2 * nz
    scale = float(HD) ** -0.5
    zdev = [y * nz + lax.rem(z + 1, nz), y * nz + lax.rem(z + nz - 1, nz)]
    ydev = [lax.rem(y + 1, NY) * nz + z, lax.rem(y + NY - 1, NY) * nz + z]
    mid = half // 2
    zfar = [y * nz + lax.rem(z + mid + 1, nz), y * nz + lax.rem(z + nz - mid - 1, nz)]
    agq = [agq0, agq1]
    agg = [agg0, agg1]
    own = [own0, own1]
    chain_refs = [agq0, agg0, agq1, agg1]

    barrier = pltpu.get_barrier_semaphore()
    for dev in zdev + zfar + ydev:
        pl.semaphore_signal(
            barrier, inc=1, device_id={"seq": dev}, device_id_type=pl.DeviceIdType.MESH
        )

    def put_blocks(ref, own_ref, h):
        for j in range(2):
            ref[2 * z + j] = own_ref[j * BLOCK : (j + 1) * BLOCK, h * HD : (h + 1) * HD]

    line = lax.broadcasted_iota(I32, (8, BLOCK), 0)
    lane = lax.broadcasted_iota(I32, (8, BLOCK), 1)

    def put_rows():
        rows = jnp.zeros((8, BLOCK), I32)
        for j in range(2):
            hit = jnp.where(jnp.abs(lane - (2 * me + j)) <= 1, 1, 0)
            for r in range(remote_ref.shape[1]):
                used = jnp.where(count_ref[j] > r, 1, 0)
                hit = jnp.maximum(hit, jnp.where(lane == remote_ref[j, r], used, 0))
            rows = jnp.where(line == j, hit, rows)
        meta[z] = rows

    def put_stats():
        for h in range(2):
            cols = slice(h * HD, (h + 1) * HD)
            for j in range(2):
                rows = slice(j * BLOCK, (j + 1) * BLOCK)
                prod = g_ref[rows, cols].astype(F32) * o_ref[rows, cols].astype(F32)
                at = 4 * h + 2 * j
                ags[z, at : at + 1, :] = lse_ref[h : h + 1, rows] * LOG2E
                ags[z, at + 1 : at + 2, :] = jnp.sum(prod.T, axis=0, keepdims=True)

    def put_rest():
        for h in range(2):
            own[h][EMPTY] = jnp.zeros((HD, BLOCK), F32)
            for n in range(NY):
                dkacc[h, n] = jnp.zeros((2 * BLOCK, HD), F32)
                dvacc[h, n] = jnp.zeros((2 * BLOCK, HD), F32)
            kt_ref[h] = k_ref[:, h * HD : (h + 1) * HD].T

    put_blocks(agq[0], q_ref, 0)
    put_rows()
    pl.semaphore_wait(barrier, 6)

    def remote(src, dst, send, recv, dev):
        return pltpu.make_async_remote_copy(
            src_ref=src,
            dst_ref=dst,
            send_sem=send,
            recv_sem=recv,
            device_id={"seq": dev},
            device_id_type=pl.DeviceIdType.MESH,
        )

    def z_view(u, j, d, k, at):
        if u > 3:
            return (ags, meta)[u - 4].at[at]
        if j == 2 and k < half:
            return chain_refs[u].at[pl.ds(2 * at, 2)]
        return chain_refs[u].at[pl.ds(2 * at + (d if j == 2 else j), 1)]

    def z_copy(u, j, d, k, receiving=False):
        direct = u > 3 and k == mid + 1
        hop = k if receiving else 0 if direct else k - 1
        at = lax.rem(z + nz - hop, nz) if d == 0 else lax.rem(z + hop, nz)
        view = z_view(u, j, d, k, at)
        c = CHAINS.index((u, j))
        sems = z_send.at[c, d, k - 1], z_recv.at[c, d, k - 1]
        return remote(view, view, *sems, (zfar if direct else zdev)[d])

    def z_step(u, j, d, k):
        if k > 0:
            z_copy(u, j, d, k, receiving=True).wait_recv()
        end = last(u, j, d, half)
        if k < end and not (u > 3 and k == mid):
            z_copy(u, j, d, k + 1).start()
        if k == 0 and u > 3 and mid < end:
            z_copy(u, j, d, mid + 1).start()

    def z_drain(u):
        for c, j in CHAINS:
            if c == u:
                for d in range(2):
                    for k in range(1, last(u, j, d, half) + 1):
                        z_copy(u, j, d, k).wait_send()

    def table_copy():
        return pltpu.make_async_copy(meta, table, t_sem)

    def table_start():
        table_copy().start()

    def build_tables():
        table_copy().wait()

        def bit(c, yy, b):
            return table[c // 2, c % 2, lax.rem(y + yy, NY) * cands + 2 * z + b]

        def scan(c, carry):
            count = []
            for yy in range(NY):
                live = bit(c, yy, 0) | bit(c, yy, 1)
                place = jnp.where(carry[yy] < CAPS[yy], FIRST[yy] + carry[yy], EMPTY)
                pos[yy, c] = jnp.where(live > 0, place, EMPTY)
                lists[yy, c] = live
                count.append(carry[yy] + live)
            return tuple(count)

        counts = lax.fori_loop(0, cands, scan, (jnp.int32(0),) * NY)
        most = counts[0] - CAPS[0]
        for yy in range(1, NY):
            most = jnp.maximum(most, counts[yy] - CAPS[yy])
        full[...] = jnp.broadcast_to(jnp.where(most > 0, 1.0, 0.0).astype(F32), (8, BLOCK))

        for yy in range(NY):
            nxt[yy, cands] = jnp.int32(cands)
            nxt[yy, cands + 1] = jnp.int32(cands)

        def back(i, carry):
            c = cands - 1 - i
            out = []
            for yy in range(NY):
                cur = jnp.where(lists[yy, c] > 0, c, carry[yy])
                nxt[yy, c] = cur
                out.append(cur)
            return tuple(out)

        lax.fori_loop(0, cands, back, (jnp.int32(cands),) * NY)

        for yy in range(NY):
            cur = nxt[yy, 0]
            for p in range(FIRST[yy], FIRST[yy] + CAPS[yy]):
                c = jnp.minimum(cur, cands - 1)
                live = jnp.where(cur < cands, 1, 0)
                idx[p] = c
                msk[0, p] = live * bit(c, yy, 0)
                msk[1, p] = live * bit(c, yy, 1)
                cur = nxt[yy, jnp.minimum(cur + 1, cands + 1)]

    def pairs(h, n, queries, grads, lse0, lse1, delta):
        cols = slice(h * HD, (h + 1) * HD)
        keys = nkv[n - 1, 0, :, cols] if n else k_ref[:, cols]
        values = nkv[n - 1, 1, :, cols] if n else v_ref[:, cols]
        scores = dot(keys, queries, 1, 1) * (scale * LOG2E)
        weights = jnp.concatenate(
            [jnp.exp2(scores[:BLOCK] - lse0), jnp.exp2(scores[BLOCK:] - lse1)], axis=0
        )
        dvacc[h, n] += dot(weights.astype(BF16), grads, 1, 0)
        grad_probs = dot(values, grads, 1, 1)
        grad_scores = (weights * (grad_probs - delta)).astype(BF16)
        dkacc[h, n] += dot(grad_scores, queries, 1, 0)
        return dot(nkt[n - 1, h] if n else kt_ref[h], grad_scores, 1, 0) * scale

    def stat_rows(h, c):
        tile = ags[c // 2]
        odd = c % 2 > 0
        lse = jnp.where(odd, tile[4 * h + 2 : 4 * h + 3], tile[4 * h : 4 * h + 1])
        delta = jnp.where(odd, tile[4 * h + 3 : 4 * h + 4], tile[4 * h + 1 : 4 * h + 2])
        return lse, delta

    def join(parts, axis):
        return jnp.concatenate(parts, axis=axis)

    def list_pairs(h, yy, i):
        lo = FIRST[yy] + sum(GROUPS[yy][:i])
        hi = lo + GROUPS[yy][i]
        qs, gs, l0, l1, dl = [], [], [], [], []
        for p in range(lo, hi):
            c = idx[p]
            lse, delta = stat_rows(h, c)
            qs.append(agq[h][c])
            gs.append(agg[h][c])
            l0.append(jnp.where(msk[0, p] > 0, lse, DEAD))
            l1.append(jnp.where(msk[1, p] > 0, lse, DEAD))
            dl.append(delta)
        n = (0, 1, 3, 2)[yy]
        got = pairs(h, n, join(qs, 0), join(gs, 0), join(l0, 1), join(l1, 1), join(dl, 1))
        for p in range(lo, hi):
            own[h][p] = got[:, (p - lo) * BLOCK : (p - lo + 1) * BLOCK]

    def k_copy(d, n):
        src = (k_ref, v_ref)[n]
        return remote(src, nkv.at[d, n], k_send.at[d, n], k_recv.at[d, n], ydev[1 - d])

    def keys_send(d):
        for n in range(2):
            k_copy(d, n).start()

    def k2_copy(d):
        src, dst = nkv.at[d, d], nkv.at[2, d]
        return remote(src, dst, k2_send.at[d], k2_recv.at[d], ydev[1 - d])

    def keys_wait(d):
        for n in range(2):
            k_copy(d, n).wait_recv()
        k2_copy(d).start()
        for h in range(2):
            nkt[d, h] = nkv[d, 0, :, h * HD : (h + 1) * HD].T

    def keys_end():
        for d in range(2):
            k2_copy(d).wait_recv()
        for h in range(2):
            nkt[2, h] = nkv[2, 0, :, h * HD : (h + 1) * HD].T

    def d1_copy(h, d):
        sems = d1_send.at[h, d], d1_recv.at[h, d]
        return remote(d1snd.at[h, d], d1rcv.at[h, d], *sems, ydev[d])

    def d_copy(h, d):
        return remote(dsnd.at[h, d], drcv.at[h, d], d_send.at[h, d], d_recv.at[h, d], ydev[d])

    def far_send(h):
        for d in range(2):
            d1snd[h, d, : 2 * BLOCK] = (dkacc, dvacc)[d][h, 3].astype(BF16)
            d1snd[h, d, 2 * BLOCK :] = jnp.broadcast_to(full[0:1], (16, HD)).astype(BF16)
            d1_copy(h, d).start()

    def near_send(h):
        seen = full[0:1]
        for d in range(2):
            d1_copy(h, d).wait_recv()
            seen = jnp.maximum(seen, d1rcv[h, d, 2 * BLOCK :].astype(F32)[0:1])
        for d in range(2):
            sums = [dkacc[h, 1 + d], dvacc[h, 1 + d]]
            sums[d] = sums[d] + d1rcv[h, d, : 2 * BLOCK].astype(F32)
            dsnd[h, d, 0 : 2 * BLOCK] = sums[0].astype(BF16)
            dsnd[h, d, 2 * BLOCK : 4 * BLOCK] = sums[1].astype(BF16)
            dsnd[h, d, 4 * BLOCK :] = jnp.broadcast_to(seen, (16, HD)).astype(BF16)
            d_copy(h, d).start()

    def terms(h, at, j):
        c = 2 * at + j
        total = own[h][pos[0, c]]
        for yy in range(1, NY):
            total = total + own[h][pos[yy, c]]
        return total

    def s_copy(h, d, j, k):
        at = pl.ds(0, BLOCK + 16 if h == 1 and j == d else BLOCK)
        return remote(
            rsnd.at[h, d, j, k - 1, at],
            rrcv.at[h, d, j, k - 1, at],
            s_send.at[h, d, j, k - 1],
            s_recv.at[h, d, j, k - 1],
            (zfar if h in CUT and k == mid else zdev)[1 - d],
        )

    extra = slice(BLOCK, BLOCK + 16)

    def s_step(h, d, j, k):
        dist = half + 1 - k
        at = lax.rem(z + nz - dist, nz) if d == 0 else lax.rem(z + dist, nz)
        total = terms(h, at, j)
        carries = h == 1 and j == d
        if carries:
            rsnd[h, d, j, k - 1, extra] = jnp.broadcast_to(full[0:1], (16, HD)).astype(BF16)
        cut = h in CUT
        if (k > 2 or (k == 2 and j == d)) and not (cut and k == mid + 1):
            s_copy(h, d, j, k - 1).wait_recv()
            total = total + rrcv[h, d, j, k - 2, :BLOCK].astype(F32)
            if carries:
                rsnd[h, d, j, k - 1, extra] = jnp.maximum(
                    rsnd[h, d, j, k - 1, extra], rrcv[h, d, j, k - 2, extra]
                )
        rsnd[h, d, j, k - 1, :BLOCK] = total.astype(BF16)
        s_copy(h, d, j, k).start()
        if k - 2 >= (mid + 1 if cut and k > mid else 1 if j == d else 2):
            s_copy(h, d, j, k - 2).wait_send()

    def s_end(h):
        cols = slice(h * HD, (h + 1) * HD)
        any_full = full[0:1]
        for j in range(2):
            total = terms(h, z, j)
            for d in range(2):
                for k in (mid, half) if h in CUT else (half,):
                    if k > 1 or j == d:
                        s_copy(h, d, j, k).wait_recv()
                        total = total + rrcv[h, d, j, k - 1, :BLOCK].astype(F32)
                        if h == 1 and j == d:
                            got = rrcv[h, d, j, k - 1, extra].astype(F32)
                            any_full = jnp.maximum(any_full, got[0:1])
                lo = 1 if j == d else 2
                for lo, hi in ((lo, mid), (mid + 1, half)) if h in CUT else ((lo, half),):
                    for k in range(max(lo, hi - 1), hi + 1):
                        s_copy(h, d, j, k).wait_send()
            dq_ref[j * BLOCK : (j + 1) * BLOCK, cols] = total.T.astype(BF16)
        if h == 1:
            over_ref[...] = jnp.broadcast_to(any_full, (8, BLOCK))

    def results(h):
        cols = slice(h * HD, (h + 1) * HD)
        grad_k, grad_v = dkacc[h, 0], dvacc[h, 0]
        seen = full[0:1]
        for d in range(2):
            d_copy(h, d).wait_recv()
            grad_k = grad_k + drcv[h, d, 0 : 2 * BLOCK].astype(F32)
            grad_v = grad_v + drcv[h, d, 2 * BLOCK : 4 * BLOCK].astype(F32)
            seen = jnp.maximum(seen, drcv[h, d, 4 * BLOCK :].astype(F32)[0:1])
        dk_ref[:, cols] = (grad_k * scale).astype(BF16)
        dv_ref[:, cols] = grad_v.astype(BF16)
        if h == 0:
            full[...] = jnp.broadcast_to(seen, (8, BLOCK))

    def y_drain(h):
        k2_copy(h).wait_send()
        for d in range(2):
            k_copy(d, h).wait_send()
            d1_copy(h, d).wait_send()
            d_copy(h, d).wait_send()

    def put(u):
        if u == 4:
            put_stats()
        elif u == 6:
            put_rest()
        else:
            put_blocks(chain_refs[u], (q_ref, g_ref)[u % 2], u // 2)

    do = {
        "z": z_step,
        "put": put,
        "tc": table_start,
        "tab": build_tables,
        "own": list_pairs,
        "ks": keys_send,
        "kw": keys_wait,
        "kx": keys_end,
        "d1": far_send,
        "d2": near_send,
        "kv": results,
        "zq": z_drain,
        "yq": y_drain,
        "s": s_step,
        "e": s_end,
    }
    steps = plan(half)
    ahead = [("z", *c, d, 0) for c in CHAINS if c[0] == 0 for d in range(2)]
    ahead += [("z", 5, 2, d, 0) for d in range(2)] + [("ks", 0), ("ks", 1)]
    for step in ahead:
        do[step[0]](*step[1:])
    for step in steps:
        if step not in ahead:
            do[step[0]](*step[1:])


def fast(nz, remote, count, query, key, value, output, grad_out, logsumexp):
    rows, width = query.shape
    half = nz // 2
    blocks = (2 * nz, BLOCK, HD)
    vmem, dma = pltpu.VMEM, pltpu.SemaphoreType.DMA
    smem = pltpu.SMEM
    outs = [jax.ShapeDtypeStruct((rows, width), BF16)] * 3
    outs.append(jax.ShapeDtypeStruct((8, BLOCK), F32))
    in_vmem = pl.BlockSpec(memory_space=pltpu.VMEM)
    scratch = [
        *[vmem(blocks, BF16)] * 4,
        vmem((nz, 8, BLOCK), F32),
        vmem((nz, 8, BLOCK), I32),
        vmem((8, BLOCK), F32),
        vmem((3, 2, rows, width), BF16),
        vmem((3, 2, HD, 2 * BLOCK), BF16),
        vmem((2, 2, 2 * BLOCK + 16, HD), BF16),
        vmem((2, 2, 2 * BLOCK + 16, HD), BF16),
        vmem((2, 2, 4 * BLOCK + 16, HD), BF16),
        vmem((2, 2, 4 * BLOCK + 16, HD), BF16),
        *[vmem((EMPTY + 1, HD, BLOCK), F32)] * 2,
        vmem((2, 2, 2, half, BLOCK + 16, HD), BF16),
        vmem((2, 2, 2, half, BLOCK + 16, HD), BF16),
        vmem((2, NY, 2 * BLOCK, HD), F32),
        vmem((2, NY, 2 * BLOCK, HD), F32),
        vmem((2, HD, 2 * BLOCK), BF16),
        smem((nz, 8, BLOCK), I32),
        smem((NY, 2 * nz), I32),
        smem((NY, 2 * nz + 2), I32),
        smem((NY, 2 * nz), I32),
        smem((EMPTY,), I32),
        smem((2, EMPTY), I32),
        pltpu.SemaphoreType.DMA,
        *[dma((len(CHAINS), 2, half))] * 2,
        *[dma((2, 2))] * 2,
        *[dma((2,))] * 2,
        *[dma((2, 2))] * 2,
        *[dma((2, 2))] * 2,
        *[dma((2, 2, 2, half))] * 2,
    ]
    return pl.pallas_call(
        functools.partial(kernel, nz),
        out_shape=outs,
        in_specs=[pl.BlockSpec(memory_space=pltpu.SMEM)] * 2 + [in_vmem] * 6,
        out_specs=[in_vmem] * 4,
        scratch_shapes=scratch,
        compiler_params=pltpu.CompilerParams(
            collective_id=0, has_side_effects=True, vmem_limit_bytes=48 * 1024 * 1024
        ),
        cost_estimate=pl.CostEstimate(
            flops=4 * 10**9, bytes_accessed=4 * 2**20, transcendentals=5 * 10**6
        ),
    )(remote, count, query, key, value, output, grad_out, logsumexp)


def per_device(query, key, value, output, grad_out, logsumexp, remote_blocks, remote_count):
    nz = lax.axis_size("seq") // NY
    *found, over = fast(
        nz, remote_blocks, remote_count, query, key, value, output, grad_out, logsumexp
    )
    return lax.cond(
        over[0, 0] > 0,
        lambda: general(
            query, key, value, output, grad_out, logsumexp, remote_blocks, remote_count
        ),
        lambda: tuple(found),
    )


def solution(mesh):
    return jax.shard_map(
        per_device,
        mesh=mesh,
        in_specs=(
            P("seq", "head"),
            P("seq", "head"),
            P("seq", "head"),
            P("seq", "head"),
            P("seq", "head"),
            P("head", "seq"),
            P("seq", None),
            P("seq"),
        ),
        out_specs=(P("seq", "head"), P("seq", "head"), P("seq", "head")),
        check_vma=False,
    )
```
